32 devices in a mesh: batch: 8 (over y, x, core), seq: 4 (over z).
Axes of the slice: x: 2, y: 2, z: 4, core: 2. Of those that a mesh axis runs over, the one named last changes fastest.
Arguments:
- hidden_states: bfloat16 [24, 1024, 768], P('batch', 'seq'), may hold values from -6 to 6
- mask_flags: int32 [24, 1024], P('batch', 'seq'), may hold values from 0 to 1, as said below
- block_offsets: int32 [24, 4], P('batch', 'seq'), may hold values from 0 to 1533, as said below
- alibi_slopes: float32 [12], replicated, may hold values from 0.00024414062 to 0.001953125
- mask_embedding: bfloat16 [768], replicated, may hold values from -6 to 6
- qkv_weight: bfloat16 [768, 2304], replicated, may hold values from -0.21875 to 0.21875
- query_bias: bfloat16 [768], replicated, may hold values from -3 to 3
- value_bias: bfloat16 [768], replicated, may hold values from -3 to 3
- out_weight: bfloat16 [768, 768], replicated, may hold values from -0.875 to 0.875
- out_bias: bfloat16 [768], replicated, may hold values from -3 to 3
- first_gain: float32 [768], replicated, may hold values from 0.25 to 1.75
- first_shift: float32 [768], replicated, may hold values from -2 to 2
- gate_up_weight: bfloat16 [768, 6144], replicated, may hold values from -0.21875 to 0.21875
- down_weight: bfloat16 [3072, 768], replicated, may hold values from -0.21875 to 0.21875
- down_bias: bfloat16 [768], replicated, may hold values from -3 to 3
- second_gain: float32 [768], replicated, may hold values from 0.25 to 1.75
- second_shift: float32 [768], replicated, may hold values from -2 to 2
- output_grad: bfloat16 [24, 1024, 768], P('batch', 'seq'), may hold values from -6 to 6
Outputs:
- output: bfloat16 [24, 1024, 768], P('batch', 'seq')
- input_grad: bfloat16 [24, 1024, 768], P('batch', 'seq')
- grad_mask_embedding: float32 [768], P(('batch', 'seq'))
- grad_qkv_weight: float32 [768, 2304], P(('batch', 'seq'))
- grad_query_bias: float32 [768], P(('batch', 'seq'))
- grad_value_bias: float32 [768], P(('batch', 'seq'))
- grad_out_weight: float32 [768, 768], P(('batch', 'seq'))
- grad_out_bias: float32 [768], P(('batch', 'seq'))
- grad_first_gain: float32 [768], P(('batch', 'seq'))
- grad_first_shift: float32 [768], P(('batch', 'seq'))
- grad_gate_up_weight: float32 [768, 6144], P(('batch', 'seq'))
- grad_down_weight: float32 [3072, 768], P(('batch', 'seq'))
- grad_down_bias: float32 [768], P(('batch', 'seq'))
- grad_second_gain: float32 [768], P(('batch', 'seq'))
- grad_second_shift: float32 [768], P(('batch', 'seq'))
The draws below stay inside these ranges and needn't reach their ends.
Inputs may be any that keep to these rules, and one draw needn't show every extreme that they name: `mask_flags`: each sequence has its own expected share of masked tokens, between 5 and 20 percent. `block_offsets`: the first block of every sequence starts at 0; each next block starts 256 to 511 after the one before; in one sequence every step is 511.
All inputs are finite; a program needn't handle non-finite values.
Results may differ from the reference program's by a relative error of at most 0.02.
Values may be sent and summed in bfloat16 or wider, within the bound.
No kernel may reach another device: no remote copies, remote signals or barrier semaphores. Data moves between devices by JAX's collectives and lax.ppermute only.
A program may use at most 320 MiB of HBM per device.

```python
import math
import jax
import jax.numpy as jnp
from jax import lax

D = 768
FF = 3072
H = 12
HD = 64
BLK = 256
SEQS = 24
LEN = 1024
BLOCKS = 4


def draw_mask_flags(key, part):
    key = jax.random.fold_in(key, 11)
    rate_key, pick_key = jax.random.split(key)
    rates = jax.random.randint(rate_key, (SEQS, 1), 2, 9)
    picks = jax.random.randint(pick_key, (SEQS, LEN), 0, 40)
    return (picks < rates).astype(jnp.int32)


def draw_block_offsets(key, part):
    key = jax.random.fold_in(key, 23)
    gap_key, seq_key = jax.random.split(key)
    gaps = jax.random.randint(gap_key, (SEQS, BLOCKS), 0, BLK)
    widest = jax.random.randint(seq_key, (), 0, SEQS)
    rows = jnp.arange(SEQS, dtype=jnp.int32)[:, None]
    gaps = jnp.where(rows == widest, BLK - 1, gaps).astype(jnp.int32)
    steps_before = jnp.cumsum(gaps, axis=1) - gaps
    return (jnp.arange(BLOCKS, dtype=jnp.int32)[None, :] * BLK + steps_before).astype(jnp.int32)


def levels(rng, extent, cuts, low, top_value):
    def one(axis_at, blocks):
        steps = jax.random.uniform(jax.random.fold_in(jax.random.fold_in(rng, 6), axis_at), (blocks,), jnp.float32, low / len(cuts), top_value / len(cuts))
        return jnp.repeat(jnp.exp(steps), extent[axis_at] // blocks).reshape((-1,) + (1,) * (len(extent) - axis_at - 1))

    level = one(*cuts[0])
    for cut in cuts[1:]:
        level = level * one(*cut)
    return level


def bell_draw(key, extent, scale, bound, cuts=(), kind=jnp.bfloat16):
    drawn = scale * jax.random.normal(key, extent, jnp.float32)
    if cuts:
        drawn = drawn * levels(key, extent, cuts, -0.22, 0.18)
    return jnp.clip(drawn, -bound, bound).astype(kind)


def setup_inputs(seed: int = 0) -> dict:
    key_of = jax.random.split(jax.random.key(seed), 19)
    return {
        "hidden_states": bell_draw(key_of[0], (SEQS, LEN, D), 1.0, 6.0, ((0, 8), (1, 4))),
        "mask_flags": draw_mask_flags(jax.random.fold_in(key_of[18], 71), 0),
        "block_offsets": draw_block_offsets(jax.random.fold_in(key_of[18], 71), 0),
        "alibi_slopes": jnp.clip(jnp.exp(jax.random.uniform(key_of[3], (H,), jnp.float32, math.log(0.00024414062), math.log(0.001953125))), 0.00024414062, 0.001953125),
        "mask_embedding": bell_draw(key_of[4], (D,), 1.0, 6.0),
        "qkv_weight": bell_draw(key_of[5], (D, 3 * D), D ** -0.5, 0.21875),
        "query_bias": bell_draw(key_of[6], (D,), 0.5, 3.0),
        "value_bias": bell_draw(key_of[7], (D,), 0.5, 3.0),
        "out_weight": bell_draw(key_of[8], (D, D), (D // 16) ** -0.5, 0.875),
        "out_bias": bell_draw(key_of[9], (D,), 0.5, 3.0),
        "first_gain": jnp.clip(1.0 + 0.15 * jax.random.normal(key_of[10], (D,), jnp.float32), 0.25, 1.75),
        "first_shift": bell_draw(key_of[11], (D,), 0.3, 2.0, (), jnp.float32),
        "gate_up_weight": bell_draw(key_of[12], (D, 2 * FF), D ** -0.5, 0.21875),
        "down_weight": bell_draw(key_of[13], (FF, D), (FF // 4) ** -0.5, 0.21875),
        "down_bias": bell_draw(key_of[14], (D,), 0.5, 3.0),
        "second_gain": jnp.clip(1.0 + 0.15 * jax.random.normal(key_of[15], (D,), jnp.float32), 0.25, 1.75),
        "second_shift": bell_draw(key_of[16], (D,), 0.3, 2.0, (), jnp.float32),
        "output_grad": bell_draw(key_of[17], (SEQS, LEN, D), 1.0, 6.0, ((0, 8), (1, 4))),
    }


@jax.custom_vjp
def low(v):
    return lax.optimization_barrier(v.astype(jnp.bfloat16)).astype(jnp.float32)

@jax.custom_vjp
def low_back(v):
    return v

def low_keep(v):
    return (low(v), None)

def low_pass(kept, grad):
    return (grad,)

def back_keep(v):
    return (v, None)

def back_low(kept, grad):
    return (low(grad),)
low.defvjp(low_keep, low_pass)
low_back.defvjp(back_keep, back_low)
HIGH = lax.Precision.HIGHEST

def layer_norm(values_in, gain, shift):
    row_mean = lax.optimization_barrier(jnp.mean(values_in, axis=-1, keepdims=True))
    centred = values_in - row_mean
    variance = lax.optimization_barrier(jnp.mean(centred * centred, axis=-1, keepdims=True))
    return centred * lax.rsqrt(variance + 1e-05) * gain + shift

def forward(params, hidden, flags, positions, slopes):
    embedding, qkv_weight, query_bias, value_bias, out_weight, out_bias, first_gain, first_shift, gate_up_weight, down_weight, down_bias, second_gain, second_shift = params
    groups, length = flags.shape
    inputs = jnp.where(flags[..., None] == 1, embedding, hidden)
    biases = jnp.concatenate([query_bias, jnp.zeros_like(query_bias), value_bias])
    projected = jnp.dot(low(inputs), qkv_weight, precision=HIGH) + biases
    projected = low(low_back(projected))
    queries = projected[..., :D].reshape(groups, length, H, HD)
    keys_all = projected[..., D:2 * D].reshape(groups, length, H, HD)
    values_all = projected[..., 2 * D:].reshape(groups, length, H, HD)
    width = min(512, length)

    def attend(start):
        query_block = lax.dynamic_slice_in_dim(queries, start, width, 1)
        pos_block = lax.dynamic_slice_in_dim(positions, start, width, 1)
        raw_scores = jnp.einsum('gqhe,gkhe->ghqk', query_block, keys_all, precision=HIGH) * HD ** (-0.5)
        distance = jnp.abs(pos_block[:, :, None] - positions[:, None, :]).astype(jnp.float32)
        scores = low_back(raw_scores - slopes[None, :, None, None] * distance[:, None])
        top_score = lax.optimization_barrier(jnp.max(scores, axis=-1, keepdims=True))
        weights = jnp.exp(scores - top_score)
        probs = weights / lax.optimization_barrier(jnp.sum(weights, axis=-1, keepdims=True))
        return jnp.einsum('ghqk,gkhe->gqhe', probs, values_all, precision=HIGH)
    starts = jnp.arange(length // width, dtype=jnp.int32) * width
    blocks = lax.map(jax.checkpoint(attend), starts)
    attended = jnp.transpose(blocks, (1, 0, 2, 3, 4)).reshape(groups, length, D)
    attended = low(low_back(attended))
    branch = low_back(jnp.dot(attended, out_weight, precision=HIGH) + out_bias)
    first_out = layer_norm(inputs + branch, first_gain, first_shift)
    gate_up = low_back(jnp.dot(low(first_out), gate_up_weight, precision=HIGH))
    gate_part = gate_up[..., :FF]
    up_part = gate_up[..., FF:]
    mixed = low(low_back(jax.nn.gelu(gate_part, approximate=False) * up_part))
    ffn_out = low_back(jnp.dot(mixed, down_weight, precision=HIGH) + down_bias)
    return layer_norm(first_out + ffn_out, second_gain, second_shift)

def reference(hidden_states, mask_flags, block_offsets, alibi_slopes, mask_embedding, qkv_weight, query_bias, value_bias, out_weight, out_bias, first_gain, first_shift, gate_up_weight, down_weight, down_bias, second_gain, second_shift, output_grad):
    params = tuple((item.astype(jnp.float32) for item in (mask_embedding, qkv_weight, query_bias, value_bias, out_weight, out_bias, first_gain, first_shift, gate_up_weight, down_weight, down_bias, second_gain, second_shift)))
    positions = (block_offsets[:, :, None] + jnp.arange(BLK, dtype=jnp.int32)[None, None, :]).reshape(SEQS, LEN)
    group = math.gcd(SEQS, max(1, 4096 // LEN))
    count = SEQS // group

    def regroup(values_in):
        return values_in.reshape((count, group) + values_in.shape[1:])
    hidden = regroup(hidden_states.astype(jnp.float32))
    flags = regroup(mask_flags)
    places = regroup(positions)
    cotangent = regroup(output_grad.astype(jnp.float32) * mask_flags[..., None].astype(jnp.float32))

    def step(totals, pieces):
        hidden_in, flags_in, places_in, cotangent_in = pieces

        def layer(params_in, states_in):
            return forward(params_in, states_in, flags_in, places_in, alibi_slopes)
        result, pullback = jax.vjp(layer, params, hidden_in)
        grad_params, grad_hidden = pullback(cotangent_in)
        return (jax.tree.map(jnp.add, totals, grad_params), (result, grad_hidden))
    zeros = jax.tree.map(jnp.zeros_like, params)
    totals, (results, grads) = lax.scan(step, zeros, (hidden, flags, places, cotangent))
    grad_embed, grad_qkv, grad_qbias, grad_vbias, grad_outw, grad_outb, grad_gain1, grad_shift1, grad_gateup, grad_down, grad_downb, grad_gain2, grad_shift2 = totals
    return (results.reshape(SEQS, LEN, D).astype(jnp.bfloat16), grads.reshape(SEQS, LEN, D).astype(jnp.bfloat16), grad_embed, grad_qkv, grad_qbias, grad_vbias, grad_outw, grad_outb, grad_gain1, grad_shift1, grad_gateup, grad_down, grad_downb, grad_gain2, grad_shift2)
```

```python
import functools
import math

import jax
import jax.numpy as jnp
import numpy as np
from jax import lax
from jax.experimental import pallas as pl
from jax.experimental.pallas import tpu as pltpu
from jax.sharding import PartitionSpec as P

D = 768
FF = 3072
H = 12
HD = 64
CAP = 192
CHUNK = 768
LANES = 128
MSG = 16
SMALL = 24

F32 = jnp.float32
BF16 = jnp.bfloat16


def params(limit=62):
    return pltpu.CompilerParams(vmem_limit_bytes=limit * 1024 * 1024)


def cost(micros):
    return pl.CostEstimate(flops=int(micros * 1.15e9), bytes_accessed=1024, transcendentals=0)


def dot(a, b):
    return lax.dot_general(a, b, (((1,), (0,)), ((), ())), preferred_element_type=F32)


def dot_nt(a, b):
    return lax.dot_general(a, b, (((1,), (1,)), ((), ())), preferred_element_type=F32)


def dot_tn(a, b):
    return lax.dot_general(a, b, (((0,), (0,)), ((), ())), preferred_element_type=F32)


def split2(v):
    high = v.astype(BF16)
    return high, (v - high.astype(F32)).astype(BF16)


def dot_wide(v, b):
    high, rest = split2(v)
    return dot(high, b) + dot(rest, b)


def expand_one():
    row = lax.broadcasted_iota(jnp.int32, (LANES, D), 0)
    lane = lax.broadcasted_iota(jnp.int32, (LANES, D), 1)
    return jnp.where(lax.shift_right_logical(lane, 6) == row, 1.0, 0.0).astype(BF16)


def reduce_one():
    row = lax.broadcasted_iota(jnp.int32, (D, LANES), 0)
    lane = lax.broadcasted_iota(jnp.int32, (D, LANES), 1)
    return jnp.where(lax.shift_right_logical(row, 6) == lane, 1.0, 0.0).astype(BF16)


def permuting(place_row, me, rows):
    n = place_row.shape[1]
    distance = place_row[0:1, :]
    source = (distance ^ me) * rows + place_row[1:2, :]
    row = lax.broadcasted_iota(jnp.int32, (n, n), 0)
    return jnp.where(row == source, 1.0, 0.0).astype(BF16)


def decay(slope_lane, block_len):
    t = lax.broadcasted_iota(jnp.int32, (block_len, D), 0).astype(F32)
    return jnp.exp(-slope_lane * t), jnp.exp(-slope_lane * (block_len - 1.0 - t))


def head_decay(slope, block_len):
    row = lax.broadcasted_iota(jnp.int32, (block_len, block_len), 0)
    lane = lax.broadcasted_iota(jnp.int32, (block_len, block_len), 1)
    return jnp.exp(-slope * jnp.abs(row - lane).astype(F32)).astype(BF16)


def local_decay_sums(slopes_ref, first, second, first_out, second_out, block_len, seqs):
    lane = lax.broadcasted_iota(jnp.int32, (block_len, LANES), 1)
    for pair in range(H // 2):
        low, high = pair * LANES, (pair + 1) * LANES
        right = jnp.concatenate(
            [first[s][:, low:high] for s in range(seqs)]
            + [second[s][:, low:high] for s in range(seqs)],
            axis=1,
        )
        even = dot(head_decay(slopes_ref[2 * pair], block_len), right)
        odd = dot(head_decay(slopes_ref[2 * pair + 1], block_len), right)
        for s in range(seqs):
            rows = slice(s * block_len, (s + 1) * block_len)
            for part, out in ((0, first_out), (1, second_out)):
                at = (part * seqs + s) * LANES
                out[rows, low:high] = jnp.where(
                    lane < HD, even[:, at : at + LANES], odd[:, at : at + LANES]
                )


def steps_of(others, direct):
    return others if direct else (others + 1).bit_length() - 1


def messages_of(refs, others, direct):
    if direct:
        return list(refs)
    out = []
    for k in range(1, others + 1):
        at = k.bit_length() - 1
        out.append(refs[at].at[pl.ds((k - 2**at) * MSG, MSG), :])
    return out


def lane_value(row, index):
    lane = lax.broadcasted_iota(jnp.int32, row.shape, 1)
    return jnp.sum(jnp.where(lane == index, row, 0.0), axis=1, keepdims=True)


GELU = (
    0.7978849414614602, 0.03633308456815623, -3.259496805730905e-05, -5.530619733817487e-05,
    3.9647451634764645e-06, -1.322634044387524e-07, 1.756172658552303e-09,
)


def normal_cdf(v):
    square = v * v
    poly = GELU[6]
    for c in GELU[5::-1]:
        poly = poly * square + c
    return 0.5 + 0.5 * jnp.tanh(v * poly)


def norm_rows(v):
    centred = v - jnp.mean(v, axis=1, keepdims=True)
    scale = lax.rsqrt(jnp.mean(centred * centred, axis=1, keepdims=True) + 1e-05)
    return centred * scale, scale


def norm_back(upstream, normed, scale, gain):
    scaled = upstream * gain
    return scale * (
        scaled
        - jnp.mean(scaled, axis=1, keepdims=True)
        - normed * jnp.mean(scaled * normed, axis=1, keepdims=True)
    )


def colsum(v):
    return jnp.sum(v, axis=0, keepdims=True)


def inputs_kernel(seqs, block_len, blocks, slopes_ref, offs_ref, hidden_ref, flags_ref, *refs):
    vec_refs, (x_ref, head_ref, tail_ref, vecs_ref, flagx_ref, sc_ref) = refs[:-6], refs[-6:]
    emb = vec_refs[0][...].astype(F32).reshape(1, D)
    lane = lax.broadcasted_iota(jnp.int32, (1, D), 1)
    slope = jnp.zeros((1, D), F32)
    for h in range(H):
        slope = jnp.where(lax.shift_right_logical(lane, 6) == h, slopes_ref[h], slope)
    vecs_ref[...] = jnp.zeros_like(vecs_ref)
    vecs_ref[0:1, :] = slope
    for k, r in enumerate(vec_refs):
        vecs_ref[k + 1 : k + 2, :] = r[...].astype(F32).reshape(1, D)
    sc_ref[0] = lax.axis_index("batch") * blocks + lax.axis_index("seq")
    sc_ref[1] = lax.axis_index("seq")
    sc_ref[2] = jnp.maximum(1, (jnp.sum(flags_ref[...]) + CAP - 1) // CAP)
    flags = flags_ref[...].astype(F32)
    for s in range(seqs):
        rows = slice(s * block_len, (s + 1) * block_len)
        column = jnp.broadcast_to(flags[s : s + 1, :], (LANES, block_len)).T
        flagx_ref[rows, :] = column
        mask = jnp.broadcast_to(column[:, 0:1], (block_len, D)) > 0.5
        x = jnp.where(mask, emb, hidden_ref[rows, :].astype(F32)).astype(BF16)
        x_ref[rows, :] = x
        if s == 0:
            head_ref[...] = x
        else:
            tail_ref[(s - 1) * block_len : s * block_len, :] = x
        sc_ref[4 + s] = offs_ref[0, s]


def project_kernel(scale, groups, x_refs, w_ref, bias_ref, out_ref):
    at = 0
    for group in groups:
        x = sum(x_refs[k][first : first + rows, :] for k, first, rows in group)
        out = dot(x, w_ref[...])
        if scale is not None:
            out = (out + bias_ref[9:10, :]) * scale
        out_ref[at : at + x.shape[0], :] = out.astype(BF16)
        at += x.shape[0]


def project(values, weight, vecs, first, count, scale=None):
    flat, groups = [], []
    for group in values:
        height = min(part.shape[0] for part in group if not isinstance(part, tuple))
        spec = []
        for part in group:
            part, at = part if isinstance(part, tuple) else (part, 0)
            spec.append((len(flat), at, height))
            flat.append(part)
        groups.append(spec)
    rows = sum(group[0][2] for group in groups)

    def kernel(*refs):
        project_kernel(scale, groups, refs[: len(flat)], *refs[len(flat) :])

    return pl.pallas_call(
        kernel,
        name="project",
        out_shape=jax.ShapeDtypeStruct((rows, count * D), BF16),
        grid=(count,),
        in_specs=[pl.BlockSpec(x.shape, lambda i: (0, 0)) for x in flat]
        + [pl.BlockSpec((D, D), lambda i: (0, first + i)), pl.BlockSpec((16, D), lambda i: (0, 0))],
        out_specs=pl.BlockSpec((rows, D), lambda i: (0, i)),
        compiler_params=params(),
        cost_estimate=cost(1),
    )(*flat, weight, vecs)


def prep_kernel(
    seqs, block_len, slopes_ref, sc_ref, x_ref, wqkv_ref, vecs_ref,
    v_ref, wx_ref, num_ref, den_ref, msg_ref, g_ref, qm_ref,
):
    slope_lane = vecs_ref[0:1, :]
    emb8 = jnp.broadcast_to(vecs_ref[1:2, :], (8, D)).astype(BF16)
    qm = (dot(emb8, wqkv_ref[:, 0:D]) + vecs_ref[9:10, :]).astype(BF16).astype(F32)
    qm_ref[...] = qm
    scaled = wqkv_ref[:, D : 2 * D].astype(F32) * (qm[0:1, :] * (HD**-0.5))
    g = dot_wide(scaled, reduce_one())
    g_high, g_rest = split2(g)
    g_ref[...] = g_high
    expand = expand_one()
    dec_f, dec_r = decay(slope_lane, block_len)
    weighted, plain = [], []
    msg_ref[...] = jnp.zeros_like(msg_ref)
    lane8 = lax.broadcasted_iota(jnp.int32, (1, D), 1)
    offs_row = jnp.zeros((1, D), F32)
    for s in range(seqs):
        rows = slice(s * block_len, (s + 1) * block_len)
        x = x_ref[rows, :]
        a = dot(x, g_high) + dot(x, g_rest)
        v = dot(x, wqkv_ref[:, 2 * D :]).astype(BF16)
        v_ref[rows, :] = v
        top = jnp.max(a, axis=0, keepdims=True)
        wx = dot_wide(jnp.exp(a - top), expand)
        wx_ref[rows, :] = wx
        vw = v.astype(F32) * wx
        weighted.append(vw.astype(BF16))
        plain.append(wx.astype(BF16))
        t1, t2 = split2(top)
        t3 = (top - t1.astype(F32) - t2.astype(F32)).astype(BF16)
        tops = sum(dot(jnp.broadcast_to(t, (8, LANES)), expand) for t in (t1, t2, t3))
        msg_ref[s : s + 1, :] = tops[0:1, :]
        msg_ref[seqs + s : seqs + s + 1, :] = colsum(dec_r * vw)
        msg_ref[2 * seqs + s : 2 * seqs + s + 1, :] = colsum(dec_r * wx)
        msg_ref[3 * seqs + s : 3 * seqs + s + 1, :] = colsum(dec_f * vw)
        msg_ref[4 * seqs + s : 4 * seqs + s + 1, :] = colsum(dec_f * wx)
        offs_row = jnp.where(lane8 == s, sc_ref[4 + s].astype(F32), offs_row)
    msg_ref[MSG - 1 : MSG, :] = offs_row
    local_decay_sums(slopes_ref, weighted, plain, num_ref, den_ref, block_len, seqs)


def masked_kernel(others, seqs, block_len, rows_d, rows_f, low_count, top_bit, sc_ref, *refs):
    (flags_ref, msg_ref, *refs) = refs
    recv_refs, refs = messages_of(refs[:others], others, True), refs[others:]
    (
        num_ref, den_ref, og_ref, wo_ref, vecs_ref, placex_ref, placey_ref, placed_ref,
        wgu_ref, wd_ref,
        gs_ref, gk_ref, us_ref, uk_ref, ds_ref, dk_ref,
        att_ref, invden_ref, dheads_ref, small_ref,
        wg_s, wu_s, wd_s, g_s, u_s, dk_s, ds_s, os_s, ok_s, lowx_s, lowy_s, mixed_s, d1_s, d2_s,
        acc_s, fn_s, in_sems, out_sems,
    ) = refs
    n = FF // CHUNK
    half = D // 2
    wide = CHUNK // 2
    me, z = sc_ref[0], sc_ref[1]
    tokens = seqs * block_len
    core = lax.shift_right_logical(me, top_bit) & 1
    plane = lax.shift_right_logical(me, top_bit + 1)

    def at(i):
        return pl.ds(pl.multiple_of(i * CHUNK, CHUNK), CHUNK)

    unit = wide + half // n

    def out_stores():
        copies = []
        for i in range(n):
            rows = pl.ds(i * unit + wide, half // n)
            for k, (inside, outside) in enumerate(((ok_s, dk_ref), (os_s, ds_ref))):
                copies.append(
                    pltpu.make_async_copy(
                        inside.at[pl.ds(i * (half // n), half // n), :], outside.at[rows, :],
                        out_sems.at[6 + k, i],
                    )
                )
        return copies

    def loads(i):
        up_at = pl.ds(pl.multiple_of(FF + i * CHUNK, CHUNK), CHUNK)
        return [
            pltpu.make_async_copy(wgu_ref.at[:, at(i)], wg_s.at[i], in_sems.at[0, i]),
            pltpu.make_async_copy(wgu_ref.at[:, up_at], wu_s.at[i], in_sems.at[1, i]),
            pltpu.make_async_copy(wd_ref.at[at(i), :], wd_s.at[i], in_sems.at[2, i]),
        ]

    def stores(i):
        place = swap_pair(i ^ plane)
        rows = pl.ds(pl.multiple_of(place * unit, 32), wide)
        return [
            pltpu.make_async_copy(g_s.at[i, pl.ds(0, half)], gk_ref.at[:, at(i)], out_sems.at[0, i]),
            pltpu.make_async_copy(g_s.at[i, pl.ds(half, half)], gs_ref.at[:, at(i)], out_sems.at[1, i]),
            pltpu.make_async_copy(u_s.at[i, pl.ds(0, half)], uk_ref.at[:, at(i)], out_sems.at[2, i]),
            pltpu.make_async_copy(u_s.at[i, pl.ds(half, half)], us_ref.at[:, at(i)], out_sems.at[3, i]),
            pltpu.make_async_copy(dk_s.at[i], dk_ref.at[rows, :], out_sems.at[4, i]),
            pltpu.make_async_copy(ds_s.at[i], ds_ref.at[rows, :], out_sems.at[5, i]),
        ]

    for i in range(n):
        for copy in loads(i):
            copy.start()

    slope_lane = vecs_ref[0:1, :]
    dec_f, dec_r = decay(slope_lane, block_len)
    for s in range(seqs):
        rows = slice(s * block_len, (s + 1) * block_len)

        def row(ref, kind):
            return ref[kind * seqs + s : kind * seqs + s + 1, :]

        own_off = lane_value(msg_ref[MSG - 1 : MSG, :], s)
        top = row(msg_ref, 0)
        for r in recv_refs:
            top = jnp.maximum(top, row(r, 0))
        own = jnp.exp(row(msg_ref, 0) - top)
        zero = jnp.zeros((1, D), F32)
        left_v, left_z, right_v, right_z = zero, zero, zero, zero
        for k, r in enumerate(recv_refs):
            gap = jnp.abs(lane_value(r[MSG - 1 : MSG, :], s) - own_off) - (block_len - 1.0)
            factor = jnp.exp(row(r, 0) - top - slope_lane * gap)
            is_left = (z ^ (k + 1)) < z
            f_left = jnp.where(is_left, factor, 0.0)
            f_right = jnp.where(is_left, 0.0, factor)
            left_v += f_left * row(r, 1)
            left_z += f_left * row(r, 2)
            right_v += f_right * row(r, 3)
            right_z += f_right * row(r, 4)
        den = own * den_ref[rows, :] + dec_f * left_z + dec_r * right_z
        num = own * num_ref[rows, :] + dec_f * left_v + dec_r * right_v
        inv = 1.0 / den
        invden_ref[rows, :] = inv
        att_ref[rows, :] = (num * inv).astype(BF16)
    rank = masked_ranks(flags_ref, seqs, tokens)
    small_ref[...] = jnp.zeros_like(small_ref)

    masked_tile(
        0, True, me, rows_d, rows_f, low_count, core, rank, att_ref, og_ref, wo_ref, vecs_ref,
        placex_ref, placey_ref, placed_ref, wg_s, wu_s, wd_s, g_s, u_s, dk_s, ds_s, os_s, ok_s,
        dheads_ref, small_ref, lowx_s, lowy_s, mixed_s, d1_s, d2_s, acc_s, fn_s, loads, stores,
    )
    for copy in out_stores():
        copy.start()
    for i in range(n):
        for copy in stores(i):
            copy.wait()
    for copy in out_stores():
        copy.wait()


def masked_tile(
    t, first, me, rows_d, rows_f, low_count, core, rank, att_ref, og_ref, wo_ref, vecs_ref,
    placex_ref, placey_ref, placed_ref, wg_s, wu_s, wd_s, g_s, u_s, dk_s, ds_s, os_ref, ok_ref,
    dheads_ref, small_ref, lowx_s, lowy_s, mixed_s, d1_s, d2_s, acc_s, fn_s, loads, stores,
):
    n = FF // CHUNK
    half = D // 2
    wide = CHUNK // 2
    tokens = att_ref.shape[0]

    def put(ref, value):
        ref[...] = (value if first else ref[...].astype(F32) + value).astype(BF16)

    place = lax.broadcasted_iota(jnp.int32, (CAP, tokens), 0) + t * CAP
    comp = jnp.where(place.astype(F32) == rank, 1.0, 0.0).astype(BF16)
    att_low = (dot(comp, att_ref[...]) + vecs_ref[2:3, :]).astype(BF16)
    first_sum = vecs_ref[1:2, :] + (dot(att_low, wo_ref[...]) + vecs_ref[3:4, :])
    first_normed, first_scale = norm_rows(first_sum)
    fn_s[...] = first_normed
    low = (first_normed * vecs_ref[4:5, :] + vecs_ref[5:6, :]).astype(BF16)
    lowx_s[...] = dot(low, permuting(placex_ref[...], me, rows_d)).astype(BF16).T
    lowy_s[...] = dot(low, permuting(placey_ref[...], me, rows_d)).astype(BF16).T
    acc_s[...] = jnp.zeros((CAP, D), F32)

    def forward(i, c):
        for copy in loads(i):
            copy.wait()
        gate = dot(low, wg_s[i])
        up = dot(low, wu_s[i])
        phi = normal_cdf(gate)
        act = gate * phi
        mixed = (act * up).astype(BF16)
        mixed_s[i] = mixed
        d2_s[i] = act.astype(BF16)
        slope = phi + gate * (jnp.exp(-0.5 * gate * gate) * ((2.0 * math.pi) ** -0.5))
        d1_s[i] = (up * slope).astype(BF16)
        acc_s[...] += dot(mixed, wd_s[i])
        return c

    lax.fori_loop(0, n, forward, 0)
    first_out = fn_s[...] * vecs_ref[4:5, :] + vecs_ref[5:6, :]
    normed, scale = norm_rows(first_out + (acc_s[...] + vecs_ref[6:7, :]))
    up = dot(comp, og_ref[...])
    grad_second = norm_back(up, normed, scale, vecs_ref[7:8, :])
    acc_s[...] = grad_second
    bg = grad_second.astype(BF16)
    small_ref[0:1, :] += colsum(up * normed)
    small_ref[1:2, :] += colsum(up)
    small_ref[2:3, :] += colsum(bg.astype(F32))
    change_d = permuting(placed_ref[...], me & (low_count - 1), rows_f)

    def backward(i, c):
        mixed_grad = dot_nt(bg, wd_s[i]).astype(BF16).astype(F32)
        gate_grad = (mixed_grad * d1_s[i].astype(F32)).astype(BF16)
        up_grad = (mixed_grad * d2_s[i].astype(F32)).astype(BF16)
        put(g_s.at[i], dot(lowx_s[...], gate_grad))
        put(u_s.at[i], dot(lowy_s[...], up_grad))
        mixed = mixed_s[i]
        low_half, high_half = mixed[:, :wide], mixed[:, wide:]
        keep = jnp.where(core == 0, low_half, high_half)
        send = jnp.where(core == 0, high_half, low_half)
        put(dk_s.at[i], dot_tn(dot(keep, change_d).astype(BF16), bg))
        put(ds_s.at[i], dot_tn(dot(send, change_d).astype(BF16), bg))
        for copy in stores(i):
            copy.start()
        acc_s[...] += dot_nt(gate_grad, wg_s[i]) + dot_nt(up_grad, wu_s[i])
        return c

    lax.fori_loop(0, n, backward, 0)
    grad_first = acc_s[...]
    first_normed = fn_s[...]
    grad = norm_back(grad_first, first_normed, first_scale, vecs_ref[4:5, :])
    small_ref[3:4, :] += colsum(grad_first * first_normed)
    small_ref[4:5, :] += colsum(grad_first)
    attn_grad = grad.astype(BF16)
    small_ref[5:6, :] += colsum(attn_grad.astype(F32))
    small_ref[6:7, :] += colsum(grad)
    grad_out = dot_tn(dot(att_low, permuting(placex_ref[...], me, rows_d)).astype(BF16), attn_grad)
    put(ok_ref, grad_out[:half])
    put(os_ref, grad_out[half:])
    heads = dot_nt(attn_grad, wo_ref[...]).astype(BF16)
    small_ref[7:8, :] += colsum(heads.astype(F32))
    put(dheads_ref, dot_tn(comp, heads))


def masked_ranks(flags_ref, seqs, tokens):
    flags = jnp.concatenate([flags_ref[s : s + 1, :] for s in range(seqs)], axis=1).astype(F32)
    before = lax.broadcasted_iota(jnp.int32, (tokens, tokens), 0)
    after = lax.broadcasted_iota(jnp.int32, (tokens, tokens), 1)
    upper = jnp.where(before < after, 1.0, 0.0).astype(BF16)
    rank = dot(jnp.broadcast_to(flags, (8, tokens)).astype(BF16), upper)[0:1, :]
    return jnp.where(flags > 0.5, rank, -1.0)


def more_tiles_kernel(seqs, block_len, rows_d, rows_f, low_count, top_bit, sc_ref, *refs):
    held, (wgu_ref, wd_ref), grads, scratch = refs[:8], refs[8:10], refs[18:26], refs[26:]
    (
        flags_s, att_s, og_s, wo_s, vecs_s, placex_s, placey_s, placed_s, wg_s, wu_s, wd_s, g_s, u_s,
        dk_s, ds_s, os_s, ok_s, dheads_s, small_s, lowx_s, lowy_s, mixed_s, d1_s, d2_s, acc_s, fn_s,
        sem,
    ) = scratch
    gs_ref, gk_ref, us_ref, uk_ref, ds_ref, dk_ref, dheads_ref, small_ref = grads
    n = FF // CHUNK
    half = D // 2
    wide = CHUNK // 2
    me = sc_ref[0]
    core = lax.shift_right_logical(me, top_bit) & 1
    plane = lax.shift_right_logical(me, top_bit + 1)

    def move(source, target):
        copy = pltpu.make_async_copy(source, target, sem)
        copy.start()
        copy.wait()

    part = half // n
    unit = wide + part
    pairs = [(dheads_ref, dheads_s), (small_ref, small_s)]
    for i in range(n):
        at = pl.ds(i * CHUNK, CHUNK)
        rows = pl.ds(pl.multiple_of(swap_pair(i ^ plane) * unit, 32), wide)
        out_rows = pl.ds(i * unit + wide, part)
        pairs += [
            (dk_ref.at[out_rows, :], ok_s.at[pl.ds(i * part, part), :]),
            (ds_ref.at[out_rows, :], os_s.at[pl.ds(i * part, part), :]),
            (gk_ref.at[:, at], g_s.at[i, pl.ds(0, half)]),
            (gs_ref.at[:, at], g_s.at[i, pl.ds(half, half)]),
            (uk_ref.at[:, at], u_s.at[i, pl.ds(0, half)]),
            (us_ref.at[:, at], u_s.at[i, pl.ds(half, half)]),
            (dk_ref.at[rows, :], dk_s.at[i]),
            (ds_ref.at[rows, :], ds_s.at[i]),
        ]

    @pl.when(sc_ref[2] > 1)
    def _():
        for i in range(n):
            at = pl.ds(i * CHUNK, CHUNK)
            move(wgu_ref.at[:, at], wg_s.at[i])
            move(wgu_ref.at[:, pl.ds(FF + i * CHUNK, CHUNK)], wu_s.at[i])
            move(wd_ref.at[at, :], wd_s.at[i])
        for source, target in zip(held, scratch[:8]):
            move(source, target)
        for outside, inside in pairs:
            move(outside, inside)
        rank = masked_ranks(flags_s, seqs, seqs * block_len)

        def tile(t, carry):
            masked_tile(
                t, False, me, rows_d, rows_f, low_count, core, rank, att_s, og_s, wo_s, vecs_s,
                placex_s, placey_s, placed_s, wg_s, wu_s, wd_s, g_s, u_s, dk_s, ds_s, os_s, ok_s,
                dheads_s, small_s, lowx_s, lowy_s, mixed_s, d1_s, d2_s, acc_s, fn_s,
                lambda i: [], lambda i: [],
            )
            return carry

        lax.fori_loop(1, sc_ref[2], tile, 0)
        for outside, inside in pairs:
            move(inside, outside)


def inner_kernel(
    seqs, block_len, slopes_ref, dheads_ref, att_ref, invden_ref, vecs_ref, uv_ref, ud_ref, msg_ref
):
    slope_lane = vecs_ref[0:1, :]
    dec_f, dec_r = decay(slope_lane, block_len)
    first, second = [], []
    msg_ref[...] = jnp.zeros_like(msg_ref)
    reduce, expand = reduce_one(), expand_one()
    for s in range(seqs):
        rows = slice(s * block_len, (s + 1) * block_len)
        dheads = dheads_ref[rows, :].astype(F32)
        inner = dot_wide(dot_wide(dheads * att_ref[rows, :].astype(F32), reduce), expand)
        inv = invden_ref[rows, :]
        yv, yd = dheads * inv, inner * inv
        first.append(yv.astype(BF16))
        second.append(yd.astype(BF16))
        msg_ref[s : s + 1, :] = colsum(dec_r * yv)
        msg_ref[seqs + s : seqs + s + 1, :] = colsum(dec_r * yd)
        msg_ref[2 * seqs + s : 2 * seqs + s + 1, :] = colsum(dec_f * yv)
        msg_ref[3 * seqs + s : 3 * seqs + s + 1, :] = colsum(dec_f * yd)
    local_decay_sums(slopes_ref, first, second, uv_ref, ud_ref, block_len, seqs)


def value_kernel(others, seqs, block_len, rows_d, sc_ref, *refs):
    (flags_ref, msg1_ref, msg2_ref, *refs) = refs
    steps = steps_of(others, False)
    recv1 = messages_of(refs[:others], others, True)
    recv2 = messages_of(refs[others : others + steps], others, False)
    refs = refs[others + steps :]
    (
        uv_ref, ud_ref, wx_ref, v_ref, x_ref, wqkv_ref, g_ref, vecs_ref, placey_ref, smalla_ref,
        ig_ref, vs_ref, vk_ref, small_ref, dv_s, t_s,
    ) = refs
    me, z = sc_ref[0], sc_ref[1]
    slope_lane = vecs_ref[0:1, :]
    dec_f, dec_r = decay(slope_lane, block_len)
    reduce = reduce_one()
    embed = smalla_ref[6:7, :]
    half = D // 2
    for s in range(seqs):
        rows = slice(s * block_len, (s + 1) * block_len)

        def row(ref, kind):
            return ref[kind * seqs + s : kind * seqs + s + 1, :]

        own_off = lane_value(msg1_ref[MSG - 1 : MSG, :], s)
        top = row(msg1_ref, 0)
        for r in recv1:
            top = jnp.maximum(top, row(r, 0))
        own = jnp.exp(row(msg1_ref, 0) - top)
        zero = jnp.zeros((1, D), F32)
        left_v, left_d, right_v, right_d = zero, zero, zero, zero
        for k, (r1, r2) in enumerate(zip(recv1, recv2)):
            gap = jnp.abs(lane_value(r1[MSG - 1 : MSG, :], s) - own_off) - (block_len - 1.0)
            factor = jnp.exp(-slope_lane * gap)
            is_left = (z ^ (k + 1)) < z
            f_left = jnp.where(is_left, factor, 0.0)
            f_right = jnp.where(is_left, 0.0, factor)
            left_v += f_left * row(r2, 0)
            left_d += f_left * row(r2, 1)
            right_v += f_right * row(r2, 2)
            right_d += f_right * row(r2, 3)
        weight = wx_ref[rows, :] * own
        uv = weight * (uv_ref[rows, :] + dec_f * left_v + dec_r * right_v)
        ud = weight * (ud_ref[rows, :] + dec_f * left_d + dec_r * right_d)
        dv = uv.astype(BF16)
        dv_s[rows, :] = dv
        t = dot_wide(uv * v_ref[rows, :].astype(F32) - ud * (1.0 / HD), reduce)
        t_s[rows, :] = t
        dx = dot_nt(dv, wqkv_ref[:, 2 * D :]) + dot_nt(t.astype(BF16), g_ref[...])
        masked = jnp.broadcast_to(flags_ref[rows, 0:1], (block_len, D)) > 0.5
        ig_ref[rows, :] = jnp.where(masked, 0.0, dx).astype(BF16)
        embed += colsum(jnp.where(masked, dx, 0.0))
    x = x_ref[...]
    xp = dot(x, permuting(placey_ref[...], me, rows_d)).astype(BF16)
    gv = dot_tn(xp, dv_s[...]).astype(BF16)
    vk_ref[...] = gv[:half]
    vs_ref[2 * SMALL :, :] = gv[half:]
    t_high, t_rest = split2(t_s[...])
    a_t = (dot_tn(t_high, x) + dot_tn(t_rest, x))[0:16, :]
    both = dot_wide(a_t, wqkv_ref[:, D : 2 * D]) * (HD**-0.5)
    head = lax.broadcasted_iota(jnp.int32, (16, D), 0)
    lane = lax.broadcasted_iota(jnp.int32, (16, D), 1)
    query = colsum(jnp.where(lax.shift_right_logical(lane, 6) == head, both, 0.0))
    q_high, q_rest = split2(jnp.broadcast_to(query, (8, D)))
    wq = wqkv_ref[:, 0:D]
    embed += (dot_nt(q_high, wq) + dot_nt(q_rest, wq))[0:1, :]
    small_ref[0:8, :] = smalla_ref[...]
    small_ref[6:7, :] = embed
    small_ref[8:24, :] = a_t
    small_ref[20:21, :] = query
    put_small(vs_ref, small_ref[...])


FEATS = 6
LOG2E = math.log2(math.e)


def attention_kernel(others, slopes_ref, sc_ref, q_ref, own_ref, *refs):
    kv_refs, msg_refs, (msg_ref, vecs_ref, out_ref, bias_s, qfeat_s) = (
        refs[:others], refs[others : 2 * others], refs[2 * others :],
    )
    s = pl.program_id(0)
    block_len = q_ref.shape[0]
    z = sc_ref[1]
    lane = lax.broadcasted_iota(jnp.int32, (block_len, LANES), 1)
    token = lax.broadcasted_iota(jnp.int32, (block_len, LANES), 0).astype(F32)
    head_of = lane // FEATS
    kind = lane - head_of * FEATS

    @pl.when(s == 0)
    def _():
        row = lax.broadcasted_iota(jnp.int32, (block_len, block_len), 0)
        col = lax.broadcasted_iota(jnp.int32, (block_len, block_len), 1)
        apart = jnp.abs(row - col).astype(F32)
        value = jnp.where(kind < 3, token, 1.0)
        for h in range(H):
            bias_s[h] = apart * (slopes_ref[h] * LOG2E)
            qfeat_s[h] = jnp.where(head_of == h, value, 0.0).astype(BF16)

    slope = jnp.zeros((1, LANES), F32)
    lane1 = lax.broadcasted_iota(jnp.int32, (1, LANES), 1)
    for h in range(H):
        slope = jnp.where(lane1 // FEATS == h, slopes_ref[h] * LOG2E, slope)
    kind1 = lane1 - (lane1 // FEATS) * FEATS
    own_off = lane_value(msg_ref[MSG - 1 : MSG, :], s)
    feats = []
    for k in range(others):
        gap = jnp.abs(lane_value(msg_refs[k][MSG - 1 : MSG, :], s) - own_off)
        sign = jnp.where((z ^ (k + 1)) < z, 1.0, -1.0)
        value = jnp.where(kind1 < 3, -sign * slope, slope * (sign * token - gap))
        p1 = value.astype(BF16).astype(F32)
        p2 = (value - p1).astype(BF16).astype(F32)
        p3 = value - p1 - p2
        part = jnp.where(kind1 % 3 == 0, p1, jnp.where(kind1 % 3 == 1, p2, p3))
        feats.append(part.astype(BF16))
    ones = jnp.ones((block_len, LANES), BF16)
    zero = jnp.zeros((), BF16)
    for pair in range(H // 2):
        low, high = pair * LANES, (pair + 1) * LANES
        q = q_ref[:, low:high]
        own_k = own_ref[:, low:high]
        keys = [
            jnp.concatenate([r[:, low:high], feats[k]], axis=1) for k, r in enumerate(kv_refs)
        ]
        own_v = jnp.concatenate([own_ref[:, D + low : D + high], ones], axis=1)
        values = [jnp.concatenate([r[:, D + low : D + high], ones], axis=1) for r in kv_refs]
        outs = []
        for e in range(2):
            h = 2 * pair + e
            mine = (lane < HD) if e == 0 else (lane >= HD)
            qh = jnp.where(mine, q, zero)
            qf = jnp.concatenate([qh, qfeat_s[h]], axis=1)
            scores = [dot_nt(qh, own_k) - bias_s[h]] + [dot_nt(qf, key) for key in keys]
            top = scores[0]
            for sc in scores[1:]:
                top = jnp.maximum(top, sc)
            top = jnp.max(top, axis=1, keepdims=True)
            total = dot(jnp.exp2(scores[0] - top).astype(BF16), own_v)
            for sc, value in zip(scores[1:], values):
                total += dot(jnp.exp2(sc - top).astype(BF16), value)
            outs.append(total[:, :LANES] / total[:, LANES:])
        out_ref[:, low:high] = (
            jnp.where(lane < HD, outs[0], outs[1]) + vecs_ref[2:3, low:high]
        ).astype(BF16)


def dense_kernel(
    x_ref, att_ref, wo_ref, vecs_ref, wg_ref, wu_ref, wd_ref, out_ref, fo_s, low_s, acc_s
):
    step = pl.program_id(0)

    @pl.when(step == 0)
    def _():
        first_sum = x_ref[...].astype(F32) + (dot(att_ref[...], wo_ref[...]) + vecs_ref[3:4, :])
        normed, _scale = norm_rows(first_sum)
        first_out = normed * vecs_ref[4:5, :] + vecs_ref[5:6, :]
        fo_s[...] = first_out
        low_s[...] = first_out.astype(BF16)
        acc_s[...] = jnp.zeros_like(acc_s)

    low = low_s[...]
    gate = dot(low, wg_ref[...])
    up = dot(low, wu_ref[...])
    mixed = (gate * normal_cdf(gate) * up).astype(BF16)
    acc_s[...] += dot(mixed, wd_ref[...])

    @pl.when(step == pl.num_programs(0) - 1)
    def _():
        normed, _scale = norm_rows(fo_s[...] + (acc_s[...] + vecs_ref[6:7, :]))
        out_ref[...] = (normed * vecs_ref[7:8, :] + vecs_ref[8:9, :]).astype(BF16)


def put_small(ref, small):
    high, rest = split2(small)
    ref[0:SMALL, :] = high
    ref[SMALL : 2 * SMALL, :] = rest


def get_small(ref):
    return ref[0:SMALL, :].astype(F32) + ref[SMALL : 2 * SMALL, :].astype(F32)


def add_split_kernel(keep, got, keep_out, send_out):
    half = keep.shape[0] // 2
    for part, out in enumerate((keep_out, send_out)):
        rows = pl.ds(part * half, half)
        out[...] = (keep[rows, :].astype(F32) + got[rows, :].astype(F32)).astype(BF16)


def add_split(keep, got, name):
    rows, width = keep.shape
    cut = max(1, rows * width // (512 * 1024))
    while width % (cut * LANES):
        cut -= 1
    return pl.pallas_call(
        add_split_kernel,
        name=name,
        out_shape=[jax.ShapeDtypeStruct((rows // 2, width), BF16)] * 2,
        grid=(cut,),
        in_specs=[pl.BlockSpec((rows, width // cut), lambda i: (0, i))] * 2,
        out_specs=[pl.BlockSpec((rows // 2, width // cut), lambda i: (0, i))] * 2,
        compiler_params=params(),
        cost_estimate=cost(0.5),
    )(keep, got)


def add_small_kernel(keep, small, got, keep_out, send_out, small_out):
    half = keep.shape[0] // 2
    total = keep[...].astype(F32) + got[2 * SMALL :, :].astype(F32)
    keep_out[...] = total[:half].astype(BF16)
    send_out[2 * SMALL :, :] = total[half:].astype(BF16)
    both = small[...] + get_small(got)
    small_out[...] = both
    put_small(send_out, both)


def add_small(keep, small, got, name):
    rows = keep.shape[0] // 2
    full = lambda shape: pl.BlockSpec(shape, lambda i: (0, 0))
    return pl.pallas_call(
        add_small_kernel,
        name=name,
        grid=(1,),
        out_shape=[
            jax.ShapeDtypeStruct((rows, D), BF16), jax.ShapeDtypeStruct((2 * SMALL + rows, D), BF16),
            jax.ShapeDtypeStruct((SMALL, D), F32),
        ],
        in_specs=[full(keep.shape), full(small.shape), full(got.shape)],
        out_specs=[full((rows, D)), full((2 * SMALL + rows, D)), full((SMALL, D))],
        compiler_params=params(),
        cost_estimate=cost(0.5),
    )(keep, small, got)


def add_join_kernel(gate, gate_got, up, up_got, keep_out, send_out):
    half, width = gate.shape[0] // 2, gate.shape[1]
    for at, (keep, got) in enumerate(((gate, gate_got), (up, up_got))):
        total = keep[...].astype(F32) + got[...].astype(F32)
        keep_out[:, at * width : (at + 1) * width] = total[:half].astype(BF16)
        send_out[:, at * width : (at + 1) * width] = total[half:].astype(BF16)


def add_join(arrays, name):
    rows, width = arrays[0].shape
    full = lambda shape: pl.BlockSpec(shape, lambda i: (0, 0))
    return pl.pallas_call(
        add_join_kernel,
        name=name,
        grid=(1,),
        out_shape=[jax.ShapeDtypeStruct((rows // 2, 2 * width), BF16)] * 2,
        in_specs=[full((rows, width))] * 4,
        out_specs=[full((rows // 2, 2 * width))] * 2,
        compiler_params=params(),
        cost_estimate=cost(0.5),
    )(*arrays)


def halves(total, segments):
    first, second, at = [], [], 0
    for rows in segments:
        first.append(total[at : at + rows // 2])
        second.append(total[at + rows // 2 : at + rows])
        at += rows
    return jnp.concatenate(first, axis=0), jnp.concatenate(second, axis=0)


def bit_orders(batch, blocks):
    n = int(math.log2(batch * blocks))
    seq_bits = int(math.log2(blocks))
    rest = list(range(seq_bits, n - 3)) + list(range(seq_bits))
    top = [n - 3, n - 2, n - 1]
    return [*top, *rest], [top[0], top[2], top[1], *rest], rest


def places(order, rows):
    n = len(order)
    place = np.arange(2**n)
    rel = np.zeros(2**n, np.int32)
    for k, bit in enumerate(order):
        rel |= ((place >> (n - 1 - k)) & 1).astype(np.int32) << bit
    out = np.zeros((8, 2**n * rows), np.int32)
    out[0] = np.repeat(rel, rows)
    out[1] = np.tile(np.arange(rows), 2**n)
    return out


def swap_pair(i):
    return (i & 1) * 2 + lax.shift_right_logical(i, 1)


def smem():
    return pl.BlockSpec(memory_space=pltpu.SMEM)


def masked_rows(
    batch, blocks, scalars, mask_flags, msg1, recv1, num, den, grad, out_weight, vecs,
    gate_up_weight, down_weight,
):
    seqs, block_len = mask_flags.shape
    tokens = seqs * block_len
    shards = batch * blocks
    others = blocks - 1
    n = FF // CHUNK
    half = D // 2
    order_x, order_y, order_rest = bit_orders(batch, blocks)
    top_bit = len(order_x) - 3
    vmem, hbm = pl.BlockSpec(memory_space=pltpu.VMEM), pl.BlockSpec(memory_space=pl.ANY)
    f32_full = jax.ShapeDtypeStruct((tokens, D), F32)
    bf_full = jax.ShapeDtypeStruct((tokens, D), BF16)
    wide = jax.ShapeDtypeStruct((half, FF), BF16)
    tall = jax.ShapeDtypeStruct((FF // 2 + half, D), BF16)
    chunks = lambda rows, width: pltpu.VMEM((n, rows, width), BF16)
    grads = [wide] * 4 + [tall] * 2
    square_s = pltpu.VMEM((half, D), BF16)
    weights_s = [
        chunks(D, CHUNK), chunks(D, CHUNK), chunks(CHUNK, D), chunks(D, CHUNK), chunks(D, CHUNK),
        chunks(CHUNK // 2, D), chunks(CHUNK // 2, D),
    ]
    tile_s = [
        pltpu.VMEM((D, CAP), BF16), pltpu.VMEM((D, CAP), BF16), chunks(CAP, CHUNK),
        chunks(CAP, CHUNK), chunks(CAP, CHUNK), pltpu.VMEM((CAP, D), F32), pltpu.VMEM((CAP, D), F32),
    ]
    held = [
        places(order_x, D // shards), places(order_y, D // shards),
        places(order_rest, FF // shards),
    ]
    small = jax.ShapeDtypeStruct((8, D), F32)
    *sums, att, invden, dheads, small_sums = pl.pallas_call(
        functools.partial(
            masked_kernel, others, seqs, block_len, D // shards, FF // shards, shards // 8, top_bit
        ),
        name="masked_rows",
        out_shape=grads + [bf_full, f32_full, bf_full, small],
        in_specs=[smem()] + [vmem] * (10 + len(recv1)) + [hbm] * 2,
        out_specs=[hbm] * 6 + [vmem] * 4,
        scratch_shapes=weights_s + [square_s, square_s] + tile_s
        + [pltpu.SemaphoreType.DMA((3, n)), pltpu.SemaphoreType.DMA((8, n))],
        compiler_params=params(62),
        cost_estimate=cost(60),
    )(
        scalars, mask_flags, msg1, *recv1, num, den, grad, out_weight, vecs, *held, gate_up_weight,
        down_weight,
    )
    *sums, dheads, small_sums = pl.pallas_call(
        functools.partial(
            more_tiles_kernel, seqs, block_len, D // shards, FF // shards, shards // 8, top_bit
        ),
        name="more_masked_rows",
        out_shape=grads + [bf_full, small],
        in_specs=[smem()] + [hbm] * 18,
        out_specs=[hbm] * 8,
        input_output_aliases={11 + k: k for k in range(8)},
        scratch_shapes=[
            pltpu.VMEM(mask_flags.shape, jnp.int32), pltpu.VMEM((tokens, D), BF16),
            pltpu.VMEM((tokens, D), BF16), pltpu.VMEM((D, D), BF16), pltpu.VMEM((16, D), F32),
        ]
        + [pltpu.VMEM(h.shape, jnp.int32) for h in held]
        + weights_s
        + [square_s, square_s, pltpu.VMEM((tokens, D), BF16), pltpu.VMEM((8, D), F32)]
        + tile_s
        + [pltpu.SemaphoreType.DMA],
        compiler_params=params(62),
        cost_estimate=cost(1),
    )(
        scalars, mask_flags, att, grad, out_weight, vecs, *held, gate_up_weight, down_weight, *sums,
        dheads, small_sums,
    )
    return (*sums, att, invden, dheads, small_sums)


def on_device(
    hidden_states, mask_flags, block_offsets, alibi_slopes, mask_embedding, qkv_weight, query_bias,
    value_bias, out_weight, out_bias, first_gain, first_shift, gate_up_weight, down_weight,
    down_bias, second_gain, second_shift, output_grad,
):
    seqs, block_len = mask_flags.shape
    tokens = seqs * block_len
    batch, blocks = lax.axis_size("batch"), lax.axis_size("seq")
    shards = batch * blocks
    z = lax.axis_index("seq")
    me = lax.axis_index("batch") * blocks + z
    order_x, order_y, order_rest = bit_orders(batch, blocks)
    seq_bits = int(math.log2(blocks))
    place_y = places(order_y, D // shards)
    top_bit = len(order_x) - 3
    n = FF // CHUNK
    half = D // 2
    square = jax.ShapeDtypeStruct((half, D), BF16)
    others = blocks - 1
    vmem = pl.BlockSpec(memory_space=pltpu.VMEM)
    f32_full = jax.ShapeDtypeStruct((tokens, D), F32)
    bf_full = jax.ShapeDtypeStruct((tokens, D), BF16)
    last = [()]

    def after(*values):
        tied = lax.optimization_barrier((values, last[0]))[0]
        return tied if len(values) > 1 else tied[0]

    def done(value):
        last[0] = value

    def along(value, axis, pairs):
        return lax.ppermute(value, axis, pairs)

    def flip(value, bit):
        if bit >= seq_bits:
            axis, size, mask = "batch", batch, 1 << (bit - seq_bits)
        else:
            axis, size, mask = "seq", blocks, 1 << bit
        return along(value, axis, [(i, i ^ mask) for i in range(size)])

    def gathered(value, between):
        got = []
        for at in range(seq_bits):
            got.append(flip(jnp.concatenate([value, *after(*got, value)[:-1]], axis=0) if got else value, at))
            between[at]()
        return got

    nothing = lambda: None
    fixed = lambda shape: pl.BlockSpec(shape, lambda i: (0,) * len(shape))
    head_shape, tail_shape = (block_len, D), (tokens - block_len, D)
    x, x_head, x_tail, vecs, flagx, scalars = pl.pallas_call(
        functools.partial(inputs_kernel, seqs, block_len, blocks),
        name="inputs",
        grid=(1,),
        out_shape=(
            bf_full, jax.ShapeDtypeStruct(head_shape, BF16), jax.ShapeDtypeStruct(tail_shape, BF16),
            jax.ShapeDtypeStruct((16, D), F32), jax.ShapeDtypeStruct((tokens, LANES), F32),
            jax.ShapeDtypeStruct((8,), jnp.int32),
        ),
        in_specs=[smem(), smem(), fixed((tokens, D)), fixed((seqs, block_len))] + [fixed((D,))] * 9,
        out_specs=[
            fixed((tokens, D)), fixed(head_shape), fixed(tail_shape), fixed((16, D)),
            fixed((tokens, LANES)), smem(),
        ],
        compiler_params=params(),
        cost_estimate=cost(1),
    )(
        alibi_slopes, block_offsets.reshape(1, seqs), hidden_states.reshape(tokens, D), mask_flags,
        mask_embedding, value_bias, out_bias, first_gain, first_shift, down_bias, second_gain,
        second_shift, query_bias,
    )

    near = [(i, i ^ 1) for i in range(blocks)]
    centre, outward = [(1, 2), (2, 1)], [(1, 0), (2, 3)]
    hops = blocks == 4

    def round_one(rows):
        if hops:
            return along(rows, "seq", near), along(rows, "seq", centre)
        return tuple(
            along(rows, "seq", [(i, i ^ k) for i in range(blocks)]) for k in range(1, blocks)
        )

    def round_two(got):
        return along(got[1], "seq", outward), along(got[0], "seq", centre)

    def held(*values):
        values = after(*values)
        done(values)
        return values

    head1 = round_one(after(x_head))

    v, wx, num, den, msg1, g, qm = pl.pallas_call(
        functools.partial(prep_kernel, seqs, block_len),
        name="masked_prep",
        out_shape=(
            bf_full, f32_full, f32_full, f32_full, jax.ShapeDtypeStruct((MSG, D), F32),
            jax.ShapeDtypeStruct((D, LANES), BF16), jax.ShapeDtypeStruct((8, D), F32),
        ),
        in_specs=[smem(), smem()] + [vmem] * 3,
        out_specs=[vmem] * 7,
        compiler_params=params(),
        cost_estimate=cost(10),
    )(alibi_slopes, scalars, x, qkv_weight, vecs)
    done(msg1)
    recv1 = [along(msg1, "seq", [(i, i ^ k) for i in range(blocks)]) for k in range(1, blocks)]

    q_own = project([[after(x)]], qkv_weight, vecs, 0, 1, LOG2E * HD**-0.5)
    done(q_own)
    *head1, x_tail = held(*head1, x_tail)
    recv1 = list(held(*recv1, recv1[-1]))[:-1]
    tail1 = round_one(after(x_tail))

    gate_s, gate_k, up_s, up_k, down_s, down_k, att_m, invden, dheads, small_a = masked_rows(
        batch, blocks, scalars, mask_flags, msg1, recv1, num, den,
        after(output_grad.reshape(tokens, D)), out_weight, vecs, gate_up_weight, down_weight,
    )
    done(small_a)
    tail1 = held(*tail1)
    down_r, up_r, gate_r = (
        flip(down_s, order_x[0]), flip(up_s, order_y[0]), flip(gate_s, order_x[0])
    )
    if hops:
        head2 = round_two(after(*head1))

    kv = {1: project([[after(head1[0])], [tail1[0]]], qkv_weight, vecs, 1, 2)}
    done(kv[1])
    uv, ud, msg2 = pl.pallas_call(
        functools.partial(inner_kernel, seqs, block_len),
        name="masked_inner",
        out_shape=(f32_full, f32_full, jax.ShapeDtypeStruct((MSG, D), F32)),
        in_specs=[smem()] + [vmem] * 4,
        out_specs=[vmem] * 3,
        compiler_params=params(),
        cost_estimate=cost(60),
    )(alibi_slopes, after(dheads), att_m, invden, vecs)
    done(msg2)

    down_k, down_s = add_split(*after(down_k, down_r), "add_core_down")
    done(down_k)
    down_r = flip(down_s, order_x[1])
    if hops:
        head2 = held(*head2)

    def between_one():
        nonlocal up_k, up_r, gate_k, gate_r
        up_k, up_s2 = add_split(*after(up_k, up_r), "add_core_up")
        done(up_k)
        up_r = flip(up_s2, order_y[1])
        gate_k, gate_s2 = add_split(*after(gate_k, gate_r), "add_core_gate")
        done(gate_k)
        gate_r = flip(gate_s2, order_x[1])

    def between_two():
        kv[0] = project([[after(x)]], qkv_weight, vecs, 1, 2)
        done(kv[0])

    recv2 = gathered(after(msg2), [between_one, between_two] + [nothing] * seq_bits)
    recv2 = list(held(*recv2, msg2))[:-1]
    if hops:
        tail2 = round_two(after(*tail1))

    input_grad, value_s, value_k, small = pl.pallas_call(
        functools.partial(value_kernel, others, seqs, block_len, D // shards),
        name="value_grads",
        out_shape=(
            bf_full, jax.ShapeDtypeStruct((2 * SMALL + half, D), BF16),
            jax.ShapeDtypeStruct((half, D), BF16), jax.ShapeDtypeStruct((SMALL, D), F32),
        ),
        in_specs=[smem()] + [vmem] * (13 + len(recv1) + len(recv2)),
        out_specs=[vmem] * 4,
        scratch_shapes=[pltpu.VMEM((tokens, D), BF16), pltpu.VMEM((tokens, LANES), F32)],
        compiler_params=params(),
        cost_estimate=cost(60),
    )(
        scalars, flagx, msg1, msg2, *recv1, *recv2, uv, ud, wx, v, after(x), qkv_weight, g, vecs,
        place_y, small_a,
    )
    done(small)

    down_k, down_s = add_split(*after(down_k, down_r), "add_xy_down")
    done(down_k)
    down_r = flip(down_s, order_x[2])

    if hops:
        tail2 = held(*tail2)
        far = along(jnp.concatenate([head2[1], tail2[1]], axis=0), "seq", outward)
        kv[2] = project([[after(head2[0]), head2[1]], list(tail2)], qkv_weight, vecs, 1, 2)
    else:
        kv[2] = project([[after(head1[1])], [tail1[1]]], qkv_weight, vecs, 1, 2)
    done(kv[2])
    value_r = flip(after(value_s), order_y[0])

    up_k, up_s = add_split(*after(up_k, up_r), "add_xy_up")
    done(up_k)
    up_r = flip(up_s, order_y[2])
    gate_k, gate_s = add_split(*after(gate_k, gate_r), "add_xy_gate")
    done(gate_k)
    gate_r = flip(gate_s, order_x[2])
    value_k, value_s, small = add_small(*after(value_k, small, value_r), "add_core_value")
    done(small)
    value_r = flip(value_s, order_y[1])

    segments = [CHUNK // 2, half // n]

    def down_step(bit):
        nonlocal down_k, down_r
        total = (down_k.astype(F32) + down_r.astype(F32)).astype(BF16)
        down_k, down_s = halves(total, segments)
        done(down_k)
        segments[:] = [rows // 2 for rows in segments]
        down_r = flip(down_s, bit)

    down_k, down_r = after(down_k, down_r)
    down_step(order_rest[0])

    if hops:
        kv[3] = project(
            [[head1[1], (after(far), 0)], [tail1[1], (far, block_len)]], qkv_weight, vecs, 1, 2
        )
    else:
        for k in range(3, blocks):
            kv[k] = project([[after(head1[k - 1])], [tail1[k - 1]]], qkv_weight, vecs, 1, 2)
    done(kv[others])

    attended = pl.pallas_call(
        functools.partial(attention_kernel, others),
        name="dense_attention",
        out_shape=bf_full,
        grid=(seqs,),
        in_specs=[smem(), smem(), pl.BlockSpec((block_len, D), lambda s: (s, 0))]
        + [pl.BlockSpec((block_len, 2 * D), lambda s: (s, 0))] * blocks
        + [vmem] * (others + 2),
        out_specs=pl.BlockSpec((block_len, D), lambda s: (s, 0)),
        scratch_shapes=[
            pltpu.VMEM((H, block_len, block_len), F32), pltpu.VMEM((H, block_len, LANES), BF16),
        ],
        compiler_params=params(),
        cost_estimate=cost(60),
    )(alibi_slopes, scalars, after(q_own), *[kv[k] for k in range(blocks)], *recv1, msg1, vecs)
    done(attended)

    gu_k, gu_s = add_join(after(gate_k, gate_r, up_k, up_r), "add_gate_up")
    done(gu_k)
    gu_r = flip(gu_s, order_rest[0])
    value_k, value_s, small = add_small(*after(value_k, small, value_r), "add_xy_value")
    done(small)
    value_r = flip(value_s, order_y[2])
    down_k, down_r = after(down_k, down_r)
    down_step(order_rest[1])

    output = pl.pallas_call(
        dense_kernel,
        name="dense_ffn",
        out_shape=bf_full,
        grid=(n,),
        in_specs=[vmem] * 4
        + [
            pl.BlockSpec((D, CHUNK), lambda i: (0, i)),
            pl.BlockSpec((D, CHUNK), lambda i: (0, n + i)),
            pl.BlockSpec((CHUNK, D), lambda i: (i, 0)),
        ],
        out_specs=vmem,
        scratch_shapes=[
            pltpu.VMEM((tokens, D), F32), pltpu.VMEM((tokens, D), BF16), pltpu.VMEM((tokens, D), F32),
        ],
        compiler_params=params(),
        cost_estimate=cost(60),
    )(x, after(attended), out_weight, vecs, gate_up_weight, gate_up_weight, down_weight)
    done(output)

    value_k, value_s, small = add_small(*after(value_k, small, value_r), "add_value")
    done(small)
    value_r = flip(value_s, order_rest[0])
    for bit in order_rest[1:]:
        total = sum(p.astype(F32) for p in after(gu_k, gu_r)).astype(BF16)
        gu_k, gu_s = halves(total, [total.shape[0]])
        done(gu_k)
        gu_r = flip(gu_s, bit)
        value_k, value_s, small = add_small(*after(value_k, small, value_r), "add_value")
        done(small)
        value_r = flip(value_s, bit)
    for bit in order_rest[2:]:
        down_k, down_r = after(down_k, down_r)
        down_step(bit)
    down_k, down_r, gu_k, gu_r, value_k, small, value_r = after(
        down_k, down_r, gu_k, gu_r, value_k, small, value_r
    )
    grad_down_out = down_k.astype(F32) + down_r.astype(F32)
    grad_gateup = gu_k.astype(F32) + gu_r.astype(F32)
    grad_value = value_k.astype(F32) + value_r[2 * SMALL :].astype(F32)
    small = small + (value_r[:SMALL].astype(F32) + value_r[SMALL : 2 * SMALL].astype(F32))
    rows_f = FF // shards

    rows_d = D // shards
    mine = lax.dynamic_slice_in_dim(small, me * rows_d, rows_d, 1)
    emb = lax.dynamic_slice_in_dim(mask_embedding.astype(F32), me * rows_d, rows_d, 0)
    grad_q = emb[:, None] * small[20][None, :]
    grad_k = jnp.repeat(mine[8 : 8 + H].T, HD, axis=1) * (qm[0:1, :] * (HD**-0.5))
    grad_qkv = jnp.concatenate([grad_q, grad_k, grad_value], axis=1)

    shape = (seqs, block_len, D)
    return (
        output.reshape(shape), input_grad.reshape(shape), mine[6], grad_qkv, mine[20], mine[7],
        grad_down_out[rows_f:], mine[5], mine[3], mine[4], grad_gateup, grad_down_out[:rows_f],
        mine[2], mine[0], mine[1],
    )


def solution(mesh):
    data, pairs = P("batch", "seq", None), P("batch", "seq")
    in_specs = (data, pairs, pairs) + (P(),) * 14 + (data,)
    vector, matrix = P(("batch", "seq")), P(("batch", "seq"), None)
    out_specs = (
        data, data, vector, matrix, vector, vector, matrix, vector, vector, vector, matrix, matrix,
        vector, vector, vector,
    )
    return jax.shard_map(
        on_device, mesh=mesh, in_specs=in_specs, out_specs=out_specs, check_vma=False
    )
```

```python
import functools
import math

import jax
import jax.numpy as jnp
import numpy as np
from jax import lax
from jax.experimental import pallas as pl
from jax.experimental.pallas import tpu as pltpu
from jax.sharding import PartitionSpec as P

D = 768
FF = 3072
H = 12
HD = 64
CAP = 192
CHUNK = 768
LANES = 128
MSG = 16
SMALL = 24

F32 = jnp.float32
BF16 = jnp.bfloat16


def params(limit=62):
    return pltpu.CompilerParams(vmem_limit_bytes=limit * 1024 * 1024)


def cost(micros):
    return pl.CostEstimate(flops=int(micros * 1.15e9), bytes_accessed=1024, transcendentals=0)


def dot(a, b):
    return lax.dot_general(a, b, (((1,), (0,)), ((), ())), preferred_element_type=F32)


def dot_nt(a, b):
    return lax.dot_general(a, b, (((1,), (1,)), ((), ())), preferred_element_type=F32)


def dot_tn(a, b):
    return lax.dot_general(a, b, (((0,), (0,)), ((), ())), preferred_element_type=F32)


def split2(v):
    high = v.astype(BF16)
    return high, (v - high.astype(F32)).astype(BF16)


def dot_wide(v, b):
    high, rest = split2(v)
    return dot(high, b) + dot(rest, b)


def expand_one():
    row = lax.broadcasted_iota(jnp.int32, (LANES, D), 0)
    lane = lax.broadcasted_iota(jnp.int32, (LANES, D), 1)
    return jnp.where(lax.shift_right_logical(lane, 6) == row, 1.0, 0.0).astype(BF16)


def expand_seq(s):
    row = lax.broadcasted_iota(jnp.int32, (LANES, D), 0)
    lane = lax.broadcasted_iota(jnp.int32, (LANES, D), 1)
    return jnp.where(lax.shift_right_logical(lane, 6) + 16 * s == row, 1.0, 0.0).astype(BF16)


def reduce_seq(s):
    row = lax.broadcasted_iota(jnp.int32, (D, LANES), 0)
    lane = lax.broadcasted_iota(jnp.int32, (D, LANES), 1)
    return jnp.where(lax.shift_right_logical(row, 6) + 16 * s == lane, 1.0, 0.0).astype(BF16)


def reduce_one():
    row = lax.broadcasted_iota(jnp.int32, (D, LANES), 0)
    lane = lax.broadcasted_iota(jnp.int32, (D, LANES), 1)
    return jnp.where(lax.shift_right_logical(row, 6) == lane, 1.0, 0.0).astype(BF16)


def permuting(place_row, me, rows):
    n = place_row.shape[1]
    distance = place_row[0:1, :]
    source = (distance ^ me) * rows + place_row[1:2, :]
    row = lax.broadcasted_iota(jnp.int32, (n, n), 0)
    return jnp.where(row == source, 1.0, 0.0).astype(BF16)


def decay(slope_lane, block_len):
    t = lax.broadcasted_iota(jnp.int32, (block_len, D), 0).astype(F32)
    return jnp.exp(-slope_lane * t), jnp.exp(-slope_lane * (block_len - 1.0 - t))


def head_decay(slope, block_len):
    row = lax.broadcasted_iota(jnp.int32, (block_len, block_len), 0)
    lane = lax.broadcasted_iota(jnp.int32, (block_len, block_len), 1)
    return jnp.exp(-slope * jnp.abs(row - lane).astype(F32)).astype(BF16)


def local_decay_sums(slopes_ref, wide, packed, wide_out, packed_out, block_len, seqs):
    lane = lax.broadcasted_iota(jnp.int32, (block_len, LANES), 1)
    total = jnp.zeros((block_len, LANES), F32)
    for pair in range(H // 2):
        low, high = pair * LANES, (pair + 1) * LANES
        right = jnp.concatenate([wide[s][:, low:high] for s in range(seqs)] + [packed], axis=1)
        even = dot(head_decay(slopes_ref[2 * pair], block_len), right)
        odd = dot(head_decay(slopes_ref[2 * pair + 1], block_len), right)
        for s in range(seqs):
            rows = slice(s * block_len, (s + 1) * block_len)
            at = slice(s * LANES, (s + 1) * LANES)
            wide_out[rows, low:high] = jnp.where(lane < HD, even[:, at], odd[:, at]).astype(
                wide_out.dtype
            )
        at = slice(seqs * LANES, (seqs + 1) * LANES)
        total = jnp.where((lane & 15) == 2 * pair, even[:, at], total)
        total = jnp.where((lane & 15) == 2 * pair + 1, odd[:, at], total)
    packed_out[...] = total


def lane_value(row, index):
    lane = lax.broadcasted_iota(jnp.int32, row.shape, 1)
    return jnp.sum(jnp.where(lane == index, row, 0.0), axis=1, keepdims=True)


GELU = (
    0.7978849414614602, 0.03633308456815623, -3.259496805730905e-05, -5.530619733817487e-05,
    3.9647451634764645e-06, -1.322634044387524e-07, 1.756172658552303e-09,
)


def normal_cdf(v):
    square = v * v
    poly = GELU[6]
    for c in GELU[5::-1]:
        poly = poly * square + c
    return 0.5 + 0.5 * jnp.tanh(v * poly)


def norm_rows(v):
    centred = v - jnp.mean(v, axis=1, keepdims=True)
    scale = lax.rsqrt(jnp.mean(centred * centred, axis=1, keepdims=True) + 1e-05)
    return centred * scale, scale


def norm_back(upstream, normed, scale, gain):
    scaled = upstream * gain
    return scale * (
        scaled
        - jnp.mean(scaled, axis=1, keepdims=True)
        - normed * jnp.mean(scaled * normed, axis=1, keepdims=True)
    )


def colsum(v):
    return jnp.sum(v, axis=0, keepdims=True)


def inputs_kernel(seqs, block_len, blocks, slopes_ref, offs_ref, hidden_ref, flags_ref, *refs):
    vec_refs, (x_ref, vecs_ref, flagx_ref, sc_ref) = refs[:-4], refs[-4:]
    emb = vec_refs[0][...].astype(F32).reshape(1, D)
    lane = lax.broadcasted_iota(jnp.int32, (1, D), 1)
    slope = jnp.zeros((1, D), F32)
    for h in range(H):
        slope = jnp.where(lax.shift_right_logical(lane, 6) == h, slopes_ref[h], slope)
    vecs_ref[...] = jnp.zeros_like(vecs_ref)
    vecs_ref[0:1, :] = slope
    for k, r in enumerate(vec_refs):
        vecs_ref[k + 1 : k + 2, :] = r[...].astype(F32).reshape(1, D)
    sc_ref[0] = lax.axis_index("batch") * blocks + lax.axis_index("seq")
    sc_ref[1] = lax.axis_index("seq")
    sc_ref[2] = jnp.maximum(1, (jnp.sum(flags_ref[...]) + CAP - 1) // CAP)
    flags = flags_ref[...].astype(F32)
    for s in range(seqs):
        rows = slice(s * block_len, (s + 1) * block_len)
        column = jnp.broadcast_to(flags[s : s + 1, :], (LANES, block_len)).T
        flagx_ref[rows, :] = column
        mask = jnp.broadcast_to(column[:, 0:1], (block_len, D)) > 0.5
        x_ref[rows, :] = jnp.where(mask, emb, hidden_ref[rows, :].astype(F32)).astype(BF16)
        sc_ref[4 + s] = offs_ref[0, s]


def project_kernel(scale, x_ref, w_ref, bias_ref, out_ref):
    out = dot(x_ref[...], w_ref[...])
    if scale is not None:
        out = (out + bias_ref[9:10, :]) * scale
    out_ref[...] = out.astype(BF16)


def project(x, weight, vecs, first, count, scale=None):
    return pl.pallas_call(
        functools.partial(project_kernel, scale),
        name="project",
        out_shape=jax.ShapeDtypeStruct((x.shape[0], count * D), BF16),
        grid=(count,),
        in_specs=[
            pl.BlockSpec(x.shape, lambda i: (0, 0)),
            pl.BlockSpec((D, D), lambda i: (0, first + i)), pl.BlockSpec((16, D), lambda i: (0, 0)),
        ],
        out_specs=pl.BlockSpec((x.shape[0], D), lambda i: (0, i)),
        compiler_params=params(),
        cost_estimate=cost(0.1),
    )(x, weight, vecs)


def prep_kernel(
    seqs, block_len, slopes_ref, sc_ref, x_ref, wqkv_ref, vecs_ref,
    v_ref, wx_ref, num_ref, den_ref, msg_ref, g_ref, qm_ref,
):
    slope_lane = vecs_ref[0:1, :]
    emb8 = jnp.broadcast_to(vecs_ref[1:2, :], (8, D)).astype(BF16)
    qm = (dot(emb8, wqkv_ref[:, 0:D]) + vecs_ref[9:10, :]).astype(BF16).astype(F32)
    qm_ref[...] = qm
    scaled = wqkv_ref[:, D : 2 * D].astype(F32) * (qm[0:1, :] * (HD**-0.5))
    g = dot_wide(scaled, reduce_one())
    g_high, g_rest = split2(g)
    g_ref[...] = g_high
    expand = expand_one()
    dec_f, dec_r = decay(slope_lane, block_len)
    weighted = []
    packed = jnp.zeros((block_len, LANES), F32)
    lane = lax.broadcasted_iota(jnp.int32, (block_len, LANES), 1)
    msg_ref[...] = jnp.zeros_like(msg_ref)
    lane8 = lax.broadcasted_iota(jnp.int32, (1, D), 1)
    offs_row = jnp.zeros((1, D), F32)
    for s in range(seqs):
        rows = slice(s * block_len, (s + 1) * block_len)
        x = x_ref[rows, :]
        a = dot(x, g_high) + dot(x, g_rest)
        v = dot(x, wqkv_ref[:, 2 * D :]).astype(BF16)
        v_ref[rows, :] = v
        top = jnp.max(a, axis=0, keepdims=True)
        w = jnp.exp(a - top)
        wx = dot_wide(w, expand)
        w = jnp.where(lane < 16, w, 0.0)
        packed += pltpu.roll(w, 16 * s, 1) if s else w
        vw = v.astype(F32) * wx
        weighted.append(vw.astype(BF16))
        t1, t2 = split2(top)
        t3 = (top - t1.astype(F32) - t2.astype(F32)).astype(BF16)
        tops = sum(dot(jnp.broadcast_to(t, (8, LANES)), expand) for t in (t1, t2, t3))
        msg_ref[s : s + 1, :] = tops[0:1, :]
        msg_ref[seqs + s : seqs + s + 1, :] = colsum(dec_r * vw)
        msg_ref[2 * seqs + s : 2 * seqs + s + 1, :] = colsum(dec_r * wx)
        msg_ref[3 * seqs + s : 3 * seqs + s + 1, :] = colsum(dec_f * vw)
        msg_ref[4 * seqs + s : 4 * seqs + s + 1, :] = colsum(dec_f * wx)
        offs_row = jnp.where(lane8 == s, sc_ref[4 + s].astype(F32), offs_row)
    msg_ref[MSG - 1 : MSG, :] = offs_row
    wx_ref[...] = packed
    local_decay_sums(
        slopes_ref, weighted, packed.astype(BF16), num_ref, den_ref, block_len, seqs
    )


def masked_kernel(others, seqs, block_len, rows_d, rows_f, low_count, top_bit, sc_ref, *refs):
    (flags_ref, msg_ref, *refs) = refs
    recv_refs, refs = refs[:others], refs[others:]
    (
        num_ref, den_ref, og_ref, wo_ref, vecs_ref, placex_ref, placey_ref, placed_ref,
        wgu_ref, wd_ref,
        gs_ref, gk_ref, us_ref, uk_ref, ds_ref, dk_ref,
        att_ref, invden_ref, dheads_ref, small_ref,
        wg_s, wu_s, wd_s, g_s, u_s, dk_s, ds_s, os_s, ok_s, lowx_s, lowy_s, mixed_s, d1_s, d2_s,
        acc_s, fn_s, in_sems, out_sems,
    ) = refs
    n = FF // CHUNK
    half = D // 2
    wide = CHUNK // 2
    me, z = sc_ref[0], sc_ref[1]
    tokens = seqs * block_len
    core = lax.shift_right_logical(me, top_bit) & 1
    plane = lax.shift_right_logical(me, top_bit + 1)

    def at(i):
        return pl.ds(pl.multiple_of(i * CHUNK, CHUNK), CHUNK)

    unit = wide + half // n

    def out_stores():
        copies = []
        for i in range(n):
            rows = pl.ds(i * unit + wide, half // n)
            for k, (inside, outside) in enumerate(((ok_s, dk_ref), (os_s, ds_ref))):
                copies.append(
                    pltpu.make_async_copy(
                        inside.at[pl.ds(i * (half // n), half // n), :], outside.at[rows, :],
                        out_sems.at[6 + k, i],
                    )
                )
        return copies

    def loads(i):
        up_at = pl.ds(pl.multiple_of(FF + i * CHUNK, CHUNK), CHUNK)
        return [
            pltpu.make_async_copy(wgu_ref.at[:, at(i)], wg_s.at[i], in_sems.at[0, i]),
            pltpu.make_async_copy(wgu_ref.at[:, up_at], wu_s.at[i], in_sems.at[1, i]),
            pltpu.make_async_copy(wd_ref.at[at(i), :], wd_s.at[i], in_sems.at[2, i]),
        ]

    def stores(i):
        rel = i ^ plane
        rows = pl.ds(pl.multiple_of(swap_pair(rel) * unit, 32), wide)
        rows_y = pl.ds(pl.multiple_of(rel * unit, 32), wide)
        left, right = pl.ds(0, half), pl.ds(half, half)
        return [
            pltpu.make_async_copy(g_s.at[i, pl.ds(0, half)], gk_ref.at[:, at(i)], out_sems.at[0, i]),
            pltpu.make_async_copy(g_s.at[i, pl.ds(half, half)], gs_ref.at[:, at(i)], out_sems.at[1, i]),
            pltpu.make_async_copy(u_s.at[i, pl.ds(0, half)], uk_ref.at[:, at(i)], out_sems.at[2, i]),
            pltpu.make_async_copy(u_s.at[i, pl.ds(half, half)], us_ref.at[:, at(i)], out_sems.at[3, i]),
            pltpu.make_async_copy(dk_s.at[i, :, left], dk_ref.at[rows, left], out_sems.at[4, i]),
            pltpu.make_async_copy(ds_s.at[i, :, left], ds_ref.at[rows, left], out_sems.at[5, i]),
            pltpu.make_async_copy(dk_s.at[i, :, right], dk_ref.at[rows_y, right], out_sems.at[8, i]),
            pltpu.make_async_copy(ds_s.at[i, :, right], ds_ref.at[rows_y, right], out_sems.at[9, i]),
        ]

    for i in range(n):
        for copy in loads(i):
            copy.start()

    slope_lane = vecs_ref[0:1, :]
    dec_f, dec_r = decay(slope_lane, block_len)
    invden = jnp.zeros((block_len, LANES), F32)
    for s in range(seqs):
        rows = slice(s * block_len, (s + 1) * block_len)

        def row(ref, kind):
            return ref[kind * seqs + s : kind * seqs + s + 1, :]

        own_off = lane_value(msg_ref[MSG - 1 : MSG, :], s)
        top = row(msg_ref, 0)
        for r in recv_refs:
            top = jnp.maximum(top, row(r, 0))
        own = jnp.exp(row(msg_ref, 0) - top)
        zero = jnp.zeros((1, D), F32)
        left_v, left_z, right_v, right_z = zero, zero, zero, zero
        for k, r in enumerate(recv_refs):
            gap = jnp.abs(lane_value(r[MSG - 1 : MSG, :], s) - own_off) - (block_len - 1.0)
            factor = jnp.exp(row(r, 0) - top - slope_lane * gap)
            is_left = (z ^ (k + 1)) < z
            f_left = jnp.where(is_left, factor, 0.0)
            f_right = jnp.where(is_left, 0.0, factor)
            left_v += f_left * row(r, 1)
            left_z += f_left * row(r, 2)
            right_v += f_right * row(r, 3)
            right_z += f_right * row(r, 4)
        den = own * dot_wide(den_ref[...], expand_seq(s)) + dec_f * left_z + dec_r * right_z
        num = own * num_ref[rows, :].astype(F32) + dec_f * left_v + dec_r * right_v
        inv = 1.0 / den
        invden = invden + dot_wide(inv * (1.0 / HD), reduce_seq(s))
        att_ref[rows, :] = (num * inv).astype(BF16)
    invden_ref[...] = invden
    rank = masked_ranks(flags_ref, seqs, tokens)
    small_ref[...] = jnp.zeros_like(small_ref)

    masked_tile(
        0, True, me, rows_d, rows_f, low_count, core, rank, att_ref, og_ref, wo_ref, vecs_ref,
        placex_ref, placey_ref, placed_ref, wg_s, wu_s, wd_s, g_s, u_s, dk_s, ds_s, os_s, ok_s,
        dheads_ref, small_ref, lowx_s, lowy_s, mixed_s, d1_s, d2_s, acc_s, fn_s, loads, stores,
    )
    for copy in out_stores():
        copy.start()
    for i in range(n):
        for copy in stores(i):
            copy.wait()
    for copy in out_stores():
        copy.wait()


def masked_tile(
    t, first, me, rows_d, rows_f, low_count, core, rank, att_ref, og_ref, wo_ref, vecs_ref,
    placex_ref, placey_ref, placed_ref, wg_s, wu_s, wd_s, g_s, u_s, dk_s, ds_s, os_ref, ok_ref,
    dheads_ref, small_ref, lowx_s, lowy_s, mixed_s, d1_s, d2_s, acc_s, fn_s, loads, stores,
):
    n = FF // CHUNK
    half = D // 2
    wide = CHUNK // 2
    tokens = att_ref.shape[0]

    def put(ref, value):
        ref[...] = (value if first else ref[...].astype(F32) + value).astype(BF16)

    place = lax.broadcasted_iota(jnp.int32, (CAP, tokens), 0) + t * CAP
    comp = jnp.where(place.astype(F32) == rank, 1.0, 0.0).astype(BF16)
    att_low = (dot(comp, att_ref[...]) + vecs_ref[2:3, :]).astype(BF16)
    first_sum = vecs_ref[1:2, :] + (dot(att_low, wo_ref[...]) + vecs_ref[3:4, :])
    first_normed, first_scale = norm_rows(first_sum)
    fn_s[...] = first_normed
    low = (first_normed * vecs_ref[4:5, :] + vecs_ref[5:6, :]).astype(BF16)
    lowx_s[...] = dot(low, permuting(placex_ref[...], me, rows_d)).astype(BF16).T
    lowy_s[...] = dot(low, permuting(placey_ref[...], me, rows_d)).astype(BF16).T
    acc_s[...] = jnp.zeros((CAP, D), F32)

    def forward(i, c):
        for copy in loads(i):
            copy.wait()
        gate = dot(low, wg_s[i])
        up = dot(low, wu_s[i])
        phi = normal_cdf(gate)
        act = gate * phi
        mixed = (act * up).astype(BF16)
        mixed_s[i] = mixed
        d2_s[i] = act.astype(BF16)
        slope = phi + gate * (jnp.exp(-0.5 * gate * gate) * ((2.0 * math.pi) ** -0.5))
        d1_s[i] = (up * slope).astype(BF16)
        acc_s[...] += dot(mixed, wd_s[i])
        return c

    lax.fori_loop(0, n, forward, 0)
    first_out = fn_s[...] * vecs_ref[4:5, :] + vecs_ref[5:6, :]
    normed, scale = norm_rows(first_out + (acc_s[...] + vecs_ref[6:7, :]))
    up = dot(comp, og_ref[...])
    grad_second = norm_back(up, normed, scale, vecs_ref[7:8, :])
    acc_s[...] = grad_second
    bg = grad_second.astype(BF16)
    small_ref[0:1, :] += colsum(up * normed)
    small_ref[1:2, :] += colsum(up)
    small_ref[2:3, :] += colsum(bg.astype(F32))
    change_d = permuting(placed_ref[...], me & (low_count - 1), rows_f)

    def backward(i, c):
        mixed_grad = dot_nt(bg, wd_s[i]).astype(BF16).astype(F32)
        gate_grad = (mixed_grad * d1_s[i].astype(F32)).astype(BF16)
        up_grad = (mixed_grad * d2_s[i].astype(F32)).astype(BF16)
        put(g_s.at[i], dot(lowx_s[...], gate_grad))
        put(u_s.at[i], dot(lowy_s[...], up_grad))
        mixed = mixed_s[i]
        low_half, high_half = mixed[:, :wide], mixed[:, wide:]
        keep = jnp.where(core == 0, low_half, high_half)
        send = jnp.where(core == 0, high_half, low_half)
        put(dk_s.at[i], dot_tn(dot(keep, change_d).astype(BF16), bg))
        put(ds_s.at[i], dot_tn(dot(send, change_d).astype(BF16), bg))
        for copy in stores(i):
            copy.start()
        acc_s[...] += dot_nt(gate_grad, wg_s[i]) + dot_nt(up_grad, wu_s[i])
        return c

    lax.fori_loop(0, n, backward, 0)
    grad_first = acc_s[...]
    first_normed = fn_s[...]
    grad = norm_back(grad_first, first_normed, first_scale, vecs_ref[4:5, :])
    small_ref[3:4, :] += colsum(grad_first * first_normed)
    small_ref[4:5, :] += colsum(grad_first)
    attn_grad = grad.astype(BF16)
    small_ref[5:6, :] += colsum(attn_grad.astype(F32))
    small_ref[6:7, :] += colsum(grad)
    for place_ref, columns in ((placex_ref, slice(0, half)), (placey_ref, slice(half, D))):
        moved = dot(att_low, permuting(place_ref[...], me, rows_d)).astype(BF16)
        grad_out = dot_tn(moved, attn_grad[:, columns])
        put(ok_ref.at[:, columns], grad_out[:half])
        put(os_ref.at[:, columns], grad_out[half:])
    heads = dot_nt(attn_grad, wo_ref[...]).astype(BF16)
    small_ref[7:8, :] += colsum(heads.astype(F32))
    put(dheads_ref, dot_tn(comp, heads))


def masked_ranks(flags_ref, seqs, tokens):
    flags = jnp.concatenate([flags_ref[s : s + 1, :] for s in range(seqs)], axis=1).astype(F32)
    before = lax.broadcasted_iota(jnp.int32, (tokens, tokens), 0)
    after = lax.broadcasted_iota(jnp.int32, (tokens, tokens), 1)
    upper = jnp.where(before < after, 1.0, 0.0).astype(BF16)
    rank = dot(jnp.broadcast_to(flags, (8, tokens)).astype(BF16), upper)[0:1, :]
    return jnp.where(flags > 0.5, rank, -1.0)


def more_tiles_kernel(seqs, block_len, rows_d, rows_f, low_count, top_bit, sc_ref, *refs):
    held, (wgu_ref, wd_ref), grads, scratch = refs[:8], refs[8:10], refs[18:26], refs[26:]
    (
        flags_s, att_s, og_s, wo_s, vecs_s, placex_s, placey_s, placed_s, wg_s, wu_s, wd_s, g_s, u_s,
        dk_s, ds_s, os_s, ok_s, dheads_s, small_s, lowx_s, lowy_s, mixed_s, d1_s, d2_s, acc_s, fn_s,
        sem,
    ) = scratch
    gs_ref, gk_ref, us_ref, uk_ref, ds_ref, dk_ref, dheads_ref, small_ref = grads
    n = FF // CHUNK
    half = D // 2
    wide = CHUNK // 2
    me = sc_ref[0]
    core = lax.shift_right_logical(me, top_bit) & 1
    plane = lax.shift_right_logical(me, top_bit + 1)

    def move(source, target):
        copy = pltpu.make_async_copy(source, target, sem)
        copy.start()
        copy.wait()

    part = half // n
    unit = wide + part
    pairs = [(dheads_ref, dheads_s), (small_ref, small_s)]
    for i in range(n):
        at = pl.ds(i * CHUNK, CHUNK)
        rel = i ^ plane
        rows = pl.ds(pl.multiple_of(swap_pair(rel) * unit, 32), wide)
        rows_y = pl.ds(pl.multiple_of(rel * unit, 32), wide)
        left, right = pl.ds(0, half), pl.ds(half, half)
        out_rows = pl.ds(i * unit + wide, part)
        pairs += [
            (dk_ref.at[out_rows, :], ok_s.at[pl.ds(i * part, part), :]),
            (ds_ref.at[out_rows, :], os_s.at[pl.ds(i * part, part), :]),
            (gk_ref.at[:, at], g_s.at[i, pl.ds(0, half)]),
            (gs_ref.at[:, at], g_s.at[i, pl.ds(half, half)]),
            (uk_ref.at[:, at], u_s.at[i, pl.ds(0, half)]),
            (us_ref.at[:, at], u_s.at[i, pl.ds(half, half)]),
            (dk_ref.at[rows, left], dk_s.at[i, :, left]),
            (ds_ref.at[rows, left], ds_s.at[i, :, left]),
            (dk_ref.at[rows_y, right], dk_s.at[i, :, right]),
            (ds_ref.at[rows_y, right], ds_s.at[i, :, right]),
        ]

    @pl.when(sc_ref[2] > 1)
    def _():
        for i in range(n):
            at = pl.ds(i * CHUNK, CHUNK)
            move(wgu_ref.at[:, at], wg_s.at[i])
            move(wgu_ref.at[:, pl.ds(FF + i * CHUNK, CHUNK)], wu_s.at[i])
            move(wd_ref.at[at, :], wd_s.at[i])
        for source, target in zip(held, scratch[:8]):
            move(source, target)
        for outside, inside in pairs:
            move(outside, inside)
        rank = masked_ranks(flags_s, seqs, seqs * block_len)

        def tile(t, carry):
            masked_tile(
                t, False, me, rows_d, rows_f, low_count, core, rank, att_s, og_s, wo_s, vecs_s,
                placex_s, placey_s, placed_s, wg_s, wu_s, wd_s, g_s, u_s, dk_s, ds_s, os_s, ok_s,
                dheads_s, small_s, lowx_s, lowy_s, mixed_s, d1_s, d2_s, acc_s, fn_s,
                lambda i: [], lambda i: [],
            )
            return carry

        lax.fori_loop(1, sc_ref[2], tile, 0)
        for outside, inside in pairs:
            move(inside, outside)


def inner_kernel(
    seqs, block_len, slopes_ref, dheads_ref, att_ref, invden_ref, vecs_ref, uv_ref, ud_ref, msg_ref
):
    slope_lane = vecs_ref[0:1, :]
    dec_f, dec_r = decay(slope_lane, block_len)
    wide = []
    packed = jnp.zeros((block_len, LANES), F32)
    msg_ref[...] = jnp.zeros_like(msg_ref)
    for s in range(seqs):
        rows = slice(s * block_len, (s + 1) * block_len)
        dheads = dheads_ref[rows, :].astype(F32)
        expand = expand_seq(s)
        inner = dot_wide(dheads * att_ref[rows, :].astype(F32), reduce_seq(s)) * invden_ref[...]
        packed += inner
        yv = dheads * dot_wide(invden_ref[...], expand)
        yd = dot_wide(inner, expand)
        wide.append(yv.astype(BF16))
        msg_ref[s : s + 1, :] = colsum(dec_r * yv)
        msg_ref[seqs + s : seqs + s + 1, :] = colsum(dec_r * yd)
        msg_ref[2 * seqs + s : 2 * seqs + s + 1, :] = colsum(dec_f * yv)
        msg_ref[3 * seqs + s : 3 * seqs + s + 1, :] = colsum(dec_f * yd)
    local_decay_sums(slopes_ref, wide, packed.astype(BF16), uv_ref, ud_ref, block_len, seqs)


def value_kernel(others, seqs, block_len, rows_d, sc_ref, *refs):
    (flags_ref, msg1_ref, msg2_ref, *refs) = refs
    recv1, recv2, refs = refs[:others], refs[others : 2 * others], refs[2 * others :]
    (
        uv_ref, ud_ref, wx_ref, v_ref, x_ref, wqkv_ref, g_ref, vecs_ref, placey_ref, smalla_ref,
        ig_ref, vs_ref, vk_ref, small_ref, dv_s, t_s,
    ) = refs
    me, z = sc_ref[0], sc_ref[1]
    slope_lane = vecs_ref[0:1, :]
    dec_f, dec_r = decay(slope_lane, block_len)
    reduce = reduce_one()
    embed = smalla_ref[6:7, :]
    half = D // 2
    for s in range(seqs):
        rows = slice(s * block_len, (s + 1) * block_len)

        def row(ref, kind):
            return ref[kind * seqs + s : kind * seqs + s + 1, :]

        own_off = lane_value(msg1_ref[MSG - 1 : MSG, :], s)
        top = row(msg1_ref, 0)
        for r in recv1:
            top = jnp.maximum(top, row(r, 0))
        own = jnp.exp(row(msg1_ref, 0) - top)
        zero = jnp.zeros((1, D), F32)
        left_v, left_d, right_v, right_d = zero, zero, zero, zero
        for k, (r1, r2) in enumerate(zip(recv1, recv2)):
            gap = jnp.abs(lane_value(r1[MSG - 1 : MSG, :], s) - own_off) - (block_len - 1.0)
            factor = jnp.exp(-slope_lane * gap)
            is_left = (z ^ (k + 1)) < z
            f_left = jnp.where(is_left, factor, 0.0)
            f_right = jnp.where(is_left, 0.0, factor)
            left_v += f_left * row(r2, 0)
            left_d += f_left * row(r2, 1)
            right_v += f_right * row(r2, 2)
            right_d += f_right * row(r2, 3)
        expand = expand_seq(s)
        weight = dot_wide(wx_ref[...], expand) * own
        uv = weight * (uv_ref[rows, :].astype(F32) + dec_f * left_v + dec_r * right_v)
        ud = weight * (dot_wide(ud_ref[...], expand) + dec_f * left_d + dec_r * right_d)
        dv = uv.astype(BF16)
        dv_s[rows, :] = dv
        t = dot_wide(uv * v_ref[rows, :].astype(F32) - ud * (1.0 / HD), reduce)
        t_s[rows, :] = t
        dx = dot_nt(dv, wqkv_ref[:, 2 * D :]) + dot_nt(t.astype(BF16), g_ref[...])
        masked = jnp.broadcast_to(flags_ref[rows, 0:1], (block_len, D)) > 0.5
        ig_ref[rows, :] = jnp.where(masked, 0.0, dx).astype(BF16)
        embed += colsum(jnp.where(masked, dx, 0.0))
    x = x_ref[...]
    xp = dot(x, permuting(placey_ref[...], me, rows_d)).astype(BF16)
    gv = dot_tn(xp, dv_s[...]).astype(BF16)
    vk_ref[...] = gv[:half]
    vs_ref[2 * SMALL :, :] = gv[half:]
    t_high, t_rest = split2(t_s[...])
    a_t = (dot_tn(t_high, x) + dot_tn(t_rest, x))[0:16, :]
    both = dot_wide(a_t, wqkv_ref[:, D : 2 * D]) * (HD**-0.5)
    head = lax.broadcasted_iota(jnp.int32, (16, D), 0)
    lane = lax.broadcasted_iota(jnp.int32, (16, D), 1)
    query = colsum(jnp.where(lax.shift_right_logical(lane, 6) == head, both, 0.0))
    q_high, q_rest = split2(jnp.broadcast_to(query, (8, D)))
    wq = wqkv_ref[:, 0:D]
    embed += (dot_nt(q_high, wq) + dot_nt(q_rest, wq))[0:1, :]
    small_ref[0:8, :] = smalla_ref[...]
    small_ref[6:7, :] = embed
    small_ref[8:24, :] = a_t
    small_ref[20:21, :] = query
    put_small(vs_ref, small_ref[...])


FEATS = 6
LOG2E = math.log2(math.e)


def attention_kernel(s, spec, slopes_ref, sc_ref, q_ref, own_ref, wk_ref, wv_ref, *refs):
    others = len(spec)
    count = sum(len(group) for group in spec)
    part_refs, msg_refs, (msg_ref, vecs_ref, out_ref, k_s, v_s) = (
        refs[:count], refs[count : count + others], refs[count + others :],
    )
    block_len = q_ref.shape[0]
    z = sc_ref[1]
    lane = lax.broadcasted_iota(jnp.int32, (block_len, LANES), 1)
    token = lax.broadcasted_iota(jnp.int32, (block_len, LANES), 0).astype(F32)
    head_of = lane // FEATS
    kind = lane - head_of * FEATS
    row = lax.broadcasted_iota(jnp.int32, (block_len, block_len), 0)
    col = lax.broadcasted_iota(jnp.int32, (block_len, block_len), 1)
    apart = jnp.abs(row - col).astype(F32) * LOG2E
    qvalue = jnp.where(kind < 3, token, 1.0)

    for k in range(others):
        parts = [part_refs[at][...] for at in spec[k]]
        x = parts[0]
        if len(parts) == 2:
            x = jnp.where((z == 1) | (z == 2), parts[0], parts[1])
        k_s[k] = dot(x, wk_ref[...]).astype(BF16)
        v_s[k] = dot(x, wv_ref[...]).astype(BF16)

    slope = jnp.zeros((1, LANES), F32)
    lane1 = lax.broadcasted_iota(jnp.int32, (1, LANES), 1)
    for h in range(H):
        slope = jnp.where(lane1 // FEATS == h, slopes_ref[h] * LOG2E, slope)
    kind1 = lane1 - (lane1 // FEATS) * FEATS
    own_off = lane_value(msg_ref[MSG - 1 : MSG, :], s)
    feats = []
    for k in range(others):
        gap = jnp.abs(lane_value(msg_refs[k][MSG - 1 : MSG, :], s) - own_off)
        sign = jnp.where((z ^ (k + 1)) < z, 1.0, -1.0)
        value = jnp.where(kind1 < 3, -sign * slope, slope * (sign * token - gap))
        p1 = value.astype(BF16).astype(F32)
        p2 = (value - p1).astype(BF16).astype(F32)
        p3 = value - p1 - p2
        part = jnp.where(kind1 % 3 == 0, p1, jnp.where(kind1 % 3 == 1, p2, p3))
        feats.append(part.astype(BF16))
    ones = jnp.ones((block_len, LANES), BF16)
    zero = jnp.zeros((), BF16)
    for pair in range(H // 2):
        low, high = pair * LANES, (pair + 1) * LANES
        q = q_ref[:, low:high]
        own_k = own_ref[:, low:high]
        keys = [
            jnp.concatenate([k_s[k, :, low:high], feats[k]], axis=1) for k in range(others)
        ]
        own_v = jnp.concatenate([own_ref[:, D + low : D + high], ones], axis=1)
        values = [
            jnp.concatenate([v_s[k, :, low:high], ones], axis=1) for k in range(others)
        ]
        outs = []
        for e in range(2):
            h = 2 * pair + e
            mine = (lane < HD) if e == 0 else (lane >= HD)
            qh = jnp.where(mine, q, zero)
            qfeat = jnp.where(head_of == h, qvalue, 0.0).astype(BF16)
            qf = jnp.concatenate([qh, qfeat], axis=1)
            scores = [dot_nt(qh, own_k) - apart * slopes_ref[h]] + [dot_nt(qf, key) for key in keys]
            top = scores[0]
            for sc in scores[1:]:
                top = jnp.maximum(top, sc)
            top = jnp.max(top, axis=1, keepdims=True)
            total = dot(jnp.exp2(scores[0] - top).astype(BF16), own_v)
            for sc, value in zip(scores[1:], values):
                total += dot(jnp.exp2(sc - top).astype(BF16), value)
            outs.append(total[:, :LANES] / total[:, LANES:])
        out_ref[:, low:high] = (
            jnp.where(lane < HD, outs[0], outs[1]) + vecs_ref[2:3, low:high]
        ).astype(BF16)


def dense_kernel(seqs, x_ref, *refs):
    att_refs, (wo_ref, vecs_ref, wg_ref, wu_ref, wd_ref, out_ref, fo_s, low_s, acc_s) = (
        refs[:seqs], refs[seqs:],
    )
    step = pl.program_id(0)

    @pl.when(step == 0)
    def _():
        for s, att_ref in enumerate(att_refs):
            rows = slice(s * att_ref.shape[0], (s + 1) * att_ref.shape[0])
            first_sum = x_ref[rows, :].astype(F32) + (
                dot(att_ref[...], wo_ref[...]) + vecs_ref[3:4, :]
            )
            normed, _scale = norm_rows(first_sum)
            first_out = normed * vecs_ref[4:5, :] + vecs_ref[5:6, :]
            fo_s[rows, :] = first_out
            low_s[rows, :] = first_out.astype(BF16)
        acc_s[...] = jnp.zeros_like(acc_s)

    low = low_s[...]
    gate = dot(low, wg_ref[...])
    up = dot(low, wu_ref[...])
    mixed = (gate * normal_cdf(gate) * up).astype(BF16)
    acc_s[...] += dot(mixed, wd_ref[...])

    @pl.when(step == pl.num_programs(0) - 1)
    def _():
        normed, _scale = norm_rows(fo_s[...] + (acc_s[...] + vecs_ref[6:7, :]))
        out_ref[...] = (normed * vecs_ref[7:8, :] + vecs_ref[8:9, :]).astype(BF16)


def put_small(ref, small):
    high, rest = split2(small)
    ref[0:SMALL, :] = high
    ref[SMALL : 2 * SMALL, :] = rest


def get_small(ref):
    return ref[0:SMALL, :].astype(F32) + ref[SMALL : 2 * SMALL, :].astype(F32)


def add_split_kernel(count, *refs):
    for at in range(count):
        keep, got = refs[2 * at : 2 * at + 2]
        half = keep.shape[0] // 2
        for part in range(2):
            rows = pl.ds(part * half, half)
            total = keep[rows, :].astype(F32) + got[rows, :].astype(F32)
            refs[2 * count + 2 * at + part][...] = total.astype(BF16)


def add_split(arrays, name, micros=0.1):
    rows, width = arrays[0].shape
    count = len(arrays) // 2
    cut = max(1, rows * width // (512 * 1024))
    while width % (cut * LANES):
        cut -= 1
    return pl.pallas_call(
        functools.partial(add_split_kernel, count),
        name=name,
        out_shape=[jax.ShapeDtypeStruct((rows // 2, width), BF16)] * (2 * count),
        grid=(cut,),
        in_specs=[pl.BlockSpec((rows, width // cut), lambda i: (0, i))] * (2 * count),
        out_specs=[pl.BlockSpec((rows // 2, width // cut), lambda i: (0, i))] * (2 * count),
        compiler_params=params(),
        cost_estimate=cost(micros),
    )(*arrays)


def add_small_kernel(keep, small, got, keep_out, send_out, small_out):
    half = keep.shape[0] // 2
    total = keep[...].astype(F32) + got[2 * SMALL :, :].astype(F32)
    keep_out[...] = total[:half].astype(BF16)
    send_out[2 * SMALL :, :] = total[half:].astype(BF16)
    both = small[...] + get_small(got)
    small_out[...] = both
    put_small(send_out, both)


def add_small(keep, small, got, name):
    rows = keep.shape[0] // 2
    full = lambda shape: pl.BlockSpec(shape, lambda i: (0, 0))
    return pl.pallas_call(
        add_small_kernel,
        name=name,
        grid=(1,),
        out_shape=[
            jax.ShapeDtypeStruct((rows, D), BF16), jax.ShapeDtypeStruct((2 * SMALL + rows, D), BF16),
            jax.ShapeDtypeStruct((SMALL, D), F32),
        ],
        in_specs=[full(keep.shape), full(small.shape), full(got.shape)],
        out_specs=[full((rows, D)), full((2 * SMALL + rows, D)), full((SMALL, D))],
        compiler_params=params(),
        cost_estimate=cost(0.1),
    )(keep, small, got)


def add_join_kernel(segments, left, left_got, right, right_got, keep_out, send_out):
    width = left.shape[1]
    for at, (keep, got) in enumerate(((left, left_got), (right, right_got))):
        total = keep[...].astype(F32) + got[...].astype(F32)
        first, second = halves(total, segments)
        keep_out[:, at * width : (at + 1) * width] = first.astype(BF16)
        send_out[:, at * width : (at + 1) * width] = second.astype(BF16)


def add_join(arrays, segments, name):
    rows, width = arrays[0].shape
    full = lambda shape: pl.BlockSpec(shape, lambda i: (0, 0))
    return pl.pallas_call(
        functools.partial(add_join_kernel, segments),
        name=name,
        grid=(1,),
        out_shape=[jax.ShapeDtypeStruct((rows // 2, 2 * width), BF16)] * 2,
        in_specs=[full((rows, width))] * 4,
        out_specs=[full((rows // 2, 2 * width))] * 2,
        compiler_params=params(),
        cost_estimate=cost(0.1),
    )(*arrays)


def add_columns_kernel(keep, got, *outs):
    rows, half = keep.shape[0] // 2, keep.shape[1] // 2
    for side in range(2):
        for part in range(2):
            at = (pl.ds(part * rows, rows), pl.ds(side * half, half))
            outs[2 * side + part][...] = (keep[at].astype(F32) + got[at].astype(F32)).astype(BF16)


def add_columns(keep, got, name):
    rows, width = keep.shape
    full = lambda shape: pl.BlockSpec(shape, lambda i: (0, 0))
    return pl.pallas_call(
        add_columns_kernel,
        name=name,
        grid=(1,),
        out_shape=[jax.ShapeDtypeStruct((rows // 2, width // 2), BF16)] * 4,
        in_specs=[full((rows, width))] * 2,
        out_specs=[full((rows // 2, width // 2))] * 4,
        compiler_params=params(),
        cost_estimate=cost(0.1),
    )(keep, got)


def finish_kernel(
    rows_f, rows_d, sc_ref, gu_k, gu_r, down_k, down_r, value_k, value_r, small_ref, vecs_ref, qm_ref,
    gateup_ref, down_ref, out_ref, qkv_ref, *vector_refs,
):
    gateup_ref[...] = gu_k[...].astype(F32) + gu_r[...].astype(F32)
    total = down_k[...].astype(F32) + down_r[...].astype(F32)
    down_ref[...] = total[:rows_f]
    out_ref[...] = total[rows_f:]
    small = small_ref[...] + get_small(value_r)
    row = lax.broadcasted_iota(jnp.int32, (D, LANES), 0)
    lane = lax.broadcasted_iota(jnp.int32, (D, LANES), 1)
    pick = jnp.where((row == lane + sc_ref[0] * rows_d) & (lane < rows_d), 1.0, 0.0).astype(BF16)
    both = jnp.concatenate([small, jnp.broadcast_to(vecs_ref[1:2, :], (8, D))], axis=0)
    p1 = both.astype(BF16)
    p2 = (both - p1.astype(F32)).astype(BF16)
    p3 = (both - p1.astype(F32) - p2.astype(F32)).astype(BF16)
    mine = dot(p1, pick) + dot(p2, pick) + dot(p3, pick)
    for ref, at in zip(vector_refs, (6, 20, 7, 5, 3, 4, 2, 0, 1)):
        ref[...] = mine[at : at + 1, 0:rows_d].reshape(rows_d)
    columns = mine.T
    emb = jnp.broadcast_to(columns[0:rows_d, SMALL : SMALL + 1], (rows_d, D))
    qkv_ref[:, 0:D] = emb * small[20:21, :]
    heads = columns[:, 8 : 8 + 16]
    key = jnp.concatenate(
        [
            jnp.broadcast_to(heads[0:rows_d, h : h + 1], (rows_d, HD)) for h in range(H)
        ],
        axis=1,
    )
    qkv_ref[:, D : 2 * D] = key * (qm_ref[0:1, :] * (HD**-0.5))
    qkv_ref[:, 2 * D :] = value_k[...].astype(F32) + value_r[2 * SMALL :, :].astype(F32)


def finish(scalars, gu_k, gu_r, down_k, down_r, value_k, value_r, small, vecs, qm, rows_f, rows_d):
    shape = jax.ShapeDtypeStruct
    full = lambda shape: pl.BlockSpec(shape, lambda i: (0,) * len(shape))
    outs = [(rows_d, 2 * FF), (rows_f, D), (rows_d, D), (rows_d, 3 * D)] + [(rows_d,)] * 9
    arrays = (gu_k, gu_r, down_k, down_r, value_k, value_r, small, vecs, qm)
    return pl.pallas_call(
        functools.partial(finish_kernel, rows_f, rows_d),
        name="finish",
        grid=(1,),
        out_shape=[shape(o, F32) for o in outs],
        in_specs=[smem()] + [full(x.shape) for x in arrays],
        out_specs=[full(o) for o in outs],
        compiler_params=params(),
        cost_estimate=cost(1),
    )(scalars, *arrays)


def halves(total, segments):
    first, second, at = [], [], 0
    for rows in segments:
        first.append(total[at : at + rows // 2])
        second.append(total[at + rows // 2 : at + rows])
        at += rows
    return jnp.concatenate(first, axis=0), jnp.concatenate(second, axis=0)


def bit_orders(batch, blocks):
    n = int(math.log2(batch * blocks))
    seq_bits = int(math.log2(blocks))
    rest = list(range(seq_bits, n - 3)) + list(range(seq_bits))
    top = [n - 3, n - 2, n - 1]
    return [*top, *rest], [top[0], top[2], top[1], *rest], rest


def places(order, rows):
    n = len(order)
    place = np.arange(2**n)
    rel = np.zeros(2**n, np.int32)
    for k, bit in enumerate(order):
        rel |= ((place >> (n - 1 - k)) & 1).astype(np.int32) << bit
    out = np.zeros((8, 2**n * rows), np.int32)
    out[0] = np.repeat(rel, rows)
    out[1] = np.tile(np.arange(rows), 2**n)
    return out


def swap_pair(i):
    return (i & 1) * 2 + lax.shift_right_logical(i, 1)


def smem():
    return pl.BlockSpec(memory_space=pltpu.SMEM)


def masked_rows(
    batch, blocks, scalars, mask_flags, msg1, recv1, num, den, grad, out_weight, vecs,
    gate_up_weight, down_weight,
):
    seqs, block_len = mask_flags.shape
    tokens = seqs * block_len
    shards = batch * blocks
    others = blocks - 1
    n = FF // CHUNK
    half = D // 2
    order_x, order_y, order_rest = bit_orders(batch, blocks)
    top_bit = len(order_x) - 3
    vmem, hbm = pl.BlockSpec(memory_space=pltpu.VMEM), pl.BlockSpec(memory_space=pl.ANY)
    bf_full = jax.ShapeDtypeStruct((tokens, D), BF16)
    wide = jax.ShapeDtypeStruct((half, FF), BF16)
    tall = jax.ShapeDtypeStruct((FF // 2 + half, D), BF16)
    chunks = lambda rows, width: pltpu.VMEM((n, rows, width), BF16)
    grads = [wide] * 4 + [tall] * 2
    square_s = pltpu.VMEM((half, D), BF16)
    weights_s = [
        chunks(D, CHUNK), chunks(D, CHUNK), chunks(CHUNK, D), chunks(D, CHUNK), chunks(D, CHUNK),
        chunks(CHUNK // 2, D), chunks(CHUNK // 2, D),
    ]
    tile_s = [
        pltpu.VMEM((D, CAP), BF16), pltpu.VMEM((D, CAP), BF16), chunks(CAP, CHUNK),
        chunks(CAP, CHUNK), chunks(CAP, CHUNK), pltpu.VMEM((CAP, D), F32), pltpu.VMEM((CAP, D), F32),
    ]
    held = [
        places(order_x, D // shards), places(order_y, D // shards),
        places(order_rest, FF // shards),
    ]
    small = jax.ShapeDtypeStruct((8, D), F32)
    packed = jax.ShapeDtypeStruct((block_len, LANES), F32)
    *sums, att, invden, dheads, small_sums = pl.pallas_call(
        functools.partial(
            masked_kernel, others, seqs, block_len, D // shards, FF // shards, shards // 8, top_bit
        ),
        name="masked_rows",
        out_shape=grads + [bf_full, packed, bf_full, small],
        in_specs=[smem()] + [vmem] * (10 + len(recv1)) + [hbm] * 2,
        out_specs=[hbm] * 6 + [vmem] * 4,
        scratch_shapes=weights_s + [square_s, square_s] + tile_s
        + [pltpu.SemaphoreType.DMA((3, n)), pltpu.SemaphoreType.DMA((10, n))],
        compiler_params=params(62),
        cost_estimate=cost(60),
    )(
        scalars, mask_flags, msg1, *recv1, num, den, grad, out_weight, vecs, *held, gate_up_weight,
        down_weight,
    )
    *sums, dheads, small_sums = pl.pallas_call(
        functools.partial(
            more_tiles_kernel, seqs, block_len, D // shards, FF // shards, shards // 8, top_bit
        ),
        name="more_masked_rows",
        out_shape=grads + [bf_full, small],
        in_specs=[smem()] + [hbm] * 18,
        out_specs=[hbm] * 8,
        input_output_aliases={11 + k: k for k in range(8)},
        scratch_shapes=[
            pltpu.VMEM(mask_flags.shape, jnp.int32), pltpu.VMEM((tokens, D), BF16),
            pltpu.VMEM((tokens, D), BF16), pltpu.VMEM((D, D), BF16), pltpu.VMEM((16, D), F32),
        ]
        + [pltpu.VMEM(h.shape, jnp.int32) for h in held]
        + weights_s
        + [square_s, square_s, pltpu.VMEM((tokens, D), BF16), pltpu.VMEM((8, D), F32)]
        + tile_s
        + [pltpu.SemaphoreType.DMA],
        compiler_params=params(62),
        cost_estimate=cost(1),
    )(
        scalars, mask_flags, att, grad, out_weight, vecs, *held, gate_up_weight, down_weight, *sums,
        dheads, small_sums,
    )
    return (*sums, att, invden, dheads, small_sums)


def on_device(
    hidden_states, mask_flags, block_offsets, alibi_slopes, mask_embedding, qkv_weight, query_bias,
    value_bias, out_weight, out_bias, first_gain, first_shift, gate_up_weight, down_weight,
    down_bias, second_gain, second_shift, output_grad,
):
    seqs, block_len = mask_flags.shape
    tokens = seqs * block_len
    batch, blocks = lax.axis_size("batch"), lax.axis_size("seq")
    shards = batch * blocks
    z = lax.axis_index("seq")
    me = lax.axis_index("batch") * blocks + z
    order_x, order_y, order_rest = bit_orders(batch, blocks)
    seq_bits = int(math.log2(blocks))
    place_x = places(order_x, D // shards)
    top_bit = len(order_x) - 3
    n = FF // CHUNK
    half = D // 2
    square = jax.ShapeDtypeStruct((half, D), BF16)
    others = blocks - 1
    vmem = pl.BlockSpec(memory_space=pltpu.VMEM)
    packed = jax.ShapeDtypeStruct((block_len, LANES), F32)
    bf_full = jax.ShapeDtypeStruct((tokens, D), BF16)
    last = [()]

    def after(*values):
        tied = lax.optimization_barrier((values, last[0]))[0]
        return tied if len(values) > 1 else tied[0]

    def done(value):
        last[0] = value

    def along(value, axis, pairs):
        return lax.ppermute(value, axis, pairs)

    def flip(value, bit):
        if bit >= seq_bits:
            axis, size, mask = "batch", batch, 1 << (bit - seq_bits)
        else:
            axis, size, mask = "seq", blocks, 1 << bit
        return along(value, axis, [(i, i ^ mask) for i in range(size)])

    fixed = lambda shape: pl.BlockSpec(shape, lambda i: (0,) * len(shape))
    x, vecs, flagx, scalars = pl.pallas_call(
        functools.partial(inputs_kernel, seqs, block_len, blocks),
        name="inputs",
        grid=(1,),
        out_shape=(
            bf_full, jax.ShapeDtypeStruct((16, D), F32), jax.ShapeDtypeStruct((tokens, LANES), F32),
            jax.ShapeDtypeStruct((8,), jnp.int32),
        ),
        in_specs=[smem(), smem(), fixed((tokens, D)), fixed((seqs, block_len))] + [fixed((D,))] * 9,
        out_specs=[
            fixed((tokens, D)), fixed((16, D)), fixed((tokens, LANES)), smem(),
        ],
        compiler_params=params(),
        cost_estimate=cost(1),
    )(
        alibi_slopes, block_offsets.reshape(1, seqs), hidden_states.reshape(tokens, D), mask_flags,
        mask_embedding, value_bias, out_bias, first_gain, first_shift, down_bias, second_gain,
        second_shift, query_bias,
    )

    near = [(i, i ^ 1) for i in range(blocks)]
    centre, outward = [(0, 0), (1, 2), (2, 1), (3, 3)], [(1, 0), (2, 3)]
    hops = blocks == 4

    def held(*values):
        values = after(*values)
        done(values)
        return values

    v, wx, num, den, msg1, g, qm = pl.pallas_call(
        functools.partial(prep_kernel, seqs, block_len),
        name="masked_prep",
        out_shape=(
            bf_full, packed, bf_full, packed, jax.ShapeDtypeStruct((MSG, D), F32),
            jax.ShapeDtypeStruct((D, LANES), BF16), jax.ShapeDtypeStruct((8, D), F32),
        ),
        in_specs=[smem(), smem()] + [vmem] * 3,
        out_specs=[vmem] * 7,
        compiler_params=params(),
        cost_estimate=cost(10),
    )(alibi_slopes, scalars, x, qkv_weight, vecs)
    done(msg1)
    recv1 = [along(msg1, "seq", [(i, i ^ k) for i in range(blocks)]) for k in range(1, blocks)]

    q_own = project(after(x), qkv_weight, vecs, 0, 1, LOG2E * HD**-0.5)
    done(q_own)
    recv1 = list(held(*recv1, msg1))[:-1]
    x_late = after(x)
    if hops:
        round1 = along(x_late, "seq", near), along(x_late, "seq", centre)
    else:
        round1 = tuple(
            along(x_late, "seq", [(i, i ^ k) for i in range(blocks)]) for k in range(1, blocks)
        )

    gate_s, gate_k, up_s, up_k, down_s, down_k, att_m, invden, dheads, small_a = masked_rows(
        batch, blocks, scalars, mask_flags, msg1, recv1, num, den,
        after(output_grad.reshape(tokens, D)), out_weight, vecs, gate_up_weight, down_weight,
    )
    done(small_a)
    round1 = held(*round1)
    if hops:
        round2 = along(round1[1], "seq", outward), along(round1[0], "seq", centre[1:3])
    up_r, gate_r, down_r = (
        flip(up_s, order_y[0]), flip(gate_s, order_x[0]), flip(down_s, order_x[0])
    )

    uv, ud, msg2 = pl.pallas_call(
        functools.partial(inner_kernel, seqs, block_len),
        name="masked_inner",
        out_shape=(bf_full, packed, jax.ShapeDtypeStruct((MSG, D), F32)),
        in_specs=[smem()] + [vmem] * 4,
        out_specs=[vmem] * 3,
        compiler_params=params(),
        cost_estimate=cost(60),
    )(alibi_slopes, after(dheads), att_m, invden, vecs)
    done(msg2)

    left_k, left_s, right_k, right_s = add_columns(*after(down_k, down_r), "add_core_down")
    done(left_k)
    up_k, up_s, gate_k, gate_s = add_split(after(up_k, up_r, gate_k, gate_r), "add_core_gate_up")
    done(up_k)
    up_r, gate_r = flip(up_s, order_y[1]), flip(gate_s, order_x[1])
    if hops:
        round2 = held(*round2)
    msg2_now = after(msg2)
    recv2 = [along(msg2_now, "seq", [(i, i ^ k) for i in range(blocks)]) for k in range(1, blocks)]
    kv_own = project(after(x), qkv_weight, vecs, 1, 2)
    done(kv_own)
    recv2 = list(held(*recv2, msg2))[:-1]
    if hops:
        far = along(after(round2[1]), "seq", outward)

    input_grad, value_s, value_k, small = pl.pallas_call(
        functools.partial(value_kernel, others, seqs, block_len, D // shards),
        name="value_grads",
        out_shape=(
            bf_full, jax.ShapeDtypeStruct((2 * SMALL + half, D), BF16),
            jax.ShapeDtypeStruct((half, D), BF16), jax.ShapeDtypeStruct((SMALL, D), F32),
        ),
        in_specs=[smem()] + [vmem] * (13 + len(recv1) + len(recv2)),
        out_specs=[vmem] * 4,
        scratch_shapes=[pltpu.VMEM((tokens, D), BF16), pltpu.VMEM((tokens, LANES), F32)],
        compiler_params=params(),
        cost_estimate=cost(60),
    )(
        scalars, flagx, msg1, msg2, *recv1, *recv2, uv, ud, wx, v, after(x), qkv_weight, g, vecs,
        place_x, small_a,
    )
    done(small)
    value_r = flip(after(value_s), order_x[0])

    up_k, up_s, gate_k, gate_s = add_split(after(up_k, up_r, gate_k, gate_r), "add_xy_gate_up", 4)
    done(up_k)
    up_r, gate_r = flip(up_s, order_y[2]), flip(gate_s, order_x[2])
    value_k, value_s, small = add_small(*after(value_k, small, value_r), "add_core_value")
    done(small)
    if hops:
        far, _ = held(far, small)
    value_r = flip(after(value_s), order_x[1])
    if hops:
        groups = [
            [round1[0]], [round2[1], round2[0]], [round1[1], far],
        ]
    else:
        groups = [[part] for part in round1]

    def attend(s):
        block = lambda at, width=D: pl.BlockSpec((block_len, width), lambda i: (at, 0))
        spec, parts = [], []
        for group in groups:
            spec.append(list(range(len(parts), len(parts) + len(group))))
            parts += group
        out = pl.pallas_call(
            functools.partial(attention_kernel, s, spec),
            name="dense_attention",
            out_shape=jax.ShapeDtypeStruct((block_len, D), BF16),
            grid=(1,),
            in_specs=[smem(), smem(), block(s), block(s, 2 * D)]
            + [pl.BlockSpec((D, D), lambda i: (0, 1)), pl.BlockSpec((D, D), lambda i: (0, 2))]
            + [block(s)] * len(parts)
            + [pl.BlockSpec((MSG, D), lambda i: (0, 0))] * (others + 2),
            out_specs=block(0),
            scratch_shapes=[pltpu.VMEM((others, block_len, D), BF16)] * 2,
            compiler_params=params(),
            cost_estimate=cost(60),
        )(
            alibi_slopes, scalars, after(q_own), kv_own, qkv_weight, qkv_weight, *parts, *recv1, msg1,
            vecs,
        )
        done(out)
        return out

    def gate_up_step(bit):
        nonlocal gu_k, gu_r
        total = sum(p.astype(F32) for p in after(gu_k, gu_r)).astype(BF16)
        gu_k, gu_s = halves(total, [total.shape[0]])
        done(gu_k)
        gu_r = flip(gu_s, bit)

    def value_step(bit, name):
        nonlocal value_k, value_r, small
        value_k, value_s, small = add_small(*after(value_k, small, value_r), name)
        done(small)
        value_r = flip(value_s, bit)

    def down_step(bit):
        nonlocal down_k, down_r
        down_k, down_r = after(down_k, down_r)
        segments[:] = [rows // 2 for rows in segments]
        total = (down_k.astype(F32) + down_r.astype(F32)).astype(BF16)
        down_k, down_s = halves(total, segments)
        done(down_k)
        down_r = flip(down_s, bit)

    attended = [attend(0)]
    left_s, right_s = after(left_s, right_s)
    left_r, right_r = flip(left_s, order_x[1]), flip(right_s, order_y[1])
    gu_k, gu_s = add_join(after(gate_k, gate_r, up_k, up_r), [up_k.shape[0]], "add_gate_up")
    done(gu_k)
    gu_r = flip(gu_s, order_rest[0])
    value_step(order_x[2], "add_xy_value")
    attended.append(attend(1))
    left_k, left_s, right_k, right_s = add_split(
        after(left_k, left_r, right_k, right_r), "add_xy_down"
    )
    done(left_k)
    left_r, right_r = flip(left_s, order_x[2]), flip(right_s, order_y[2])
    value_step(order_rest[0], "add_value")
    attended += [attend(s) for s in range(2, seqs)]
    gate_up_step(order_rest[1])
    segments = [CHUNK // 2, half // n]
    down_k, down_s = add_join(after(left_k, left_r, right_k, right_r), segments, "add_down")
    done(down_k)
    down_r = flip(down_s, order_rest[0])
    value_step(order_rest[1], "add_value")

    output = pl.pallas_call(
        functools.partial(dense_kernel, seqs),
        name="dense_ffn",
        out_shape=bf_full,
        grid=(n,),
        in_specs=[vmem] * (3 + seqs)
        + [
            pl.BlockSpec((D, CHUNK), lambda i: (0, i)),
            pl.BlockSpec((D, CHUNK), lambda i: (0, n + i)),
            pl.BlockSpec((CHUNK, D), lambda i: (i, 0)),
        ],
        out_specs=vmem,
        scratch_shapes=[
            pltpu.VMEM((tokens, D), F32), pltpu.VMEM((tokens, D), BF16), pltpu.VMEM((tokens, D), F32),
        ],
        compiler_params=params(),
        cost_estimate=cost(60),
    )(x, *after(*attended), out_weight, vecs, gate_up_weight, gate_up_weight, down_weight)
    done(output)

    down_step(order_rest[1])
    for bit in order_rest[2:]:
        gate_up_step(bit)
        down_step(bit)
        value_step(bit, "add_value")
    (
        grad_gateup, grad_down, grad_outw, grad_qkv, grad_embed, grad_qbias, grad_vbias, grad_outb,
        grad_gain1, grad_shift1, grad_downb, grad_gain2, grad_shift2,
    ) = finish(
        scalars, *after(gu_k, gu_r, down_k, down_r, value_k, value_r, small), vecs, qm,
        FF // shards, D // shards,
    )

    shape = (seqs, block_len, D)
    return (
        output.reshape(shape), input_grad.reshape(shape), grad_embed, grad_qkv, grad_qbias,
        grad_vbias, grad_outw, grad_outb, grad_gain1, grad_shift1, grad_gateup, grad_down,
        grad_downb, grad_gain2, grad_shift2,
    )


def solution(mesh):
    data, pairs = P("batch", "seq", None), P("batch", "seq")
    in_specs = (data, pairs, pairs) + (P(),) * 14 + (data,)
    vector, matrix = P(("batch", "seq")), P(("batch", "seq"), None)
    out_specs = (
        data, data, vector, matrix, vector, vector, matrix, vector, vector, vector, matrix, matrix,
        vector, vector, vector,
    )
    return jax.shard_map(
        on_device, mesh=mesh, in_specs=in_specs, out_specs=out_specs, check_vma=False
    )
```

```python
import functools
import math

import jax
import jax.numpy as jnp
import numpy as np
from jax import lax
from jax.experimental import pallas as pl
from jax.experimental.pallas import tpu as pltpu
from jax.sharding import PartitionSpec as P

D = 768
FF = 3072
H = 12
HD = 64
CAP = 192
CHUNK = 768
LANES = 128
MSG = 16
SMALL = 24

F32 = jnp.float32
BF16 = jnp.bfloat16


def params(limit=62):
    return pltpu.CompilerParams(vmem_limit_bytes=limit * 1024 * 1024)


def cost(micros):
    return pl.CostEstimate(flops=int(micros * 1.15e9), bytes_accessed=1024, transcendentals=0)


def dot(a, b):
    return lax.dot_general(a, b, (((1,), (0,)), ((), ())), preferred_element_type=F32)


def dot_nt(a, b):
    return lax.dot_general(a, b, (((1,), (1,)), ((), ())), preferred_element_type=F32)


def dot_tn(a, b):
    return lax.dot_general(a, b, (((0,), (0,)), ((), ())), preferred_element_type=F32)


def split2(v):
    high = v.astype(BF16)
    return high, (v - high.astype(F32)).astype(BF16)


def dot_wide(v, b):
    high, rest = split2(v)
    return dot(high, b) + dot(rest, b)


def expand_one():
    row = lax.broadcasted_iota(jnp.int32, (LANES, D), 0)
    lane = lax.broadcasted_iota(jnp.int32, (LANES, D), 1)
    return jnp.where(lax.shift_right_logical(lane, 6) == row, 1.0, 0.0).astype(BF16)


def expand_seq(s):
    row = lax.broadcasted_iota(jnp.int32, (LANES, D), 0)
    lane = lax.broadcasted_iota(jnp.int32, (LANES, D), 1)
    return jnp.where(lax.shift_right_logical(lane, 6) + 16 * s == row, 1.0, 0.0).astype(BF16)


def reduce_seq(s):
    row = lax.broadcasted_iota(jnp.int32, (D, LANES), 0)
    lane = lax.broadcasted_iota(jnp.int32, (D, LANES), 1)
    return jnp.where(lax.shift_right_logical(row, 6) + 16 * s == lane, 1.0, 0.0).astype(BF16)


def reduce_one():
    row = lax.broadcasted_iota(jnp.int32, (D, LANES), 0)
    lane = lax.broadcasted_iota(jnp.int32, (D, LANES), 1)
    return jnp.where(lax.shift_right_logical(row, 6) == lane, 1.0, 0.0).astype(BF16)


def permuting(place_row, me, rows):
    n = place_row.shape[1]
    distance = place_row[0:1, :]
    source = (distance ^ me) * rows + place_row[1:2, :]
    row = lax.broadcasted_iota(jnp.int32, (n, n), 0)
    return jnp.where(row == source, 1.0, 0.0).astype(BF16)


def decay(slope_lane, block_len):
    t = lax.broadcasted_iota(jnp.int32, (block_len, D), 0).astype(F32)
    return jnp.exp(-slope_lane * t), jnp.exp(-slope_lane * (block_len - 1.0 - t))


def head_decay(slope, block_len):
    row = lax.broadcasted_iota(jnp.int32, (block_len, block_len), 0)
    lane = lax.broadcasted_iota(jnp.int32, (block_len, block_len), 1)
    return jnp.exp(-slope * jnp.abs(row - lane).astype(F32)).astype(BF16)


def local_decay_sums(slopes_ref, wide, packed, wide_out, packed_out, block_len, seqs):
    lane = lax.broadcasted_iota(jnp.int32, (block_len, LANES), 1)
    total = jnp.zeros((block_len, LANES), F32)
    for pair in range(H // 2):
        low, high = pair * LANES, (pair + 1) * LANES
        right = jnp.concatenate([wide[s][:, low:high] for s in range(seqs)] + [packed], axis=1)
        even = dot(head_decay(slopes_ref[2 * pair], block_len), right)
        odd = dot(head_decay(slopes_ref[2 * pair + 1], block_len), right)
        for s in range(seqs):
            rows = slice(s * block_len, (s + 1) * block_len)
            at = slice(s * LANES, (s + 1) * LANES)
            wide_out[rows, low:high] = jnp.where(lane < HD, even[:, at], odd[:, at]).astype(
                wide_out.dtype
            )
        at = slice(seqs * LANES, (seqs + 1) * LANES)
        total = jnp.where((lane & 15) == 2 * pair, even[:, at], total)
        total = jnp.where((lane & 15) == 2 * pair + 1, odd[:, at], total)
    packed_out[...] = total


def lane_value(row, index):
    lane = lax.broadcasted_iota(jnp.int32, row.shape, 1)
    return jnp.sum(jnp.where(lane == index, row, 0.0), axis=1, keepdims=True)


GELU = (
    0.7978849414614602, 0.03633308456815623, -3.259496805730905e-05, -5.530619733817487e-05,
    3.9647451634764645e-06, -1.322634044387524e-07, 1.756172658552303e-09,
)


def normal_cdf(v):
    square = v * v
    poly = GELU[6]
    for c in GELU[5::-1]:
        poly = poly * square + c
    return 0.5 + 0.5 * jnp.tanh(v * poly)


def norm_rows(v):
    centred = v - jnp.mean(v, axis=1, keepdims=True)
    scale = lax.rsqrt(jnp.mean(centred * centred, axis=1, keepdims=True) + 1e-05)
    return centred * scale, scale


def norm_back(upstream, normed, scale, gain):
    scaled = upstream * gain
    return scale * (
        scaled
        - jnp.mean(scaled, axis=1, keepdims=True)
        - normed * jnp.mean(scaled * normed, axis=1, keepdims=True)
    )


def colsum(v):
    return jnp.sum(v, axis=0, keepdims=True)


def inputs_kernel(seqs, block_len, blocks, slopes_ref, offs_ref, hidden_ref, flags_ref, *refs):
    vec_refs, (x_ref, vecs_ref, flagx_ref, sc_ref) = refs[:-4], refs[-4:]
    emb = vec_refs[0][...].astype(F32).reshape(1, D)
    lane = lax.broadcasted_iota(jnp.int32, (1, D), 1)
    slope = jnp.zeros((1, D), F32)
    for h in range(H):
        slope = jnp.where(lax.shift_right_logical(lane, 6) == h, slopes_ref[h], slope)
    vecs_ref[...] = jnp.zeros_like(vecs_ref)
    vecs_ref[0:1, :] = slope
    for k, r in enumerate(vec_refs):
        vecs_ref[k + 1 : k + 2, :] = r[...].astype(F32).reshape(1, D)
    sc_ref[0] = lax.axis_index("batch") * blocks + lax.axis_index("seq")
    sc_ref[1] = lax.axis_index("seq")
    sc_ref[2] = jnp.maximum(1, (jnp.sum(flags_ref[...]) + CAP - 1) // CAP)
    flags = flags_ref[...].astype(F32)
    for s in range(seqs):
        rows = slice(s * block_len, (s + 1) * block_len)
        column = jnp.broadcast_to(flags[s : s + 1, :], (LANES, block_len)).T
        flagx_ref[rows, :] = column
        mask = jnp.broadcast_to(column[:, 0:1], (block_len, D)) > 0.5
        x_ref[rows, :] = jnp.where(mask, emb, hidden_ref[rows, :].astype(F32)).astype(BF16)
        sc_ref[4 + s] = offs_ref[0, s]


def project_kernel(scale, x_ref, w_ref, bias_ref, out_ref):
    out = dot(x_ref[...], w_ref[...])
    if scale is not None:
        out = (out + bias_ref[9:10, :]) * scale
    out_ref[...] = out.astype(BF16)


def project(x, weight, vecs, first, count, scale=None):
    return pl.pallas_call(
        functools.partial(project_kernel, scale),
        name="project",
        out_shape=jax.ShapeDtypeStruct((x.shape[0], count * D), BF16),
        grid=(count,),
        in_specs=[
            pl.BlockSpec(x.shape, lambda i: (0, 0)),
            pl.BlockSpec((D, D), lambda i: (0, first + i)), pl.BlockSpec((16, D), lambda i: (0, 0)),
        ],
        out_specs=pl.BlockSpec((x.shape[0], D), lambda i: (0, i)),
        compiler_params=params(),
        cost_estimate=cost(0.1),
    )(x, weight, vecs)


def prep_kernel(
    seqs, block_len, slopes_ref, sc_ref, x_ref, wqkv_ref, vecs_ref,
    v_ref, wx_ref, num_ref, den_ref, msg_ref, g_ref, qm_ref,
):
    slope_lane = vecs_ref[0:1, :]
    emb8 = jnp.broadcast_to(vecs_ref[1:2, :], (8, D)).astype(BF16)
    qm = (dot(emb8, wqkv_ref[:, 0:D]) + vecs_ref[9:10, :]).astype(BF16).astype(F32)
    qm_ref[...] = qm
    scaled = wqkv_ref[:, D : 2 * D].astype(F32) * (qm[0:1, :] * (HD**-0.5))
    g = dot_wide(scaled, reduce_one())
    g_high, g_rest = split2(g)
    g_ref[...] = g_high
    expand = expand_one()
    dec_f, dec_r = decay(slope_lane, block_len)
    weighted = []
    packed = jnp.zeros((block_len, LANES), F32)
    lane = lax.broadcasted_iota(jnp.int32, (block_len, LANES), 1)
    msg_ref[...] = jnp.zeros_like(msg_ref)
    lane8 = lax.broadcasted_iota(jnp.int32, (1, D), 1)
    offs_row = jnp.zeros((1, D), F32)
    for s in range(seqs):
        rows = slice(s * block_len, (s + 1) * block_len)
        x = x_ref[rows, :]
        a = dot(x, g_high) + dot(x, g_rest)
        v = dot(x, wqkv_ref[:, 2 * D :]).astype(BF16)
        v_ref[rows, :] = v
        top = jnp.max(a, axis=0, keepdims=True)
        w = jnp.exp(a - top)
        wx = dot_wide(w, expand)
        w = jnp.where(lane < 16, w, 0.0)
        packed += pltpu.roll(w, 16 * s, 1) if s else w
        vw = v.astype(F32) * wx
        weighted.append(vw.astype(BF16))
        t1, t2 = split2(top)
        t3 = (top - t1.astype(F32) - t2.astype(F32)).astype(BF16)
        tops = sum(dot(jnp.broadcast_to(t, (8, LANES)), expand) for t in (t1, t2, t3))
        msg_ref[s : s + 1, :] = tops[0:1, :]
        msg_ref[seqs + s : seqs + s + 1, :] = colsum(dec_r * vw)
        msg_ref[2 * seqs + s : 2 * seqs + s + 1, :] = colsum(dec_r * wx)
        msg_ref[3 * seqs + s : 3 * seqs + s + 1, :] = colsum(dec_f * vw)
        msg_ref[4 * seqs + s : 4 * seqs + s + 1, :] = colsum(dec_f * wx)
        offs_row = jnp.where(lane8 == s, sc_ref[4 + s].astype(F32), offs_row)
    msg_ref[MSG - 1 : MSG, :] = offs_row
    wx_ref[...] = packed
    local_decay_sums(
        slopes_ref, weighted, packed.astype(BF16), num_ref, den_ref, block_len, seqs
    )


def masked_kernel(others, seqs, block_len, rows_d, rows_f, low_count, top_bit, sc_ref, *refs):
    (flags_ref, msg_ref, *refs) = refs
    recv_refs, refs = refs[:others], refs[others:]
    (
        num_ref, den_ref, og_ref, wo_ref, vecs_ref, placex_ref, placey_ref, placed_ref,
        wgu_ref, wd_ref,
        as_ref, ak_ref, bs_ref, bk_ref,
        att_ref, invden_ref, dheads_ref, small_ref,
        wg_s, wu_s, wd_s, g_s, u_s, dk_s, ds_s, os_s, ok_s, lowx_s, lowy_s, mixed_s, d1_s, d2_s,
        acc_s, fn_s, in_sems, out_sems,
    ) = refs
    n = FF // CHUNK
    half = D // 2
    wide = CHUNK // 2
    me, z = sc_ref[0], sc_ref[1]
    tokens = seqs * block_len
    core = lax.shift_right_logical(me, top_bit) & 1
    plane = lax.shift_right_logical(me, top_bit + 1)

    def at(i):
        return pl.ds(pl.multiple_of(i * CHUNK, CHUNK), CHUNK)

    def loads(i):
        up_at = pl.ds(pl.multiple_of(FF + i * CHUNK, CHUNK), CHUNK)
        return [
            pltpu.make_async_copy(wgu_ref.at[:, at(i)], wg_s.at[i], in_sems.at[0, i]),
            pltpu.make_async_copy(wgu_ref.at[:, up_at], wu_s.at[i], in_sems.at[1, i]),
            pltpu.make_async_copy(wd_ref.at[at(i), :], wd_s.at[i], in_sems.at[2, i]),
        ]

    moves = gradient_moves(
        n, plane, (g_s, u_s, dk_s, ds_s, ok_s, os_s), (ak_ref, as_ref, bk_ref, bs_ref)
    )

    def stores(i, when):
        for k, (test, inside, outside) in enumerate(moves(i)):
            if test is not False:
                copy = pltpu.make_async_copy(inside, outside, out_sems.at[k, i])
                chosen(test, functools.partial(when, copy))

    out_copies = [
        pltpu.make_async_copy(inside, outside, out_sems.at[12, k])
        for k, (inside, outside) in enumerate(out_moves((ok_s, os_s), (bk_ref, bs_ref)))
    ]

    for i in range(n):
        for copy in loads(i):
            copy.start()

    slope_lane = vecs_ref[0:1, :]
    dec_f, dec_r = decay(slope_lane, block_len)
    invden = jnp.zeros((block_len, LANES), F32)
    for s in range(seqs):
        rows = slice(s * block_len, (s + 1) * block_len)

        def row(ref, kind):
            return ref[kind * seqs + s : kind * seqs + s + 1, :]

        own_off = lane_value(msg_ref[MSG - 1 : MSG, :], s)
        top = row(msg_ref, 0)
        for r in recv_refs:
            top = jnp.maximum(top, row(r, 0))
        own = jnp.exp(row(msg_ref, 0) - top)
        zero = jnp.zeros((1, D), F32)
        left_v, left_z, right_v, right_z = zero, zero, zero, zero
        for k, r in enumerate(recv_refs):
            gap = jnp.abs(lane_value(r[MSG - 1 : MSG, :], s) - own_off) - (block_len - 1.0)
            factor = jnp.exp(row(r, 0) - top - slope_lane * gap)
            is_left = (z ^ (k + 1)) < z
            f_left = jnp.where(is_left, factor, 0.0)
            f_right = jnp.where(is_left, 0.0, factor)
            left_v += f_left * row(r, 1)
            left_z += f_left * row(r, 2)
            right_v += f_right * row(r, 3)
            right_z += f_right * row(r, 4)
        den = own * dot_wide(den_ref[...], expand_seq(s)) + dec_f * left_z + dec_r * right_z
        num = own * num_ref[rows, :].astype(F32) + dec_f * left_v + dec_r * right_v
        inv = 1.0 / den
        invden = invden + dot_wide(inv * (1.0 / HD), reduce_seq(s))
        att_ref[rows, :] = (num * inv).astype(BF16)
    invden_ref[...] = invden
    rank = masked_ranks(flags_ref, seqs, tokens)
    small_ref[...] = jnp.zeros_like(small_ref)

    masked_tile(
        0, True, me, rows_d, rows_f, low_count, core, rank, att_ref, og_ref, wo_ref, vecs_ref,
        placex_ref, placey_ref, placed_ref, wg_s, wu_s, wd_s, g_s, u_s, dk_s, ds_s, os_s, ok_s,
        dheads_ref, small_ref, lowx_s, lowy_s, mixed_s, d1_s, d2_s, acc_s, fn_s, loads, stores,
    )
    for copy in out_copies:
        copy.start()
    for i in range(n):
        stores(i, lambda copy: copy.wait())
    for copy in out_copies:
        copy.wait()


SET_A = 4
B_ROWS_X = (FF // CHUNK - SET_A) * (D // 2) + FF // 4 + D // 2
B_ROWS_Y = (FF // CHUNK - SET_A) * (D // 2) + FF // 4


def chosen(test, work):
    if test is True:
        work()
    else:
        pl.when(test)(work)


def gradient_moves(n, plane, inside, outside):
    g_s, u_s, dk_s, ds_s, _ok, _os = inside
    ak_ref, as_ref, bk_ref, bs_ref = outside
    half, part = D // 2, CHUNK // 4
    b_x = (n - SET_A) * half

    def rows_at(first, size):
        return pl.ds(first if isinstance(first, int) else pl.multiple_of(first, 32), size)

    def moves(i):
        rel = i ^ plane
        x_rows = rows_at(b_x + swap_pair(rel) * part, part)
        y_rows = rows_at(B_ROWS_X + (n - SET_A) * half + rel * part, part)
        out = []
        for side, a_ref, b_ref, d in ((0, ak_ref, bk_ref, dk_s), (half, as_ref, bs_ref, ds_s)):
            rows = pl.ds(side, half)
            for value, a_first, b_first in (
                (g_s, 0, 0), (u_s, SET_A * half, B_ROWS_X)
            ):
                if isinstance(i, int):
                    at_a, at_b = min(i, SET_A - 1), max(i - SET_A, 0)
                else:
                    at_a, at_b = jnp.minimum(i, SET_A - 1), jnp.maximum(i - SET_A, 0)
                to_a = a_ref.at[rows_at(a_first + at_a * half, half)]
                to_b = b_ref.at[rows_at(b_first + at_b * half, half)]
                out.append((i < SET_A, value.at[i, rows], to_a))
                out.append((i >= SET_A, value.at[i, rows], to_b))
            out.append((True, d.at[i, pl.ds(0, part)], b_ref.at[x_rows]))
            out.append((True, d.at[i, pl.ds(part, part)], b_ref.at[y_rows]))
        return out

    return moves


def out_moves(inside, outside):
    rows = pl.ds(B_ROWS_X - D // 2, D // 2)
    return [(value, ref.at[rows]) for value, ref in zip(inside, outside)]


def masked_tile(
    t, first, me, rows_d, rows_f, low_count, core, rank, att_ref, og_ref, wo_ref, vecs_ref,
    placex_ref, placey_ref, placed_ref, wg_s, wu_s, wd_s, g_s, u_s, dk_s, ds_s, os_ref, ok_ref,
    dheads_ref, small_ref, lowx_s, lowy_s, mixed_s, d1_s, d2_s, acc_s, fn_s, loads, stores,
):
    n = FF // CHUNK
    half = D // 2
    wide = CHUNK // 2
    tokens = att_ref.shape[0]

    def put(ref, value):
        ref[...] = (value if first else ref[...].astype(F32) + value).astype(BF16)

    place = lax.broadcasted_iota(jnp.int32, (CAP, tokens), 0) + t * CAP
    comp = jnp.where(place.astype(F32) == rank, 1.0, 0.0).astype(BF16)
    att_low = (dot(comp, att_ref[...]) + vecs_ref[2:3, :]).astype(BF16)
    first_sum = vecs_ref[1:2, :] + (dot(att_low, wo_ref[...]) + vecs_ref[3:4, :])
    first_normed, first_scale = norm_rows(first_sum)
    fn_s[...] = first_normed
    low = (first_normed * vecs_ref[4:5, :] + vecs_ref[5:6, :]).astype(BF16)
    lowx_s[...] = dot(low, permuting(placex_ref[...], me, rows_d)).astype(BF16).T
    lowy_s[...] = dot(low, permuting(placey_ref[...], me, rows_d)).astype(BF16).T
    acc_s[...] = jnp.zeros((CAP, D), F32)

    def forward(i, c):
        for copy in loads(i):
            copy.wait()
        gate = dot(low, wg_s[i])
        up = dot(low, wu_s[i])
        phi = normal_cdf(gate)
        act = gate * phi
        mixed = (act * up).astype(BF16)
        mixed_s[i] = mixed
        d2_s[i] = act.astype(BF16)
        slope = phi + gate * (jnp.exp(-0.5 * gate * gate) * ((2.0 * math.pi) ** -0.5))
        d1_s[i] = (up * slope).astype(BF16)
        acc_s[...] += dot(mixed, wd_s[i])
        return c

    lax.fori_loop(0, n, forward, 0)
    first_out = fn_s[...] * vecs_ref[4:5, :] + vecs_ref[5:6, :]
    normed, scale = norm_rows(first_out + (acc_s[...] + vecs_ref[6:7, :]))
    up = dot(comp, og_ref[...])
    grad_second = norm_back(up, normed, scale, vecs_ref[7:8, :])
    acc_s[...] = grad_second
    bg = grad_second.astype(BF16)
    small_ref[0:1, :] += colsum(up * normed)
    small_ref[1:2, :] += colsum(up)
    small_ref[2:3, :] += colsum(bg.astype(F32))
    change_d = permuting(placed_ref[...], me & (low_count - 1), rows_f)

    def backward(i, c):
        mixed_grad = dot_nt(bg, wd_s[i]).astype(BF16).astype(F32)
        gate_grad = (mixed_grad * d1_s[i].astype(F32)).astype(BF16)
        up_grad = (mixed_grad * d2_s[i].astype(F32)).astype(BF16)
        put(g_s.at[i], dot(lowx_s[...], gate_grad))
        put(u_s.at[i], dot(lowy_s[...], up_grad))
        mixed = mixed_s[i]
        low_half, high_half = mixed[:, :wide], mixed[:, wide:]
        keep = jnp.where(core == 0, low_half, high_half)
        send = jnp.where(core == 0, high_half, low_half)
        put(dk_s.at[i], dot_tn(dot(keep, change_d).astype(BF16), bg))
        put(ds_s.at[i], dot_tn(dot(send, change_d).astype(BF16), bg))
        stores(i, lambda copy: copy.start())
        acc_s[...] += dot_nt(gate_grad, wg_s[i]) + dot_nt(up_grad, wu_s[i])
        return c

    lax.fori_loop(0, n, backward, 0)
    grad_first = acc_s[...]
    first_normed = fn_s[...]
    grad = norm_back(grad_first, first_normed, first_scale, vecs_ref[4:5, :])
    small_ref[3:4, :] += colsum(grad_first * first_normed)
    small_ref[4:5, :] += colsum(grad_first)
    attn_grad = grad.astype(BF16)
    small_ref[5:6, :] += colsum(attn_grad.astype(F32))
    small_ref[6:7, :] += colsum(grad)
    moved = dot(att_low, permuting(placex_ref[...], me, rows_d)).astype(BF16)
    grad_out = dot_tn(moved, attn_grad)
    put(ok_ref, grad_out[:half])
    put(os_ref, grad_out[half:])
    heads = dot_nt(attn_grad, wo_ref[...]).astype(BF16)
    small_ref[7:8, :] += colsum(heads.astype(F32))
    put(dheads_ref, dot_tn(comp, heads))


def masked_ranks(flags_ref, seqs, tokens):
    flags = jnp.concatenate([flags_ref[s : s + 1, :] for s in range(seqs)], axis=1).astype(F32)
    before = lax.broadcasted_iota(jnp.int32, (tokens, tokens), 0)
    after = lax.broadcasted_iota(jnp.int32, (tokens, tokens), 1)
    upper = jnp.where(before < after, 1.0, 0.0).astype(BF16)
    rank = dot(jnp.broadcast_to(flags, (8, tokens)).astype(BF16), upper)[0:1, :]
    return jnp.where(flags > 0.5, rank, -1.0)


def more_tiles_kernel(seqs, block_len, rows_d, rows_f, low_count, top_bit, sc_ref, *refs):
    held, (wgu_ref, wd_ref), grads, scratch = refs[:8], refs[8:10], refs[16:22], refs[22:]
    (
        flags_s, att_s, og_s, wo_s, vecs_s, placex_s, placey_s, placed_s, wg_s, wu_s, wd_s, g_s, u_s,
        dk_s, ds_s, os_s, ok_s, dheads_s, small_s, lowx_s, lowy_s, mixed_s, d1_s, d2_s, acc_s, fn_s,
        sem,
    ) = scratch
    as_ref, ak_ref, bs_ref, bk_ref, dheads_ref, small_ref = grads
    n = FF // CHUNK
    half = D // 2
    wide = CHUNK // 2
    me = sc_ref[0]
    core = lax.shift_right_logical(me, top_bit) & 1
    plane = lax.shift_right_logical(me, top_bit + 1)

    def move(source, target):
        copy = pltpu.make_async_copy(source, target, sem)
        copy.start()
        copy.wait()

    pairs = [(dheads_ref, dheads_s), (small_ref, small_s)]
    moves = gradient_moves(
        n, plane, (g_s, u_s, dk_s, ds_s, ok_s, os_s), (ak_ref, as_ref, bk_ref, bs_ref)
    )
    for i in range(n):
        pairs += [(outside, inside) for test, inside, outside in moves(i) if test is not False]
    pairs += [(o, i) for i, o in out_moves((ok_s, os_s), (bk_ref, bs_ref))]

    @pl.when(sc_ref[2] > 1)
    def _():
        for i in range(n):
            at = pl.ds(i * CHUNK, CHUNK)
            move(wgu_ref.at[:, at], wg_s.at[i])
            move(wgu_ref.at[:, pl.ds(FF + i * CHUNK, CHUNK)], wu_s.at[i])
            move(wd_ref.at[at, :], wd_s.at[i])
        for source, target in zip(held, scratch[:8]):
            move(source, target)
        for outside, inside in pairs:
            move(outside, inside)
        rank = masked_ranks(flags_s, seqs, seqs * block_len)

        def tile(t, carry):
            masked_tile(
                t, False, me, rows_d, rows_f, low_count, core, rank, att_s, og_s, wo_s, vecs_s,
                placex_s, placey_s, placed_s, wg_s, wu_s, wd_s, g_s, u_s, dk_s, ds_s, os_s, ok_s,
                dheads_s, small_s, lowx_s, lowy_s, mixed_s, d1_s, d2_s, acc_s, fn_s,
                lambda i: [], lambda i, when: None,
            )
            return carry

        lax.fori_loop(1, sc_ref[2], tile, 0)
        for outside, inside in pairs:
            move(inside, outside)


def inner_kernel(
    seqs, block_len, slopes_ref, dheads_ref, att_ref, invden_ref, vecs_ref, uv_ref, ud_ref, msg_ref
):
    slope_lane = vecs_ref[0:1, :]
    dec_f, dec_r = decay(slope_lane, block_len)
    wide = []
    packed = jnp.zeros((block_len, LANES), F32)
    msg_ref[...] = jnp.zeros_like(msg_ref)
    for s in range(seqs):
        rows = slice(s * block_len, (s + 1) * block_len)
        dheads = dheads_ref[rows, :].astype(F32)
        expand = expand_seq(s)
        inner = dot_wide(dheads * att_ref[rows, :].astype(F32), reduce_seq(s)) * invden_ref[...]
        packed += inner
        yv = dheads * dot_wide(invden_ref[...], expand)
        yd = dot_wide(inner, expand)
        wide.append(yv.astype(BF16))
        msg_ref[s : s + 1, :] = colsum(dec_r * yv)
        msg_ref[seqs + s : seqs + s + 1, :] = colsum(dec_r * yd)
        msg_ref[2 * seqs + s : 2 * seqs + s + 1, :] = colsum(dec_f * yv)
        msg_ref[3 * seqs + s : 3 * seqs + s + 1, :] = colsum(dec_f * yd)
    local_decay_sums(slopes_ref, wide, packed.astype(BF16), uv_ref, ud_ref, block_len, seqs)


def value_kernel(others, seqs, block_len, rows_d, sc_ref, *refs):
    (flags_ref, msg1_ref, msg2_ref, *refs) = refs
    recv1, recv2, refs = refs[:others], refs[others : 2 * others], refs[2 * others :]
    (
        uv_ref, ud_ref, wx_ref, v_ref, x_ref, wqkv_ref, g_ref, vecs_ref, placey_ref, smalla_ref,
        ig_ref, vs_ref, vk_ref, small_ref, dv_s, t_s,
    ) = refs
    me, z = sc_ref[0], sc_ref[1]
    slope_lane = vecs_ref[0:1, :]
    dec_f, dec_r = decay(slope_lane, block_len)
    reduce = reduce_one()
    embed = smalla_ref[6:7, :]
    half = D // 2
    for s in range(seqs):
        rows = slice(s * block_len, (s + 1) * block_len)

        def row(ref, kind):
            return ref[kind * seqs + s : kind * seqs + s + 1, :]

        own_off = lane_value(msg1_ref[MSG - 1 : MSG, :], s)
        top = row(msg1_ref, 0)
        for r in recv1:
            top = jnp.maximum(top, row(r, 0))
        own = jnp.exp(row(msg1_ref, 0) - top)
        zero = jnp.zeros((1, D), F32)
        left_v, left_d, right_v, right_d = zero, zero, zero, zero
        for k, (r1, r2) in enumerate(zip(recv1, recv2)):
            gap = jnp.abs(lane_value(r1[MSG - 1 : MSG, :], s) - own_off) - (block_len - 1.0)
            factor = jnp.exp(-slope_lane * gap)
            is_left = (z ^ (k + 1)) < z
            f_left = jnp.where(is_left, factor, 0.0)
            f_right = jnp.where(is_left, 0.0, factor)
            left_v += f_left * row(r2, 0)
            left_d += f_left * row(r2, 1)
            right_v += f_right * row(r2, 2)
            right_d += f_right * row(r2, 3)
        expand = expand_seq(s)
        weight = dot_wide(wx_ref[...], expand) * own
        uv = weight * (uv_ref[rows, :].astype(F32) + dec_f * left_v + dec_r * right_v)
        ud = weight * (dot_wide(ud_ref[...], expand) + dec_f * left_d + dec_r * right_d)
        dv = uv.astype(BF16)
        dv_s[rows, :] = dv
        t = dot_wide(uv * v_ref[rows, :].astype(F32) - ud * (1.0 / HD), reduce)
        t_s[rows, :] = t
        dx = dot_nt(dv, wqkv_ref[:, 2 * D :]) + dot_nt(t.astype(BF16), g_ref[...])
        masked = jnp.broadcast_to(flags_ref[rows, 0:1], (block_len, D)) > 0.5
        ig_ref[rows, :] = jnp.where(masked, 0.0, dx).astype(BF16)
        embed += colsum(jnp.where(masked, dx, 0.0))
    x = x_ref[...]
    xp = dot(x, permuting(placey_ref[...], me, rows_d)).astype(BF16)
    gv = dot_tn(xp, dv_s[...]).astype(BF16)
    vk_ref[...] = gv[:half]
    vs_ref[0:half, :] = gv[half:]
    t_high, t_rest = split2(t_s[...])
    a_t = (dot_tn(t_high, x) + dot_tn(t_rest, x))[0:16, :]
    both = dot_wide(a_t, wqkv_ref[:, D : 2 * D]) * (HD**-0.5)
    head = lax.broadcasted_iota(jnp.int32, (16, D), 0)
    lane = lax.broadcasted_iota(jnp.int32, (16, D), 1)
    query = colsum(jnp.where(lax.shift_right_logical(lane, 6) == head, both, 0.0))
    q_high, q_rest = split2(jnp.broadcast_to(query, (8, D)))
    wq = wqkv_ref[:, 0:D]
    embed += (dot_nt(q_high, wq) + dot_nt(q_rest, wq))[0:1, :]
    small_ref[0:8, :] = smalla_ref[...]
    small_ref[6:7, :] = embed
    small_ref[8:24, :] = a_t
    small_ref[20:21, :] = query
    put_small(vs_ref, half, small_ref[...])


FEATS = 6
LOG2E = math.log2(math.e)


def attention_kernel(s, spec, slopes_ref, sc_ref, q_ref, own_ref, wk_ref, wv_ref, *refs):
    others = len(spec)
    count = sum(len(group) for group in spec)
    part_refs, msg_refs, (msg_ref, vecs_ref, out_ref, k_s, v_s) = (
        refs[:count], refs[count : count + others], refs[count + others :],
    )
    block_len = q_ref.shape[0]
    z = sc_ref[1]
    lane = lax.broadcasted_iota(jnp.int32, (block_len, LANES), 1)
    token = lax.broadcasted_iota(jnp.int32, (block_len, LANES), 0).astype(F32)
    head_of = lane // FEATS
    kind = lane - head_of * FEATS
    row = lax.broadcasted_iota(jnp.int32, (block_len, block_len), 0)
    col = lax.broadcasted_iota(jnp.int32, (block_len, block_len), 1)
    apart = jnp.abs(row - col).astype(F32) * LOG2E
    qvalue = jnp.where(kind < 3, token, 1.0)

    for k in range(others):
        parts = [part_refs[at][...] for at in spec[k]]
        x = parts[0]
        if len(parts) == 2:
            x = jnp.where((z == 1) | (z == 2), parts[0], parts[1])
        k_s[k] = dot(x, wk_ref[...]).astype(BF16)
        v_s[k] = dot(x, wv_ref[...]).astype(BF16)

    slope = jnp.zeros((1, LANES), F32)
    lane1 = lax.broadcasted_iota(jnp.int32, (1, LANES), 1)
    for h in range(H):
        slope = jnp.where(lane1 // FEATS == h, slopes_ref[h] * LOG2E, slope)
    kind1 = lane1 - (lane1 // FEATS) * FEATS
    own_off = lane_value(msg_ref[MSG - 1 : MSG, :], s)
    feats = []
    for k in range(others):
        gap = jnp.abs(lane_value(msg_refs[k][MSG - 1 : MSG, :], s) - own_off)
        sign = jnp.where((z ^ (k + 1)) < z, 1.0, -1.0)
        value = jnp.where(kind1 < 3, -sign * slope, slope * (sign * token - gap))
        p1 = value.astype(BF16).astype(F32)
        p2 = (value - p1).astype(BF16).astype(F32)
        p3 = value - p1 - p2
        part = jnp.where(kind1 % 3 == 0, p1, jnp.where(kind1 % 3 == 1, p2, p3))
        feats.append(part.astype(BF16))
    ones = jnp.ones((block_len, LANES), BF16)
    zero = jnp.zeros((), BF16)
    for pair in range(H // 2):
        low, high = pair * LANES, (pair + 1) * LANES
        q = q_ref[:, low:high]
        own_k = own_ref[:, low:high]
        keys = [
            jnp.concatenate([k_s[k, :, low:high], feats[k]], axis=1) for k in range(others)
        ]
        own_v = jnp.concatenate([own_ref[:, D + low : D + high], ones], axis=1)
        values = [
            jnp.concatenate([v_s[k, :, low:high], ones], axis=1) for k in range(others)
        ]
        outs = []
        for e in range(2):
            h = 2 * pair + e
            mine = (lane < HD) if e == 0 else (lane >= HD)
            qh = jnp.where(mine, q, zero)
            qfeat = jnp.where(head_of == h, qvalue, 0.0).astype(BF16)
            qf = jnp.concatenate([qh, qfeat], axis=1)
            scores = [dot_nt(qh, own_k) - apart * slopes_ref[h]] + [dot_nt(qf, key) for key in keys]
            top = scores[0]
            for sc in scores[1:]:
                top = jnp.maximum(top, sc)
            top = jnp.max(top, axis=1, keepdims=True)
            total = dot(jnp.exp2(scores[0] - top).astype(BF16), own_v)
            for sc, value in zip(scores[1:], values):
                total += dot(jnp.exp2(sc - top).astype(BF16), value)
            outs.append(total[:, :LANES] / total[:, LANES:])
        out_ref[:, low:high] = (
            jnp.where(lane < HD, outs[0], outs[1]) + vecs_ref[2:3, low:high]
        ).astype(BF16)


def dense_kernel(seqs, x_ref, *refs):
    att_refs, (wo_ref, vecs_ref, wg_ref, wu_ref, wd_ref, out_ref, fo_s, low_s, acc_s) = (
        refs[:seqs], refs[seqs:],
    )
    step = pl.program_id(0)

    @pl.when(step == 0)
    def _():
        for s, att_ref in enumerate(att_refs):
            rows = slice(s * att_ref.shape[0], (s + 1) * att_ref.shape[0])
            first_sum = x_ref[rows, :].astype(F32) + (
                dot(att_ref[...], wo_ref[...]) + vecs_ref[3:4, :]
            )
            normed, _scale = norm_rows(first_sum)
            first_out = normed * vecs_ref[4:5, :] + vecs_ref[5:6, :]
            fo_s[rows, :] = first_out
            low_s[rows, :] = first_out.astype(BF16)
        acc_s[...] = jnp.zeros_like(acc_s)

    low = low_s[...]
    gate = dot(low, wg_ref[...])
    up = dot(low, wu_ref[...])
    mixed = (gate * normal_cdf(gate) * up).astype(BF16)
    acc_s[...] += dot(mixed, wd_ref[...])

    @pl.when(step == pl.num_programs(0) - 1)
    def _():
        normed, _scale = norm_rows(fo_s[...] + (acc_s[...] + vecs_ref[6:7, :]))
        out_ref[...] = (normed * vecs_ref[7:8, :] + vecs_ref[8:9, :]).astype(BF16)


def put_small(ref, at, small):
    high, rest = split2(small)
    ref[at : at + SMALL, :] = high
    ref[at + SMALL : at + 2 * SMALL, :] = rest


def get_small(ref, at):
    return ref[at : at + SMALL, :].astype(F32) + ref[at + SMALL : at + 2 * SMALL, :].astype(F32)


def add_rows_kernel(spec, join, *refs):
    count = len(spec)
    arrays, refs = refs[: 2 * count], refs[2 * count :]
    kept, sent = [], []
    for at, (first, segments) in enumerate(spec):
        keep, got = arrays[2 * at : 2 * at + 2]
        rows = sum(segments)
        total = keep[first : first + rows, :].astype(F32) + got[first : first + rows, :].astype(F32)
        one, two = halves(total, segments)
        kept.append(one)
        sent.append(two)
    small = None
    if len(refs) == 2 * len(join) + 2:
        small_ref, refs = refs[0], refs[1:]
        got = arrays[-1]
        top = got.shape[0] - 2 * SMALL
        small = (
            small_ref[...] + got[top : top + SMALL, :].astype(F32)
            + got[top + SMALL : top + 2 * SMALL, :].astype(F32)
        )
        refs[-1][...] = small
    for at, group in enumerate(join):
        keep_out, send_out = refs[2 * at : 2 * at + 2]
        keep_out[...] = jnp.concatenate([kept[k] for k in group], axis=0).astype(BF16)
        sending = jnp.concatenate([sent[k] for k in group], axis=0).astype(BF16)
        rows = sending.shape[0]
        send_out[0:rows, :] = sending
        if small is not None and at == len(join) - 1:
            high, rest = split2(small)
            send_out[rows : rows + SMALL, :] = high
            send_out[rows + SMALL : rows + 2 * SMALL, :] = rest


def add_rows(pieces, join, name, small=None):
    spec = [(first, tuple(segments)) for _k, _r, first, segments in pieces]
    arrays = [v for keep, got, _f, _s in pieces for v in (keep, got)]
    halved = [sum(segments) // 2 for _f, segments in spec]
    sizes = [sum(halved[k] for k in group) for group in join]
    if any(rows % 16 for _f, segments in spec for rows in segments):
        return add_rows_plain(pieces, join, small)
    cut = 2 if sum(sizes) > 1024 else 1
    col = lambda rows: pl.BlockSpec((rows, D // cut), lambda i: (0, i))
    outs = []
    for at, size in enumerate(sizes):
        more = 2 * SMALL if small is not None and at == len(sizes) - 1 else 0
        outs += [size, size + more]
    shapes = [jax.ShapeDtypeStruct((rows, D), BF16) for rows in outs]
    specs = [col(rows) for rows in outs]
    if small is not None:
        arrays.append(small)
        shapes.append(jax.ShapeDtypeStruct((SMALL, D), F32))
        specs.append(col(SMALL))
    return pl.pallas_call(
        functools.partial(add_rows_kernel, spec, join),
        name=name,
        grid=(cut,),
        out_shape=shapes,
        in_specs=[col(v.shape[0]) for v in arrays],
        out_specs=specs,
        compiler_params=params(),
        cost_estimate=cost(0.1),
    )(*arrays)


def add_rows_plain(pieces, join, small):
    kept, sent = [], []
    for keep, got, first, segments in pieces:
        rows = sum(segments)
        total = keep[first : first + rows].astype(F32) + got[first : first + rows].astype(F32)
        one, two = halves(total.astype(BF16), segments)
        kept.append(one)
        sent.append(two)
    outs = []
    for at, group in enumerate(join):
        outs.append(jnp.concatenate([kept[k] for k in group], axis=0))
        send = [sent[k] for k in group]
        if small is not None and at == len(join) - 1:
            tail = pieces[-1][1][-2 * SMALL :].astype(F32)
            small = small + tail[:SMALL] + tail[SMALL:]
            send += list(split2(small))
        outs.append(jnp.concatenate(send, axis=0))
    return outs + ([small] if small is not None else [])


def add_small_kernel(keep, small, got, keep_out, send_out, small_out):
    half = keep.shape[0] // 2
    total = keep[...].astype(F32) + got[0 : 2 * half, :].astype(F32)
    keep_out[...] = total[:half].astype(BF16)
    send_out[0:half, :] = total[half:].astype(BF16)
    both = small[...] + get_small(got, 2 * half)
    small_out[...] = both
    put_small(send_out, half, both)


def add_small(keep, small, got, name):
    rows = keep.shape[0] // 2
    full = lambda shape: pl.BlockSpec(shape, lambda i: (0, 0))
    return pl.pallas_call(
        add_small_kernel,
        name=name,
        grid=(1,),
        out_shape=[
            jax.ShapeDtypeStruct((rows, D), BF16), jax.ShapeDtypeStruct((2 * SMALL + rows, D), BF16),
            jax.ShapeDtypeStruct((SMALL, D), F32),
        ],
        in_specs=[full(keep.shape), full(small.shape), full(got.shape)],
        out_specs=[full((rows, D)), full((2 * SMALL + rows, D)), full((SMALL, D))],
        compiler_params=params(),
        cost_estimate=cost(0.1),
    )(keep, small, got)


def finish_kernel(
    rows_f, rows_d, sc_ref, a_k, a_r, b_k, b_r, small_ref, vecs_ref, qm_ref,
    gateup_ref, down_ref, out_ref, qkv_ref, *vector_refs,
):
    a_total = a_k[...].astype(F32) + a_r[...].astype(F32)
    rows_b = b_k.shape[0]
    b_total = b_k[...].astype(F32) + b_r[0:rows_b, :].astype(F32)
    gateup, down, out, value = unpack(a_total, b_total, rows_f, rows_d)
    for at, part in enumerate(gateup):
        gateup_ref[:, at * CHUNK : (at + 1) * CHUNK] = part
    down_ref[...] = down
    out_ref[...] = out
    small = (
        small_ref[...] + b_r[rows_b : rows_b + SMALL, :].astype(F32)
        + b_r[rows_b + SMALL : rows_b + 2 * SMALL, :].astype(F32)
    )
    row = lax.broadcasted_iota(jnp.int32, (D, LANES), 0)
    lane = lax.broadcasted_iota(jnp.int32, (D, LANES), 1)
    pick = jnp.where((row == lane + sc_ref[0] * rows_d) & (lane < rows_d), 1.0, 0.0).astype(BF16)
    both = jnp.concatenate([small, jnp.broadcast_to(vecs_ref[1:2, :], (8, D))], axis=0)
    p1 = both.astype(BF16)
    p2 = (both - p1.astype(F32)).astype(BF16)
    p3 = (both - p1.astype(F32) - p2.astype(F32)).astype(BF16)
    mine = dot(p1, pick) + dot(p2, pick) + dot(p3, pick)
    for ref, at in zip(vector_refs, SMALL_ROWS):
        ref[...] = mine[at : at + 1, 0:rows_d].reshape(rows_d)
    columns = mine.T
    emb = jnp.broadcast_to(columns[0:rows_d, SMALL : SMALL + 1], (rows_d, D))
    qkv_ref[:, 0:D] = emb * small[20:21, :]
    heads = columns[:, 8 : 8 + 16]
    key = jnp.concatenate(
        [jnp.broadcast_to(heads[0:rows_d, h : h + 1], (rows_d, HD)) for h in range(H)], axis=1
    )
    qkv_ref[:, D : 2 * D] = key * (qm_ref[0:1, :] * (HD**-0.5))
    qkv_ref[:, 2 * D :] = value


SMALL_ROWS = (6, 20, 7, 5, 3, 4, 2, 0, 1)


def unpack(a_total, b_total, rows_f, rows_d):
    n, part = FF // CHUNK, rows_f // 2
    more = n - SET_A
    a = [a_total[k * rows_d : (k + 1) * rows_d] for k in range(2 * SET_A)]
    at, b = 0, []
    for size in [rows_d] * more + [part, rows_d] + [rows_d] * more + [part, rows_d]:
        b.append(b_total[at : at + size])
        at += size
    gate, up = a[:SET_A] + b[:more], a[SET_A:] + b[more + 2 : 2 * more + 2]
    down = jnp.concatenate([b[more], b[2 * more + 2]], axis=0)
    return gate + up, down, b[more + 1], b[2 * more + 3]


def finish(scalars, a_k, a_r, b_k, b_r, small, vecs, qm, rows_f, rows_d):
    outs = [(rows_d, 2 * FF), (rows_f, D), (rows_d, D), (rows_d, 3 * D)] + [(rows_d,)] * 9
    if rows_d % 8:
        rows_b = b_k.shape[0]
        gateup, down, out, value = unpack(
            a_k.astype(F32) + a_r.astype(F32), b_k.astype(F32) + b_r[:rows_b].astype(F32), rows_f,
            rows_d,
        )
        small = small + b_r[rows_b : rows_b + SMALL].astype(F32) + b_r[rows_b + SMALL :].astype(F32)
        mine = lax.dynamic_slice_in_dim(small, scalars[0] * rows_d, rows_d, 1)
        emb = lax.dynamic_slice_in_dim(vecs[1], scalars[0] * rows_d, rows_d, 0)
        key = jnp.repeat(mine[8 : 8 + H].T, HD, axis=1) * (qm[0:1, :] * (HD**-0.5))
        qkv = jnp.concatenate([emb[:, None] * small[20][None, :], key, value], axis=1)
        return [jnp.concatenate(gateup, axis=1), down, out, qkv] + [mine[k] for k in SMALL_ROWS]
    full = lambda shape: pl.BlockSpec(shape, lambda i: (0,) * len(shape))
    arrays = (a_k, a_r, b_k, b_r, small, vecs, qm)
    return pl.pallas_call(
        functools.partial(finish_kernel, rows_f, rows_d),
        name="finish",
        grid=(1,),
        out_shape=[jax.ShapeDtypeStruct(o, F32) for o in outs],
        in_specs=[smem()] + [full(v.shape) for v in arrays],
        out_specs=[full(o) for o in outs],
        compiler_params=params(),
        cost_estimate=cost(1),
    )(scalars, *arrays)


def halves(total, segments):
    first, second, at = [], [], 0
    for rows in segments:
        first.append(total[at : at + rows // 2])
        second.append(total[at + rows // 2 : at + rows])
        at += rows
    return jnp.concatenate(first, axis=0), jnp.concatenate(second, axis=0)


def bit_orders(batch, blocks):
    n = int(math.log2(batch * blocks))
    seq_bits = int(math.log2(blocks))
    rest = list(range(seq_bits, n - 3)) + list(range(seq_bits))
    top = [n - 3, n - 2, n - 1]
    return [*top, *rest], [top[0], top[2], top[1], *rest], rest


def places(order, rows, parts=1):
    n = len(order)
    place = np.arange(2**n)
    rel = np.zeros(2**n, np.int32)
    for k, bit in enumerate(order):
        rel |= ((place >> (n - 1 - k)) & 1).astype(np.int32) << bit
    out = np.zeros((8, 2**n * rows), np.int32)
    size = rows // parts
    out[0] = np.tile(np.repeat(rel, size), parts)
    out[1] = np.concatenate([np.tile(np.arange(size) + p * size, 2**n) for p in range(parts)])
    return out


def swap_pair(i):
    return (i & 1) * 2 + lax.shift_right_logical(i, 1)


def smem():
    return pl.BlockSpec(memory_space=pltpu.SMEM)


def masked_rows(
    batch, blocks, scalars, mask_flags, msg1, recv1, num, den, grad, out_weight, vecs,
    gate_up_weight, down_weight,
):
    seqs, block_len = mask_flags.shape
    tokens = seqs * block_len
    shards = batch * blocks
    others = blocks - 1
    n = FF // CHUNK
    half = D // 2
    order_x, order_y, order_rest = bit_orders(batch, blocks)
    top_bit = len(order_x) - 3
    vmem, hbm = pl.BlockSpec(memory_space=pltpu.VMEM), pl.BlockSpec(memory_space=pl.ANY)
    bf_full = jax.ShapeDtypeStruct((tokens, D), BF16)
    set_a = jax.ShapeDtypeStruct((2 * SET_A * half, D), BF16)
    set_b = jax.ShapeDtypeStruct((B_ROWS_X + B_ROWS_Y, D), BF16)
    chunks = lambda rows, width: pltpu.VMEM((n, rows, width), BF16)
    grads = [set_a] * 2 + [set_b] * 2
    square_s = pltpu.VMEM((half, D), BF16)
    weights_s = [
        chunks(D, CHUNK), chunks(D, CHUNK), chunks(CHUNK, D), chunks(D, CHUNK), chunks(D, CHUNK),
        chunks(CHUNK // 2, D), chunks(CHUNK // 2, D),
    ]
    tile_s = [
        pltpu.VMEM((D, CAP), BF16), pltpu.VMEM((D, CAP), BF16), chunks(CAP, CHUNK),
        chunks(CAP, CHUNK), chunks(CAP, CHUNK), pltpu.VMEM((CAP, D), F32), pltpu.VMEM((CAP, D), F32),
    ]
    held = [
        places(order_x, D // shards), places(order_y, D // shards),
        places(order_rest, FF // shards, 2),
    ]
    small = jax.ShapeDtypeStruct((8, D), F32)
    packed = jax.ShapeDtypeStruct((block_len, LANES), F32)
    *sums, att, invden, dheads, small_sums = pl.pallas_call(
        functools.partial(
            masked_kernel, others, seqs, block_len, D // shards, FF // shards, shards // 8, top_bit
        ),
        name="masked_rows",
        out_shape=grads + [bf_full, packed, bf_full, small],
        in_specs=[smem()] + [vmem] * (10 + len(recv1)) + [hbm] * 2,
        out_specs=[hbm] * 4 + [vmem] * 4,
        scratch_shapes=weights_s + [square_s, square_s] + tile_s
        + [pltpu.SemaphoreType.DMA((3, n)), pltpu.SemaphoreType.DMA((13, n))],
        compiler_params=params(62),
        cost_estimate=cost(60),
    )(
        scalars, mask_flags, msg1, *recv1, num, den, grad, out_weight, vecs, *held, gate_up_weight,
        down_weight,
    )
    *sums, dheads, small_sums = pl.pallas_call(
        functools.partial(
            more_tiles_kernel, seqs, block_len, D // shards, FF // shards, shards // 8, top_bit
        ),
        name="more_masked_rows",
        out_shape=grads + [bf_full, small],
        in_specs=[smem()] + [hbm] * 16,
        out_specs=[hbm] * 6,
        input_output_aliases={11 + k: k for k in range(6)},
        scratch_shapes=[
            pltpu.VMEM(mask_flags.shape, jnp.int32), pltpu.VMEM((tokens, D), BF16),
            pltpu.VMEM((tokens, D), BF16), pltpu.VMEM((D, D), BF16), pltpu.VMEM((16, D), F32),
        ]
        + [pltpu.VMEM(h.shape, jnp.int32) for h in held]
        + weights_s
        + [square_s, square_s, pltpu.VMEM((tokens, D), BF16), pltpu.VMEM((8, D), F32)]
        + tile_s
        + [pltpu.SemaphoreType.DMA],
        compiler_params=params(62),
        cost_estimate=cost(1),
    )(
        scalars, mask_flags, att, grad, out_weight, vecs, *held, gate_up_weight, down_weight, *sums,
        dheads, small_sums,
    )
    return (*sums, att, invden, dheads, small_sums)


def on_device(
    hidden_states, mask_flags, block_offsets, alibi_slopes, mask_embedding, qkv_weight, query_bias,
    value_bias, out_weight, out_bias, first_gain, first_shift, gate_up_weight, down_weight,
    down_bias, second_gain, second_shift, output_grad,
):
    seqs, block_len = mask_flags.shape
    tokens = seqs * block_len
    batch, blocks = lax.axis_size("batch"), lax.axis_size("seq")
    shards = batch * blocks
    z = lax.axis_index("seq")
    me = lax.axis_index("batch") * blocks + z
    order_x, order_y, order_rest = bit_orders(batch, blocks)
    seq_bits = int(math.log2(blocks))
    place_y = places(order_y, D // shards)
    top_bit = len(order_x) - 3
    n = FF // CHUNK
    half = D // 2
    square = jax.ShapeDtypeStruct((half, D), BF16)
    others = blocks - 1
    vmem = pl.BlockSpec(memory_space=pltpu.VMEM)
    packed = jax.ShapeDtypeStruct((block_len, LANES), F32)
    bf_full = jax.ShapeDtypeStruct((tokens, D), BF16)
    last = [()]

    def after(*values):
        tied = lax.optimization_barrier((values, last[0]))[0]
        return tied if len(values) > 1 else tied[0]

    def done(value):
        last[0] = value

    def along(value, axis, pairs):
        return lax.ppermute(value, axis, pairs)

    def flip(value, bit):
        if bit >= seq_bits:
            axis, size, mask = "batch", batch, 1 << (bit - seq_bits)
        else:
            axis, size, mask = "seq", blocks, 1 << bit
        return along(value, axis, [(i, i ^ mask) for i in range(size)])

    fixed = lambda shape: pl.BlockSpec(shape, lambda i: (0,) * len(shape))
    x, vecs, flagx, scalars = pl.pallas_call(
        functools.partial(inputs_kernel, seqs, block_len, blocks),
        name="inputs",
        grid=(1,),
        out_shape=(
            bf_full, jax.ShapeDtypeStruct((16, D), F32), jax.ShapeDtypeStruct((tokens, LANES), F32),
            jax.ShapeDtypeStruct((8,), jnp.int32),
        ),
        in_specs=[smem(), smem(), fixed((tokens, D)), fixed((seqs, block_len))] + [fixed((D,))] * 9,
        out_specs=[
            fixed((tokens, D)), fixed((16, D)), fixed((tokens, LANES)), smem(),
        ],
        compiler_params=params(),
        cost_estimate=cost(1),
    )(
        alibi_slopes, block_offsets.reshape(1, seqs), hidden_states.reshape(tokens, D), mask_flags,
        mask_embedding, value_bias, out_bias, first_gain, first_shift, down_bias, second_gain,
        second_shift, query_bias,
    )

    near = [(i, i ^ 1) for i in range(blocks)]
    hops = blocks == 4

    def centre(value):
        pairs = []
        for b in range(batch):
            for at in range(blocks):
                to = b * blocks + 3 - at if at in (1, 2) else (b ^ 1) * blocks + at
                pairs.append((b * blocks + at, to))
        return along(value, ("batch", "seq"), pairs)

    def held(*values):
        values = after(*values)
        done(values)
        return values

    v, wx, num, den, msg1, g, qm = pl.pallas_call(
        functools.partial(prep_kernel, seqs, block_len),
        name="masked_prep",
        out_shape=(
            bf_full, packed, bf_full, packed, jax.ShapeDtypeStruct((MSG, D), F32),
            jax.ShapeDtypeStruct((D, LANES), BF16), jax.ShapeDtypeStruct((8, D), F32),
        ),
        in_specs=[smem(), smem()] + [vmem] * 3,
        out_specs=[vmem] * 7,
        compiler_params=params(),
        cost_estimate=cost(10),
    )(alibi_slopes, scalars, x, qkv_weight, vecs)
    done(msg1)
    recv1 = [along(msg1, "seq", [(i, i ^ k) for i in range(blocks)]) for k in range(1, blocks)]

    q_own = project(after(x), qkv_weight, vecs, 0, 1, LOG2E * HD**-0.5)
    done(q_own)
    recv1 = list(held(*recv1, msg1))[:-1]
    x_late = after(x)
    if hops:
        round1 = along(x_late, "seq", near), centre(x_late)
    else:
        round1 = tuple(
            along(x_late, "seq", [(i, i ^ k) for i in range(blocks)]) for k in range(1, blocks)
        )

    a_s, a_k, b_s, b_k, att_m, invden, dheads, small_a = masked_rows(
        batch, blocks, scalars, mask_flags, msg1, recv1, num, den,
        after(output_grad.reshape(tokens, D)), out_weight, vecs, gate_up_weight, down_weight,
    )
    done(small_a)
    round1 = held(*round1)
    if hops:
        round2 = along(round1[1], "seq", near), centre(round1[0])
    a_r, b_r = flip(a_s, order_x[0]), flip(b_s, order_x[0])

    uv, ud, msg2 = pl.pallas_call(
        functools.partial(inner_kernel, seqs, block_len),
        name="masked_inner",
        out_shape=(bf_full, packed, jax.ShapeDtypeStruct((MSG, D), F32)),
        in_specs=[smem()] + [vmem] * 4,
        out_specs=[vmem] * 3,
        compiler_params=params(),
        cost_estimate=cost(60),
    )(alibi_slopes, after(dheads), att_m, invden, vecs)
    done(msg2)

    rows_a = SET_A * half
    seg_a = [[half] * SET_A] * 2
    more = n - SET_A
    seg_b = [[half] * more + [FF // 4, half], [half] * more + [FF // 4]]
    cut_in_half = lambda groups: [[rows // 2 for rows in group] for group in groups]
    a_k, a_r = after(a_k, a_r)
    ax_k, ax_s, ay_k, ay_s = add_rows(
        [(a_k, a_r, 0, seg_a[0]), (a_k, a_r, rows_a, seg_a[1])], [[0], [1]], "add_core_a"
    )
    done(ax_k)
    ax_r, ay_r = flip(ax_s, order_x[1]), flip(ay_s, order_y[1])
    b_k, b_r = after(b_k, b_r)
    bx_k, bx_s, by_k, by_s = add_rows(
        [(b_k, b_r, 0, seg_b[0]), (b_k, b_r, B_ROWS_X, seg_b[1])], [[0], [1]], "add_core_b"
    )
    done(bx_k)
    seg_a, seg_b = cut_in_half(seg_a), cut_in_half(seg_b)
    if hops:
        round2 = held(*round2)
    msg2_now = after(msg2)
    recv2 = [along(msg2_now, "seq", [(i, i ^ k) for i in range(blocks)]) for k in range(1, blocks)]
    kv_own = project(after(x), qkv_weight, vecs, 1, 2)
    done(kv_own)
    recv2 = list(held(*recv2, msg2))[:-1]
    if hops:
        far = along(after(round2[1]), "seq", near)

    bx_s, by_s = after(bx_s, by_s)
    bx_r, by_r = flip(bx_s, order_x[1]), flip(by_s, order_y[1])
    input_grad, value_s, value_k, small = pl.pallas_call(
        functools.partial(value_kernel, others, seqs, block_len, D // shards),
        name="value_grads",
        out_shape=(
            bf_full, jax.ShapeDtypeStruct((2 * SMALL + half, D), BF16),
            jax.ShapeDtypeStruct((half, D), BF16), jax.ShapeDtypeStruct((SMALL, D), F32),
        ),
        in_specs=[smem()] + [vmem] * (13 + len(recv1) + len(recv2)),
        out_specs=[vmem] * 4,
        scratch_shapes=[pltpu.VMEM((tokens, D), BF16), pltpu.VMEM((tokens, LANES), F32)],
        compiler_params=params(),
        cost_estimate=cost(60),
    )(
        scalars, flagx, msg1, msg2, *recv1, *recv2, uv, ud, wx, v, after(x), qkv_weight, g, vecs,
        place_y, small_a,
    )
    done(small)
    value_r = flip(after(value_s), order_y[0])
    ax_k, ax_r, ay_k, ay_r = after(ax_k, ax_r, ay_k, ay_r)
    ax_k, ax_s, ay_k, ay_s = add_rows(
        [(ax_k, ax_r, 0, seg_a[0]), (ay_k, ay_r, 0, seg_a[1])], [[0], [1]], "add_xy_a"
    )
    done(ax_k)
    ax_r, ay_r = flip(ax_s, order_x[2]), flip(ay_s, order_y[2])
    seg_a = cut_in_half(seg_a)
    value_k, value_s, small = add_small(*after(value_k, small, value_r), "add_core_value")
    done(small)
    value_r = flip(after(value_s), order_y[1])
    if hops:
        far, _ = held(far, small)
    if hops:
        groups = [
            [round1[0]], [round2[1], round2[0]], [round1[1], far],
        ]
    else:
        groups = [[part] for part in round1]

    def attend(s, micros):
        block = lambda at, width=D: pl.BlockSpec((block_len, width), lambda i: (at, 0))
        spec, parts = [], []
        for group in groups:
            spec.append(list(range(len(parts), len(parts) + len(group))))
            parts += group
        out = pl.pallas_call(
            functools.partial(attention_kernel, s, spec),
            name="dense_attention",
            out_shape=jax.ShapeDtypeStruct((block_len, D), BF16),
            grid=(1,),
            in_specs=[smem(), smem(), block(s), block(s, 2 * D)]
            + [pl.BlockSpec((D, D), lambda i: (0, 1)), pl.BlockSpec((D, D), lambda i: (0, 2))]
            + [block(s)] * len(parts)
            + [pl.BlockSpec((MSG, D), lambda i: (0, 0))] * (others + 2),
            out_specs=block(0),
            scratch_shapes=[pltpu.VMEM((others, block_len, D), BF16)] * 2,
            compiler_params=params(),
            cost_estimate=cost(micros),
        )(
            alibi_slopes, scalars, after(q_own), kv_own, qkv_weight, qkv_weight, *parts, *recv1, msg1,
            vecs,
        )
        done(out)
        return out

    attended = [attend(0, 0.1)]
    bx_r, by_r = held(bx_r, by_r)
    attended.append(attend(1, 0.1))
    bx_k, bx_r, by_k, by_r, value_k, value_r = after(bx_k, bx_r, by_k, by_r, value_k, value_r)
    bx_k, bx_s, by_k, by_s, small = add_rows(
        [
            (bx_k, bx_r, 0, seg_b[0]), (by_k, by_r, 0, seg_b[1]),
            (value_k, value_r, 0, [value_k.shape[0]]),
        ],
        [[0], [1, 2]], "add_xy_b", small,
    )
    done(bx_k)
    bx_r, by_r = flip(bx_s, order_x[2]), flip(by_s, order_y[2])
    seg_b = cut_in_half([seg_b[0], seg_b[1] + [value_k.shape[0]]])
    ax_k, ax_r, ay_k, ay_r = after(ax_k, ax_r, ay_k, ay_r)
    a_k, a_s = add_rows(
        [(ax_k, ax_r, 0, seg_a[0]), (ay_k, ay_r, 0, seg_a[1])], [[0, 1]], "add_a"
    )
    done(a_k)
    a_r = flip(a_s, order_rest[0])
    seg_a = cut_in_half([seg_a[0] + seg_a[1]])
    attended += [attend(s, 60) for s in range(2, seqs)]

    def step_a(bit):
        nonlocal a_k, a_r, seg_a
        a_k, a_r = after(a_k, a_r)
        a_k, a_s = add_rows([(a_k, a_r, 0, seg_a[0])], [[0]], "add_a")
        done(a_k)
        seg_a = cut_in_half(seg_a)
        a_r = flip(a_s, bit)

    def step_b(bit):
        nonlocal b_k, b_r, seg_b, small
        b_k, b_r, small = after(b_k, b_r, small)
        b_k, b_s, small = add_rows([(b_k, b_r, 0, seg_b[0])], [[0]], "add_b", small)
        done(b_k)
        seg_b = cut_in_half(seg_b)
        b_r = flip(b_s, bit)

    bx_k, bx_r, by_k, by_r = after(bx_k, bx_r, by_k, by_r)
    b_k, b_s, small = add_rows(
        [(bx_k, bx_r, 0, seg_b[0]), (by_k, by_r, 0, seg_b[1])], [[0, 1]], "add_b", small
    )
    done(b_k)
    b_r = flip(b_s, order_rest[0])
    seg_b = cut_in_half([seg_b[0] + seg_b[1]])

    step_a(order_rest[1])

    output = pl.pallas_call(
        functools.partial(dense_kernel, seqs),
        name="dense_ffn",
        out_shape=bf_full,
        grid=(n,),
        in_specs=[vmem] * (3 + seqs)
        + [
            pl.BlockSpec((D, CHUNK), lambda i: (0, i)),
            pl.BlockSpec((D, CHUNK), lambda i: (0, n + i)),
            pl.BlockSpec((CHUNK, D), lambda i: (i, 0)),
        ],
        out_specs=vmem,
        scratch_shapes=[
            pltpu.VMEM((tokens, D), F32), pltpu.VMEM((tokens, D), BF16), pltpu.VMEM((tokens, D), F32),
        ],
        compiler_params=params(),
        cost_estimate=cost(60),
    )(x, *after(*attended), out_weight, vecs, gate_up_weight, gate_up_weight, down_weight)
    done(output)

    (a_r, _) = held(a_r, output)
    step_b(order_rest[1])
    for bit in order_rest[2:]:
        step_a(bit)
        step_b(bit)
    (
        grad_gateup, grad_down, grad_outw, grad_qkv, grad_embed, grad_qbias, grad_vbias, grad_outb,
        grad_gain1, grad_shift1, grad_downb, grad_gain2, grad_shift2,
    ) = finish(
        scalars, *after(a_k, a_r, b_k, b_r, small), vecs, qm, FF // shards, D // shards,
    )

    shape = (seqs, block_len, D)
    return (
        output.reshape(shape), input_grad.reshape(shape), grad_embed, grad_qkv, grad_qbias,
        grad_vbias, grad_outw, grad_outb, grad_gain1, grad_shift1, grad_gateup, grad_down,
        grad_downb, grad_gain2, grad_shift2,
    )


def solution(mesh):
    data, pairs = P("batch", "seq", None), P("batch", "seq")
    in_specs = (data, pairs, pairs) + (P(),) * 14 + (data,)
    vector, matrix = P(("batch", "seq")), P(("batch", "seq"), None)
    out_specs = (
        data, data, vector, matrix, vector, vector, matrix, vector, vector, vector, matrix, matrix,
        vector, vector, vector,
    )
    return jax.shard_map(
        on_device, mesh=mesh, in_specs=in_specs, out_specs=out_specs, check_vma=False
    )
```

```python
import functools
import math

import jax
import jax.numpy as jnp
import numpy as np
from jax import lax
from jax.experimental import pallas as pl
from jax.experimental.pallas import tpu as pltpu
from jax.sharding import PartitionSpec as P

D = 768
FF = 3072
H = 12
HD = 64
CAP = 192
CHUNK = 768
LANES = 128
MSG = 16
SMALL = 24

F32 = jnp.float32
BF16 = jnp.bfloat16


def params(limit=62):
    return pltpu.CompilerParams(vmem_limit_bytes=limit * 1024 * 1024)


def cost(micros):
    return pl.CostEstimate(flops=int(micros * 1.15e9), bytes_accessed=1024, transcendentals=0)


def dot(a, b):
    return lax.dot_general(a, b, (((1,), (0,)), ((), ())), preferred_element_type=F32)


def dot_nt(a, b):
    return lax.dot_general(a, b, (((1,), (1,)), ((), ())), preferred_element_type=F32)


def dot_tn(a, b):
    return lax.dot_general(a, b, (((0,), (0,)), ((), ())), preferred_element_type=F32)


def split2(v):
    high = v.astype(BF16)
    return high, (v - high.astype(F32)).astype(BF16)


def dot_wide(v, b):
    high, rest = split2(v)
    return dot(high, b) + dot(rest, b)


def expand_one():
    row = lax.broadcasted_iota(jnp.int32, (LANES, D), 0)
    lane = lax.broadcasted_iota(jnp.int32, (LANES, D), 1)
    return jnp.where(lax.shift_right_logical(lane, 6) == row, 1.0, 0.0).astype(BF16)


def expand_seq(s):
    row = lax.broadcasted_iota(jnp.int32, (LANES, D), 0)
    lane = lax.broadcasted_iota(jnp.int32, (LANES, D), 1)
    return jnp.where(lax.shift_right_logical(lane, 6) + 16 * s == row, 1.0, 0.0).astype(BF16)


def reduce_seq(s):
    row = lax.broadcasted_iota(jnp.int32, (D, LANES), 0)
    lane = lax.broadcasted_iota(jnp.int32, (D, LANES), 1)
    return jnp.where(lax.shift_right_logical(row, 6) + 16 * s == lane, 1.0, 0.0).astype(BF16)


def reduce_one():
    row = lax.broadcasted_iota(jnp.int32, (D, LANES), 0)
    lane = lax.broadcasted_iota(jnp.int32, (D, LANES), 1)
    return jnp.where(lax.shift_right_logical(row, 6) == lane, 1.0, 0.0).astype(BF16)


def permuting(place_row, me, rows):
    n = place_row.shape[1]
    distance = place_row[0:1, :]
    source = (distance ^ me) * rows + place_row[1:2, :]
    row = lax.broadcasted_iota(jnp.int32, (n, n), 0)
    return jnp.where(row == source, 1.0, 0.0).astype(BF16)


def decay(slope_lane, block_len):
    t = lax.broadcasted_iota(jnp.int32, (block_len, D), 0).astype(F32)
    return jnp.exp(-slope_lane * t), jnp.exp(-slope_lane * (block_len - 1.0 - t))


def head_decay(slope, block_len):
    row = lax.broadcasted_iota(jnp.int32, (block_len, block_len), 0)
    lane = lax.broadcasted_iota(jnp.int32, (block_len, block_len), 1)
    return jnp.exp(-slope * jnp.abs(row - lane).astype(F32)).astype(BF16)


def local_decay_sums(slopes_ref, wide, packed, wide_out, packed_out, block_len, seqs):
    lane = lax.broadcasted_iota(jnp.int32, (block_len, LANES), 1)
    total = jnp.zeros((block_len, LANES), F32)
    for pair in range(H // 2):
        low, high = pair * LANES, (pair + 1) * LANES
        right = jnp.concatenate([wide[s][:, low:high] for s in range(seqs)] + [packed], axis=1)
        even = dot(head_decay(slopes_ref[2 * pair], block_len), right)
        odd = dot(head_decay(slopes_ref[2 * pair + 1], block_len), right)
        for s in range(seqs):
            rows = slice(s * block_len, (s + 1) * block_len)
            at = slice(s * LANES, (s + 1) * LANES)
            wide_out[rows, low:high] = jnp.where(lane < HD, even[:, at], odd[:, at]).astype(
                wide_out.dtype
            )
        at = slice(seqs * LANES, (seqs + 1) * LANES)
        total = jnp.where((lane & 15) == 2 * pair, even[:, at], total)
        total = jnp.where((lane & 15) == 2 * pair + 1, odd[:, at], total)
    packed_out[...] = total


def lane_value(row, index):
    lane = lax.broadcasted_iota(jnp.int32, row.shape, 1)
    return jnp.sum(jnp.where(lane == index, row, 0.0), axis=1, keepdims=True)


GELU = (
    0.7978849414614602, 0.03633308456815623, -3.259496805730905e-05, -5.530619733817487e-05,
    3.9647451634764645e-06, -1.322634044387524e-07, 1.756172658552303e-09,
)


def normal_cdf(v):
    square = v * v
    poly = GELU[6]
    for c in GELU[5::-1]:
        poly = poly * square + c
    return 0.5 + 0.5 * jnp.tanh(v * poly)


def norm_rows(v):
    centred = v - jnp.mean(v, axis=1, keepdims=True)
    scale = lax.rsqrt(jnp.mean(centred * centred, axis=1, keepdims=True) + 1e-05)
    return centred * scale, scale


def norm_back(upstream, normed, scale, gain):
    scaled = upstream * gain
    return scale * (
        scaled
        - jnp.mean(scaled, axis=1, keepdims=True)
        - normed * jnp.mean(scaled * normed, axis=1, keepdims=True)
    )


def colsum(v):
    return jnp.sum(v, axis=0, keepdims=True)


def inputs_kernel(seqs, block_len, blocks, slopes_ref, offs_ref, hidden_ref, flags_ref, *refs):
    vec_refs, (x_ref, vecs_ref, flagx_ref, sc_ref) = refs[:-4], refs[-4:]
    emb = vec_refs[0][...].astype(F32).reshape(1, D)
    lane = lax.broadcasted_iota(jnp.int32, (1, D), 1)
    slope = jnp.zeros((1, D), F32)
    for h in range(H):
        slope = jnp.where(lax.shift_right_logical(lane, 6) == h, slopes_ref[h], slope)
    vecs_ref[...] = jnp.zeros_like(vecs_ref)
    vecs_ref[0:1, :] = slope
    for k, r in enumerate(vec_refs):
        vecs_ref[k + 1 : k + 2, :] = r[...].astype(F32).reshape(1, D)
    sc_ref[0] = lax.axis_index("batch") * blocks + lax.axis_index("seq")
    sc_ref[1] = lax.axis_index("seq")
    sc_ref[2] = jnp.maximum(1, (jnp.sum(flags_ref[...]) + CAP - 1) // CAP)
    flags = flags_ref[...].astype(F32)
    for s in range(seqs):
        rows = slice(s * block_len, (s + 1) * block_len)
        column = jnp.broadcast_to(flags[s : s + 1, :], (LANES, block_len)).T
        flagx_ref[rows, :] = column
        mask = jnp.broadcast_to(column[:, 0:1], (block_len, D)) > 0.5
        x_ref[rows, :] = jnp.where(mask, emb, hidden_ref[rows, :].astype(F32)).astype(BF16)
        sc_ref[4 + s] = offs_ref[0, s]


def project_kernel(scale, x_ref, w_ref, bias_ref, out_ref):
    out = dot(x_ref[...], w_ref[...])
    if scale is not None:
        out = (out + bias_ref[9:10, :]) * scale
    out_ref[...] = out.astype(BF16)


def project(x, weight, vecs, first, count, scale=None):
    return pl.pallas_call(
        functools.partial(project_kernel, scale),
        name="project",
        out_shape=jax.ShapeDtypeStruct((x.shape[0], count * D), BF16),
        grid=(count,),
        in_specs=[
            pl.BlockSpec(x.shape, lambda i: (0, 0)),
            pl.BlockSpec((D, D), lambda i: (0, first + i)), pl.BlockSpec((16, D), lambda i: (0, 0)),
        ],
        out_specs=pl.BlockSpec((x.shape[0], D), lambda i: (0, i)),
        compiler_params=params(),
        cost_estimate=cost(0.1),
    )(x, weight, vecs)


def prep_kernel(
    seqs, block_len, slopes_ref, sc_ref, x_ref, wqkv_ref, vecs_ref,
    v_ref, vw_ref, wx_ref, msg_ref, g_ref, qm_ref,
):
    slope_lane = vecs_ref[0:1, :]
    emb8 = jnp.broadcast_to(vecs_ref[1:2, :], (8, D)).astype(BF16)
    qm = (dot(emb8, wqkv_ref[:, 0:D]) + vecs_ref[9:10, :]).astype(BF16).astype(F32)
    qm_ref[...] = qm
    scaled = wqkv_ref[:, D : 2 * D].astype(F32) * (qm[0:1, :] * (HD**-0.5))
    g = dot_wide(scaled, reduce_one())
    g_high, g_rest = split2(g)
    g_ref[...] = g_high
    expand = expand_one()
    dec_f, dec_r = decay(slope_lane, block_len)
    packed = jnp.zeros((block_len, LANES), F32)
    lane = lax.broadcasted_iota(jnp.int32, (block_len, LANES), 1)
    msg_ref[...] = jnp.zeros_like(msg_ref)
    lane8 = lax.broadcasted_iota(jnp.int32, (1, D), 1)
    offs_row = jnp.zeros((1, D), F32)
    x = x_ref[...]
    both = dot(x, jnp.concatenate([g_high, g_rest], axis=1))
    v_ref[...] = dot(x, wqkv_ref[:, 2 * D :]).astype(BF16)
    for s in range(seqs):
        rows = slice(s * block_len, (s + 1) * block_len)
        a = both[rows, :LANES] + both[rows, LANES:]
        v = v_ref[rows, :]
        top = jnp.max(a, axis=0, keepdims=True)
        w = jnp.exp(a - top)
        wx = dot_wide(w, expand)
        w = jnp.where(lane < 16, w, 0.0)
        packed += pltpu.roll(w, 16 * s, 1) if s else w
        vw = v.astype(F32) * wx
        vw_ref[rows, :] = vw.astype(BF16)
        t1, t2 = split2(top)
        t3 = (top - t1.astype(F32) - t2.astype(F32)).astype(BF16)
        tops = sum(dot(jnp.broadcast_to(t, (8, LANES)), expand) for t in (t1, t2, t3))
        msg_ref[s : s + 1, :] = tops[0:1, :]
        msg_ref[seqs + s : seqs + s + 1, :] = colsum(dec_r * vw)
        msg_ref[2 * seqs + s : 2 * seqs + s + 1, :] = colsum(dec_r * wx)
        msg_ref[3 * seqs + s : 3 * seqs + s + 1, :] = colsum(dec_f * vw)
        msg_ref[4 * seqs + s : 4 * seqs + s + 1, :] = colsum(dec_f * wx)
        offs_row = jnp.where(lane8 == s, sc_ref[4 + s].astype(F32), offs_row)
    msg_ref[MSG - 1 : MSG, :] = offs_row
    wx_ref[...] = packed


def local_kernel(seqs, block_len, slopes_ref, vw_ref, wx_ref, num_ref, den_ref):
    weighted = [vw_ref[s * block_len : (s + 1) * block_len, :] for s in range(seqs)]
    local_decay_sums(
        slopes_ref, weighted, wx_ref[...].astype(BF16), num_ref, den_ref, block_len, seqs
    )


def masked_kernel(others, seqs, block_len, rows_d, rows_f, low_count, top_bit, sc_ref, *refs):
    (flags_ref, msg_ref, *refs) = refs
    recv_refs, refs = refs[:others], refs[others:]
    (
        num_ref, den_ref, og_ref, wo_ref, vecs_ref, placex_ref, placey_ref, placed_ref,
        wgu_ref, wd_ref,
        as_ref, ak_ref, bs_ref, bk_ref,
        att_ref, invden_ref, dheads_ref, small_ref,
        wg_s, wu_s, wd_s, g_s, u_s, dk_s, ds_s, os_s, ok_s, lowx_s, lowy_s, mixed_s, d1_s, d2_s,
        acc_s, fn_s, in_sems, out_sems,
    ) = refs
    n = FF // CHUNK
    half = D // 2
    wide = CHUNK // 2
    me, z = sc_ref[0], sc_ref[1]
    tokens = seqs * block_len
    core = lax.shift_right_logical(me, top_bit) & 1
    plane = lax.shift_right_logical(me, top_bit + 1)

    def at(i):
        return pl.ds(pl.multiple_of(i * CHUNK, CHUNK), CHUNK)

    def loads(i):
        up_at = pl.ds(pl.multiple_of(FF + i * CHUNK, CHUNK), CHUNK)
        return [
            pltpu.make_async_copy(wgu_ref.at[:, at(i)], wg_s.at[i], in_sems.at[0, i]),
            pltpu.make_async_copy(wgu_ref.at[:, up_at], wu_s.at[i], in_sems.at[1, i]),
            pltpu.make_async_copy(wd_ref.at[at(i), :], wd_s.at[i], in_sems.at[2, i]),
        ]

    moves = gradient_moves(
        n, plane, (g_s, u_s, dk_s, ds_s, ok_s, os_s), (ak_ref, as_ref, bk_ref, bs_ref)
    )

    def stores(i, when):
        for k, (test, inside, outside) in enumerate(moves(i)):
            if test is not False:
                copy = pltpu.make_async_copy(inside, outside, out_sems.at[k, i])
                chosen(test, functools.partial(when, copy))

    out_copies = [
        pltpu.make_async_copy(inside, outside, out_sems.at[12, k])
        for k, (inside, outside) in enumerate(out_moves((ok_s, os_s), (bk_ref, bs_ref)))
    ]

    for i in range(n):
        for copy in loads(i):
            copy.start()

    slope_lane = vecs_ref[0:1, :]
    dec_f, dec_r = decay(slope_lane, block_len)
    invden = jnp.zeros((block_len, LANES), F32)
    for s in range(seqs):
        rows = slice(s * block_len, (s + 1) * block_len)

        def row(ref, kind):
            return ref[kind * seqs + s : kind * seqs + s + 1, :]

        own_off = lane_value(msg_ref[MSG - 1 : MSG, :], s)
        top = row(msg_ref, 0)
        for r in recv_refs:
            top = jnp.maximum(top, row(r, 0))
        own = jnp.exp(row(msg_ref, 0) - top)
        zero = jnp.zeros((1, D), F32)
        left_v, left_z, right_v, right_z = zero, zero, zero, zero
        for k, r in enumerate(recv_refs):
            gap = jnp.abs(lane_value(r[MSG - 1 : MSG, :], s) - own_off) - (block_len - 1.0)
            factor = jnp.exp(row(r, 0) - top - slope_lane * gap)
            is_left = (z ^ (k + 1)) < z
            f_left = jnp.where(is_left, factor, 0.0)
            f_right = jnp.where(is_left, 0.0, factor)
            left_v += f_left * row(r, 1)
            left_z += f_left * row(r, 2)
            right_v += f_right * row(r, 3)
            right_z += f_right * row(r, 4)
        den = own * dot_wide(den_ref[...], expand_seq(s)) + dec_f * left_z + dec_r * right_z
        num = own * num_ref[rows, :].astype(F32) + dec_f * left_v + dec_r * right_v
        inv = 1.0 / den
        invden = invden + dot_wide(inv * (1.0 / HD), reduce_seq(s))
        att_ref[rows, :] = (num * inv).astype(BF16)
    invden_ref[...] = invden
    rank = masked_ranks(flags_ref, seqs, tokens)
    small_ref[...] = jnp.zeros_like(small_ref)

    masked_tile(
        0, True, me, rows_d, rows_f, low_count, core, rank, att_ref, og_ref, wo_ref, vecs_ref,
        placex_ref, placey_ref, placed_ref, wg_s, wu_s, wd_s, g_s, u_s, dk_s, ds_s, os_s, ok_s,
        dheads_ref, small_ref, lowx_s, lowy_s, mixed_s, d1_s, d2_s, acc_s, fn_s, loads, stores,
    )
    for copy in out_copies:
        copy.start()
    for i in range(n):
        stores(i, lambda copy: copy.wait())
    for copy in out_copies:
        copy.wait()


SET_A = 4
B_ROWS_X = (FF // CHUNK - SET_A) * (D // 2) + FF // 4 + D // 2
B_ROWS_Y = (FF // CHUNK - SET_A) * (D // 2) + FF // 4


def chosen(test, work):
    if test is True:
        work()
    else:
        pl.when(test)(work)


def gradient_moves(n, plane, inside, outside):
    g_s, u_s, dk_s, ds_s, _ok, _os = inside
    ak_ref, as_ref, bk_ref, bs_ref = outside
    half, part = D // 2, CHUNK // 4
    b_x = (n - SET_A) * half

    def rows_at(first, size):
        return pl.ds(first if isinstance(first, int) else pl.multiple_of(first, 32), size)

    def moves(i):
        rel = i ^ plane
        x_rows = rows_at(b_x + swap_pair(rel) * part, part)
        y_rows = rows_at(B_ROWS_X + (n - SET_A) * half + rel * part, part)
        out = []
        for side, a_ref, b_ref, d in ((0, ak_ref, bk_ref, dk_s), (half, as_ref, bs_ref, ds_s)):
            rows = pl.ds(side, half)
            for value, a_first, b_first in (
                (g_s, 0, 0), (u_s, SET_A * half, B_ROWS_X)
            ):
                if isinstance(i, int):
                    at_a, at_b = min(i, SET_A - 1), max(i - SET_A, 0)
                else:
                    at_a, at_b = jnp.minimum(i, SET_A - 1), jnp.maximum(i - SET_A, 0)
                to_a = a_ref.at[rows_at(a_first + at_a * half, half)]
                to_b = b_ref.at[rows_at(b_first + at_b * half, half)]
                out.append((i < SET_A, value.at[i, rows], to_a))
                out.append((i >= SET_A, value.at[i, rows], to_b))
            out.append((True, d.at[i, pl.ds(0, part)], b_ref.at[x_rows]))
            out.append((True, d.at[i, pl.ds(part, part)], b_ref.at[y_rows]))
        return out

    return moves


def out_moves(inside, outside):
    rows = pl.ds(B_ROWS_X - D // 2, D // 2)
    return [(value, ref.at[rows]) for value, ref in zip(inside, outside)]


def masked_tile(
    t, first, me, rows_d, rows_f, low_count, core, rank, att_ref, og_ref, wo_ref, vecs_ref,
    placex_ref, placey_ref, placed_ref, wg_s, wu_s, wd_s, g_s, u_s, dk_s, ds_s, os_ref, ok_ref,
    dheads_ref, small_ref, lowx_s, lowy_s, mixed_s, d1_s, d2_s, acc_s, fn_s, loads, stores,
):
    n = FF // CHUNK
    half = D // 2
    wide = CHUNK // 2
    tokens = att_ref.shape[0]

    def put(ref, value):
        ref[...] = (value if first else ref[...].astype(F32) + value).astype(BF16)

    place = lax.broadcasted_iota(jnp.int32, (CAP, tokens), 0) + t * CAP
    comp = jnp.where(place.astype(F32) == rank, 1.0, 0.0).astype(BF16)
    att_low = (dot(comp, att_ref[...]) + vecs_ref[2:3, :]).astype(BF16)
    first_sum = vecs_ref[1:2, :] + (dot(att_low, wo_ref[...]) + vecs_ref[3:4, :])
    first_normed, first_scale = norm_rows(first_sum)
    fn_s[...] = first_normed
    low = (first_normed * vecs_ref[4:5, :] + vecs_ref[5:6, :]).astype(BF16)
    lowx_s[...] = dot(low, permuting(placex_ref[...], me, rows_d)).astype(BF16).T
    lowy_s[...] = dot(low, permuting(placey_ref[...], me, rows_d)).astype(BF16).T
    acc_s[...] = jnp.zeros((CAP, D), F32)

    def forward(i, c):
        for copy in loads(i):
            copy.wait()
        gate = dot(low, wg_s[i])
        up = dot(low, wu_s[i])
        phi = normal_cdf(gate)
        act = gate * phi
        mixed = (act * up).astype(BF16)
        mixed_s[i] = mixed
        d2_s[i] = act.astype(BF16)
        slope = phi + gate * (jnp.exp(-0.5 * gate * gate) * ((2.0 * math.pi) ** -0.5))
        d1_s[i] = (up * slope).astype(BF16)
        acc_s[...] += dot(mixed, wd_s[i])
        return c

    lax.fori_loop(0, n, forward, 0)
    first_out = fn_s[...] * vecs_ref[4:5, :] + vecs_ref[5:6, :]
    normed, scale = norm_rows(first_out + (acc_s[...] + vecs_ref[6:7, :]))
    up = dot(comp, og_ref[...])
    grad_second = norm_back(up, normed, scale, vecs_ref[7:8, :])
    acc_s[...] = grad_second
    bg = grad_second.astype(BF16)
    small_ref[0:1, :] += colsum(up * normed)
    small_ref[1:2, :] += colsum(up)
    small_ref[2:3, :] += colsum(bg.astype(F32))
    change_d = permuting(placed_ref[...], me & (low_count - 1), rows_f)

    def backward(i, c):
        mixed_grad = dot_nt(bg, wd_s[i]).astype(BF16).astype(F32)
        gate_grad = (mixed_grad * d1_s[i].astype(F32)).astype(BF16)
        up_grad = (mixed_grad * d2_s[i].astype(F32)).astype(BF16)
        put(g_s.at[i], dot(lowx_s[...], gate_grad))
        put(u_s.at[i], dot(lowy_s[...], up_grad))
        mixed = mixed_s[i]
        low_half, high_half = mixed[:, :wide], mixed[:, wide:]
        keep = jnp.where(core == 0, low_half, high_half)
        send = jnp.where(core == 0, high_half, low_half)
        put(dk_s.at[i], dot_tn(dot(keep, change_d).astype(BF16), bg))
        put(ds_s.at[i], dot_tn(dot(send, change_d).astype(BF16), bg))
        stores(i, lambda copy: copy.start())
        acc_s[...] += dot_nt(gate_grad, wg_s[i]) + dot_nt(up_grad, wu_s[i])
        return c

    lax.fori_loop(0, n, backward, 0)
    grad_first = acc_s[...]
    first_normed = fn_s[...]
    grad = norm_back(grad_first, first_normed, first_scale, vecs_ref[4:5, :])
    small_ref[3:4, :] += colsum(grad_first * first_normed)
    small_ref[4:5, :] += colsum(grad_first)
    attn_grad = grad.astype(BF16)
    small_ref[5:6, :] += colsum(attn_grad.astype(F32))
    small_ref[6:7, :] += colsum(grad)
    moved = dot(att_low, permuting(placex_ref[...], me, rows_d)).astype(BF16)
    grad_out = dot_tn(moved, attn_grad)
    put(ok_ref, grad_out[:half])
    put(os_ref, grad_out[half:])
    heads = dot_nt(attn_grad, wo_ref[...]).astype(BF16)
    small_ref[7:8, :] += colsum(heads.astype(F32))
    put(dheads_ref, dot_tn(comp, heads))


def masked_ranks(flags_ref, seqs, tokens):
    flags = jnp.concatenate([flags_ref[s : s + 1, :] for s in range(seqs)], axis=1).astype(F32)
    before = lax.broadcasted_iota(jnp.int32, (tokens, tokens), 0)
    after = lax.broadcasted_iota(jnp.int32, (tokens, tokens), 1)
    upper = jnp.where(before < after, 1.0, 0.0).astype(BF16)
    rank = dot(jnp.broadcast_to(flags, (8, tokens)).astype(BF16), upper)[0:1, :]
    return jnp.where(flags > 0.5, rank, -1.0)


def more_tiles_kernel(seqs, block_len, rows_d, rows_f, low_count, top_bit, sc_ref, *refs):
    held, (wgu_ref, wd_ref), grads, scratch = refs[:8], refs[8:10], refs[16:22], refs[22:]
    (
        flags_s, att_s, og_s, wo_s, vecs_s, placex_s, placey_s, placed_s, wg_s, wu_s, wd_s, g_s, u_s,
        dk_s, ds_s, os_s, ok_s, dheads_s, small_s, lowx_s, lowy_s, mixed_s, d1_s, d2_s, acc_s, fn_s,
        sem,
    ) = scratch
    as_ref, ak_ref, bs_ref, bk_ref, dheads_ref, small_ref = grads
    n = FF // CHUNK
    half = D // 2
    wide = CHUNK // 2
    me = sc_ref[0]
    core = lax.shift_right_logical(me, top_bit) & 1
    plane = lax.shift_right_logical(me, top_bit + 1)

    def move(source, target):
        copy = pltpu.make_async_copy(source, target, sem)
        copy.start()
        copy.wait()

    pairs = [(dheads_ref, dheads_s), (small_ref, small_s)]
    moves = gradient_moves(
        n, plane, (g_s, u_s, dk_s, ds_s, ok_s, os_s), (ak_ref, as_ref, bk_ref, bs_ref)
    )
    for i in range(n):
        pairs += [(outside, inside) for test, inside, outside in moves(i) if test is not False]
    pairs += [(o, i) for i, o in out_moves((ok_s, os_s), (bk_ref, bs_ref))]

    @pl.when(sc_ref[2] > 1)
    def _():
        for i in range(n):
            at = pl.ds(i * CHUNK, CHUNK)
            move(wgu_ref.at[:, at], wg_s.at[i])
            move(wgu_ref.at[:, pl.ds(FF + i * CHUNK, CHUNK)], wu_s.at[i])
            move(wd_ref.at[at, :], wd_s.at[i])
        for source, target in zip(held, scratch[:8]):
            move(source, target)
        for outside, inside in pairs:
            move(outside, inside)
        rank = masked_ranks(flags_s, seqs, seqs * block_len)

        def tile(t, carry):
            masked_tile(
                t, False, me, rows_d, rows_f, low_count, core, rank, att_s, og_s, wo_s, vecs_s,
                placex_s, placey_s, placed_s, wg_s, wu_s, wd_s, g_s, u_s, dk_s, ds_s, os_s, ok_s,
                dheads_s, small_s, lowx_s, lowy_s, mixed_s, d1_s, d2_s, acc_s, fn_s,
                lambda i: [], lambda i, when: None,
            )
            return carry

        lax.fori_loop(1, sc_ref[2], tile, 0)
        for outside, inside in pairs:
            move(inside, outside)


def inner_kernel(
    seqs, block_len, slopes_ref, dheads_ref, att_ref, invden_ref, vecs_ref, uv_ref, ud_ref, msg_ref
):
    slope_lane = vecs_ref[0:1, :]
    dec_f, dec_r = decay(slope_lane, block_len)
    wide = []
    packed = jnp.zeros((block_len, LANES), F32)
    msg_ref[...] = jnp.zeros_like(msg_ref)
    for s in range(seqs):
        rows = slice(s * block_len, (s + 1) * block_len)
        dheads = dheads_ref[rows, :].astype(F32)
        expand = expand_seq(s)
        inner = dot_wide(dheads * att_ref[rows, :].astype(F32), reduce_seq(s)) * invden_ref[...]
        packed += inner
        yv = dheads * dot_wide(invden_ref[...], expand)
        yd = dot_wide(inner, expand)
        wide.append(yv.astype(BF16))
        msg_ref[s : s + 1, :] = colsum(dec_r * yv)
        msg_ref[seqs + s : seqs + s + 1, :] = colsum(dec_r * yd)
        msg_ref[2 * seqs + s : 2 * seqs + s + 1, :] = colsum(dec_f * yv)
        msg_ref[3 * seqs + s : 3 * seqs + s + 1, :] = colsum(dec_f * yd)
    local_decay_sums(slopes_ref, wide, packed.astype(BF16), uv_ref, ud_ref, block_len, seqs)


def value_kernel(others, seqs, block_len, rows_d, sc_ref, *refs):
    (flags_ref, msg1_ref, msg2_ref, *refs) = refs
    recv1, recv2, refs = refs[:others], refs[others : 2 * others], refs[2 * others :]
    (
        uv_ref, ud_ref, wx_ref, v_ref, x_ref, wqkv_ref, g_ref, vecs_ref, placey_ref, smalla_ref,
        ig_ref, vs_ref, vk_ref, small_ref, dv_s, t_s,
    ) = refs
    me, z = sc_ref[0], sc_ref[1]
    slope_lane = vecs_ref[0:1, :]
    dec_f, dec_r = decay(slope_lane, block_len)
    reduce = reduce_one()
    embed = smalla_ref[6:7, :]
    half = D // 2
    for s in range(seqs):
        rows = slice(s * block_len, (s + 1) * block_len)

        def row(ref, kind):
            return ref[kind * seqs + s : kind * seqs + s + 1, :]

        own_off = lane_value(msg1_ref[MSG - 1 : MSG, :], s)
        top = row(msg1_ref, 0)
        for r in recv1:
            top = jnp.maximum(top, row(r, 0))
        own = jnp.exp(row(msg1_ref, 0) - top)
        zero = jnp.zeros((1, D), F32)
        left_v, left_d, right_v, right_d = zero, zero, zero, zero
        for k, (r1, r2) in enumerate(zip(recv1, recv2)):
            gap = jnp.abs(lane_value(r1[MSG - 1 : MSG, :], s) - own_off) - (block_len - 1.0)
            factor = jnp.exp(-slope_lane * gap)
            is_left = (z ^ (k + 1)) < z
            f_left = jnp.where(is_left, factor, 0.0)
            f_right = jnp.where(is_left, 0.0, factor)
            left_v += f_left * row(r2, 0)
            left_d += f_left * row(r2, 1)
            right_v += f_right * row(r2, 2)
            right_d += f_right * row(r2, 3)
        expand = expand_seq(s)
        weight = dot_wide(wx_ref[...], expand) * own
        uv = weight * (uv_ref[rows, :].astype(F32) + dec_f * left_v + dec_r * right_v)
        ud = weight * (dot_wide(ud_ref[...], expand) + dec_f * left_d + dec_r * right_d)
        dv = uv.astype(BF16)
        dv_s[rows, :] = dv
        t = dot_wide(uv * v_ref[rows, :].astype(F32) - ud * (1.0 / HD), reduce)
        t_s[rows, :] = t
    dx = dot_nt(dv_s[...], wqkv_ref[:, 2 * D :]) + dot_nt(t_s[...].astype(BF16), g_ref[...])
    masked = jnp.broadcast_to(flags_ref[:, 0:1], dx.shape) > 0.5
    ig_ref[...] = jnp.where(masked, 0.0, dx).astype(BF16)
    embed += colsum(jnp.where(masked, dx, 0.0))
    x = x_ref[...]
    xp = dot(x, permuting(placey_ref[...], me, rows_d)).astype(BF16)
    gv = dot_tn(xp, dv_s[...]).astype(BF16)
    vk_ref[...] = gv[:half]
    vs_ref[0:half, :] = gv[half:]
    t_high, t_rest = split2(t_s[...])
    a_t = (dot_tn(t_high, x) + dot_tn(t_rest, x))[0:16, :]
    both = dot_wide(a_t, wqkv_ref[:, D : 2 * D]) * (HD**-0.5)
    head = lax.broadcasted_iota(jnp.int32, (16, D), 0)
    lane = lax.broadcasted_iota(jnp.int32, (16, D), 1)
    query = colsum(jnp.where(lax.shift_right_logical(lane, 6) == head, both, 0.0))
    q_high, q_rest = split2(jnp.broadcast_to(query, (8, D)))
    wq = wqkv_ref[:, 0:D]
    embed += (dot_nt(q_high, wq) + dot_nt(q_rest, wq))[0:1, :]
    small_ref[0:8, :] = smalla_ref[...]
    small_ref[6:7, :] = embed
    small_ref[8:24, :] = a_t
    small_ref[20:21, :] = query
    put_small(vs_ref, half, small_ref[...])


FEATS = 6
LOG2E = math.log2(math.e)


def attention_kernel(start, spec, slopes_ref, sc_ref, q_ref, own_ref, wk_ref, wv_ref, *refs):
    others = len(spec)
    count = sum(len(group) for group in spec)
    part_refs, msg_refs, (msg_ref, vecs_ref, out_ref, k_s, v_s) = (
        refs[:count], refs[count : count + others], refs[count + others :],
    )
    s = start + pl.program_id(0)
    block_len = q_ref.shape[0]
    z = sc_ref[1]
    lane = lax.broadcasted_iota(jnp.int32, (block_len, LANES), 1)
    token = lax.broadcasted_iota(jnp.int32, (block_len, LANES), 0).astype(F32)
    head_of = lane // FEATS
    kind = lane - head_of * FEATS
    row = lax.broadcasted_iota(jnp.int32, (block_len, block_len), 0)
    col = lax.broadcasted_iota(jnp.int32, (block_len, block_len), 1)
    apart = jnp.abs(row - col).astype(F32) * LOG2E
    qvalue = jnp.where(kind < 3, token, 1.0)

    rows = []
    for k in range(others):
        parts = [part_refs[at][...] for at in spec[k]]
        x = parts[0]
        if len(parts) == 2:
            x = jnp.where((z == 1) | (z == 2), parts[0], parts[1])
        rows.append(x)
    x = jnp.concatenate(rows, axis=0)
    k_s[...] = dot(x, wk_ref[...]).astype(BF16)
    v_s[...] = dot(x, wv_ref[...]).astype(BF16)

    slope = jnp.zeros((1, LANES), F32)
    lane1 = lax.broadcasted_iota(jnp.int32, (1, LANES), 1)
    for h in range(H):
        slope = jnp.where(lane1 // FEATS == h, slopes_ref[h] * LOG2E, slope)
    kind1 = lane1 - (lane1 // FEATS) * FEATS
    own_off = lane_value(msg_ref[MSG - 1 : MSG, :], s)
    feats = []
    for k in range(others):
        gap = jnp.abs(lane_value(msg_refs[k][MSG - 1 : MSG, :], s) - own_off)
        sign = jnp.where((z ^ (k + 1)) < z, 1.0, -1.0)
        value = jnp.where(kind1 < 3, -sign * slope, slope * (sign * token - gap))
        p1 = value.astype(BF16).astype(F32)
        p2 = (value - p1).astype(BF16).astype(F32)
        p3 = value - p1 - p2
        part = jnp.where(kind1 % 3 == 0, p1, jnp.where(kind1 % 3 == 1, p2, p3))
        feats.append(part.astype(BF16))
    ones = jnp.ones((block_len, LANES), BF16)
    zero = jnp.zeros((), BF16)
    for pair in range(H // 2):
        low, high = pair * LANES, (pair + 1) * LANES
        q = q_ref[:, low:high]
        block = lambda ref, k: ref[k * block_len : (k + 1) * block_len, low:high]
        qh = jnp.concatenate([jnp.where(lane < HD, q, zero), jnp.where(lane < HD, zero, q)], axis=0)
        qfeat = jnp.concatenate(
            [jnp.where(head_of == 2 * pair + e, qvalue, 0.0).astype(BF16) for e in range(2)], axis=0
        )
        qf = jnp.concatenate([qh, qfeat], axis=1)
        bias = jnp.concatenate([apart * slopes_ref[2 * pair + e] for e in range(2)], axis=0)
        scores = [dot_nt(qh, own_ref[:, low:high]) - bias]
        for k in range(others):
            scores.append(dot_nt(qf, jnp.concatenate([block(k_s, k), feats[k]], axis=1)))
        top = scores[0]
        for sc in scores[1:]:
            top = jnp.maximum(top, sc)
        top = jnp.max(top, axis=1, keepdims=True)
        values = [own_ref[:, D + low : D + high]] + [block(v_s, k) for k in range(others)]
        total = None
        for sc, value in zip(scores, values):
            part = dot(jnp.exp2(sc - top).astype(BF16), jnp.concatenate([value, ones], axis=1))
            total = part if total is None else total + part
        out = total[:, :LANES] / total[:, LANES:]
        out_ref[:, low:high] = (
            jnp.where(lane < HD, out[:block_len], out[block_len:]) + vecs_ref[2:3, low:high]
        ).astype(BF16)


def dense_kernel(into, x_ref, att_ref, wo_ref, vecs_ref, wg_ref, wu_ref, wd_ref, *refs):
    out_ref, fo_s, low_s, acc_s = refs[1:] if into else refs
    step = pl.program_id(0)

    @pl.when(step == 0)
    def _():
        first_sum = x_ref[...].astype(F32) + (dot(att_ref[...], wo_ref[...]) + vecs_ref[3:4, :])
        normed, _scale = norm_rows(first_sum)
        first_out = normed * vecs_ref[4:5, :] + vecs_ref[5:6, :]
        fo_s[...] = first_out
        low_s[...] = first_out.astype(BF16)
        acc_s[...] = jnp.zeros_like(acc_s)

    low = low_s[...]
    gate = dot(low, wg_ref[...])
    up = dot(low, wu_ref[...])
    mixed = (gate * normal_cdf(gate) * up).astype(BF16)
    acc_s[...] += dot(mixed, wd_ref[...])

    @pl.when(step == pl.num_programs(0) - 1)
    def _():
        normed, _scale = norm_rows(fo_s[...] + (acc_s[...] + vecs_ref[6:7, :]))
        out_ref[...] = (normed * vecs_ref[7:8, :] + vecs_ref[8:9, :]).astype(BF16)


def put_small(ref, at, small):
    high, rest = split2(small)
    ref[at : at + SMALL, :] = high
    ref[at + SMALL : at + 2 * SMALL, :] = rest


def get_small(ref, at):
    return ref[at : at + SMALL, :].astype(F32) + ref[at + SMALL : at + 2 * SMALL, :].astype(F32)


def add_rows_kernel(spec, join, *refs):
    count = len(spec)
    arrays, refs = refs[: 2 * count], refs[2 * count :]
    kept, sent = [], []
    for at, ((first, got_first), segments) in enumerate(spec):
        keep, got = arrays[2 * at : 2 * at + 2]
        rows = sum(segments)
        total = keep[first : first + rows, :].astype(F32)
        total += got[got_first : got_first + rows, :].astype(F32)
        one, two = halves(total, segments)
        kept.append(one)
        sent.append(two)
    small = None
    if len(refs) == 2 * len(join) + 2:
        small_ref, refs = refs[0], refs[1:]
        got = arrays[-1]
        top = got.shape[0] - 2 * SMALL
        small = (
            small_ref[...] + got[top : top + SMALL, :].astype(F32)
            + got[top + SMALL : top + 2 * SMALL, :].astype(F32)
        )
        refs[-1][...] = small
    for at, group in enumerate(join):
        keep_out, send_out = refs[2 * at : 2 * at + 2]
        keep_out[...] = jnp.concatenate([kept[k] for k in group], axis=0).astype(BF16)
        sending = jnp.concatenate([sent[k] for k in group], axis=0).astype(BF16)
        rows = sending.shape[0]
        send_out[0:rows, :] = sending
        if small is not None and at == len(join) - 1:
            high, rest = split2(small)
            send_out[rows : rows + SMALL, :] = high
            send_out[rows + SMALL : rows + 2 * SMALL, :] = rest


def add_rows(pieces, join, name, small=None):
    spec = [(first, tuple(segments)) for _k, _r, first, segments in pieces]
    arrays = [v for keep, got, _f, _s in pieces for v in (keep, got)]
    halved = [sum(segments) // 2 for _f, segments in spec]
    sizes = [sum(halved[k] for k in group) for group in join]
    if any(rows % 16 for _f, segments in spec for rows in segments):
        return add_rows_plain(pieces, join, small)
    cut = 2 if sum(sizes) > 1024 else 1
    col = lambda rows: pl.BlockSpec((rows, D // cut), lambda i: (0, i))
    outs = []
    for at, size in enumerate(sizes):
        more = 2 * SMALL if small is not None and at == len(sizes) - 1 else 0
        outs += [size, size + more]
    shapes = [jax.ShapeDtypeStruct((rows, D), BF16) for rows in outs]
    specs = [col(rows) for rows in outs]
    if small is not None:
        arrays.append(small)
        shapes.append(jax.ShapeDtypeStruct((SMALL, D), F32))
        specs.append(col(SMALL))
    return pl.pallas_call(
        functools.partial(add_rows_kernel, spec, join),
        name=name,
        grid=(cut,),
        out_shape=shapes,
        in_specs=[col(v.shape[0]) for v in arrays],
        out_specs=specs,
        compiler_params=params(),
        cost_estimate=cost(0.1),
    )(*arrays)


def add_rows_plain(pieces, join, small):
    kept, sent = [], []
    for keep, got, (first, got_first), segments in pieces:
        rows = sum(segments)
        total = keep[first : first + rows].astype(F32) + got[got_first : got_first + rows].astype(F32)
        one, two = halves(total.astype(BF16), segments)
        kept.append(one)
        sent.append(two)
    outs = []
    for at, group in enumerate(join):
        outs.append(jnp.concatenate([kept[k] for k in group], axis=0))
        send = [sent[k] for k in group]
        if small is not None and at == len(join) - 1:
            tail = pieces[-1][1][-2 * SMALL :].astype(F32)
            small = small + tail[:SMALL] + tail[SMALL:]
            send += list(split2(small))
        outs.append(jnp.concatenate(send, axis=0))
    return outs + ([small] if small is not None else [])


def add_small_kernel(keep, small, got, keep_out, send_out, small_out):
    half = keep.shape[0] // 2
    total = keep[...].astype(F32) + got[0 : 2 * half, :].astype(F32)
    keep_out[...] = total[:half].astype(BF16)
    send_out[0:half, :] = total[half:].astype(BF16)
    both = small[...] + get_small(got, 2 * half)
    small_out[...] = both
    put_small(send_out, half, both)


def add_small(keep, small, got, name):
    rows = keep.shape[0] // 2
    full = lambda shape: pl.BlockSpec(shape, lambda i: (0, 0))
    outs = [(rows, D), (rows + 2 * SMALL, D), (SMALL, D)]
    return pl.pallas_call(
        add_small_kernel,
        name=name,
        grid=(1,),
        out_shape=[
            jax.ShapeDtypeStruct(o, t) for o, t in zip(outs, (BF16, BF16, F32))
        ],
        in_specs=[full(v.shape) for v in (keep, small, got)],
        out_specs=[full(o) for o in outs],
        compiler_params=params(),
        cost_estimate=cost(0.1),
    )(keep, small, got)


def finish_kernel(
    rows_f, rows_d, sc_ref, a_k, a_r, b_k, b_r, small_ref, vecs_ref, qm_ref,
    gateup_ref, down_ref, out_ref, qkv_ref, *vector_refs,
):
    rows_a = a_k.shape[0]
    a_total = a_k[...].astype(F32) + a_r[0:rows_a, :].astype(F32)
    b_total = b_k[...].astype(F32) + b_r[...].astype(F32)
    gateup, down, out, value = unpack(a_total, b_total, rows_f, rows_d)
    for at, part in enumerate(gateup):
        gateup_ref[:, at * CHUNK : (at + 1) * CHUNK] = part
    down_ref[...] = down
    out_ref[...] = out
    small = (
        small_ref[...] + a_r[rows_a : rows_a + SMALL, :].astype(F32)
        + a_r[rows_a + SMALL : rows_a + 2 * SMALL, :].astype(F32)
    )
    row = lax.broadcasted_iota(jnp.int32, (D, LANES), 0)
    lane = lax.broadcasted_iota(jnp.int32, (D, LANES), 1)
    pick = jnp.where((row == lane + sc_ref[0] * rows_d) & (lane < rows_d), 1.0, 0.0).astype(BF16)
    both = jnp.concatenate([small, jnp.broadcast_to(vecs_ref[1:2, :], (8, D))], axis=0)
    p1 = both.astype(BF16)
    p2 = (both - p1.astype(F32)).astype(BF16)
    p3 = (both - p1.astype(F32) - p2.astype(F32)).astype(BF16)
    mine = dot(p1, pick) + dot(p2, pick) + dot(p3, pick)
    for ref, at in zip(vector_refs, SMALL_ROWS):
        ref[...] = mine[at : at + 1, 0:rows_d].reshape(rows_d)
    columns = mine.T
    emb = jnp.broadcast_to(columns[0:rows_d, SMALL : SMALL + 1], (rows_d, D))
    qkv_ref[:, 0:D] = emb * small[20:21, :]
    heads = columns[:, 8 : 8 + 16]
    key = jnp.concatenate(
        [jnp.broadcast_to(heads[0:rows_d, h : h + 1], (rows_d, HD)) for h in range(H)], axis=1
    )
    qkv_ref[:, D : 2 * D] = key * (qm_ref[0:1, :] * (HD**-0.5))
    qkv_ref[:, 2 * D :] = value


SMALL_ROWS = (6, 20, 7, 5, 3, 4, 2, 0, 1)


def unpack(a_total, b_total, rows_f, rows_d):
    n, part = FF // CHUNK, rows_f // 2
    a = [a_total[k * rows_d : (k + 1) * rows_d] for k in range(2 * n + 1)]
    down = jnp.concatenate([b_total[:part], b_total[part + rows_d :]], axis=0)
    return a[: 2 * n], down, b_total[part : part + rows_d], a[2 * n]


def finish(scalars, a_k, a_r, b_k, b_r, small, vecs, qm, rows_f, rows_d):
    outs = [(rows_d, 2 * FF), (rows_f, D), (rows_d, D), (rows_d, 3 * D)] + [(rows_d,)] * 9
    if rows_d % 8:
        rows_a = a_k.shape[0]
        gateup, down, out, value = unpack(
            a_k.astype(F32) + a_r[:rows_a].astype(F32), b_k.astype(F32) + b_r.astype(F32), rows_f,
            rows_d,
        )
        small = small + a_r[rows_a : rows_a + SMALL].astype(F32) + a_r[rows_a + SMALL :].astype(F32)
        mine = lax.dynamic_slice_in_dim(small, scalars[0] * rows_d, rows_d, 1)
        emb = lax.dynamic_slice_in_dim(vecs[1], scalars[0] * rows_d, rows_d, 0)
        key = jnp.repeat(mine[8 : 8 + H].T, HD, axis=1) * (qm[0:1, :] * (HD**-0.5))
        qkv = jnp.concatenate([emb[:, None] * small[20][None, :], key, value], axis=1)
        return [jnp.concatenate(gateup, axis=1), down, out, qkv] + [mine[k] for k in SMALL_ROWS]
    full = lambda shape: pl.BlockSpec(shape, lambda i: (0,) * len(shape))
    arrays = (a_k, a_r, b_k, b_r, small, vecs, qm)
    return pl.pallas_call(
        functools.partial(finish_kernel, rows_f, rows_d),
        name="finish",
        grid=(1,),
        out_shape=[jax.ShapeDtypeStruct(o, F32) for o in outs],
        in_specs=[smem()] + [full(v.shape) for v in arrays],
        out_specs=[full(o) for o in outs],
        compiler_params=params(),
        cost_estimate=cost(1),
    )(scalars, *arrays)


def halves(total, segments):
    first, second, at = [], [], 0
    for rows in segments:
        first.append(total[at : at + rows // 2])
        second.append(total[at + rows // 2 : at + rows])
        at += rows
    return jnp.concatenate(first, axis=0), jnp.concatenate(second, axis=0)


def bit_orders(batch, blocks):
    n = int(math.log2(batch * blocks))
    seq_bits = int(math.log2(blocks))
    rest = list(range(seq_bits, n - 3)) + list(range(seq_bits))
    top = [n - 3, n - 2, n - 1]
    return [*top, *rest], [top[0], top[2], top[1], *rest], rest


def places(order, rows, parts=1):
    n = len(order)
    place = np.arange(2**n)
    rel = np.zeros(2**n, np.int32)
    for k, bit in enumerate(order):
        rel |= ((place >> (n - 1 - k)) & 1).astype(np.int32) << bit
    out = np.zeros((8, 2**n * rows), np.int32)
    size = rows // parts
    out[0] = np.tile(np.repeat(rel, size), parts)
    out[1] = np.concatenate([np.tile(np.arange(size) + p * size, 2**n) for p in range(parts)])
    return out


def swap_pair(i):
    return (i & 1) * 2 + lax.shift_right_logical(i, 1)


def smem():
    return pl.BlockSpec(memory_space=pltpu.SMEM)


def masked_rows(
    batch, blocks, scalars, mask_flags, msg1, recv1, num, den, grad, out_weight, vecs,
    gate_up_weight, down_weight,
):
    seqs, block_len = mask_flags.shape
    tokens = seqs * block_len
    shards = batch * blocks
    others = blocks - 1
    n = FF // CHUNK
    half = D // 2
    order_x, order_y, order_rest = bit_orders(batch, blocks)
    top_bit = len(order_x) - 3
    vmem, hbm = pl.BlockSpec(memory_space=pltpu.VMEM), pl.BlockSpec(memory_space=pl.ANY)
    bf_full = jax.ShapeDtypeStruct((tokens, D), BF16)
    set_a = jax.ShapeDtypeStruct((2 * SET_A * half, D), BF16)
    set_b = jax.ShapeDtypeStruct((B_ROWS_X + B_ROWS_Y, D), BF16)
    chunks = lambda rows, width: pltpu.VMEM((n, rows, width), BF16)
    grads = [set_a] * 2 + [set_b] * 2
    square_s = pltpu.VMEM((half, D), BF16)
    weights_s = [
        chunks(D, CHUNK), chunks(D, CHUNK), chunks(CHUNK, D), chunks(D, CHUNK), chunks(D, CHUNK),
        chunks(CHUNK // 2, D), chunks(CHUNK // 2, D),
    ]
    tile_s = [
        pltpu.VMEM((D, CAP), BF16), pltpu.VMEM((D, CAP), BF16), chunks(CAP, CHUNK),
        chunks(CAP, CHUNK), chunks(CAP, CHUNK), pltpu.VMEM((CAP, D), F32), pltpu.VMEM((CAP, D), F32),
    ]
    held = [
        places(order_x, D // shards), places(order_y, D // shards),
        places(order_rest, FF // shards, 2),
    ]
    small = jax.ShapeDtypeStruct((8, D), F32)
    packed = jax.ShapeDtypeStruct((block_len, LANES), F32)
    *sums, att, invden, dheads, small_sums = pl.pallas_call(
        functools.partial(
            masked_kernel, others, seqs, block_len, D // shards, FF // shards, shards // 8, top_bit
        ),
        name="masked_rows",
        out_shape=grads + [bf_full, packed, bf_full, small],
        in_specs=[smem()] + [vmem] * (10 + len(recv1)) + [hbm] * 2,
        out_specs=[hbm] * 4 + [vmem] * 4,
        scratch_shapes=weights_s + [square_s, square_s] + tile_s
        + [pltpu.SemaphoreType.DMA((3, n)), pltpu.SemaphoreType.DMA((13, n))],
        compiler_params=params(62),
        cost_estimate=cost(60),
    )(
        scalars, mask_flags, msg1, *recv1, num, den, grad, out_weight, vecs, *held, gate_up_weight,
        down_weight,
    )
    *sums, dheads, small_sums = pl.pallas_call(
        functools.partial(
            more_tiles_kernel, seqs, block_len, D // shards, FF // shards, shards // 8, top_bit
        ),
        name="more_masked_rows",
        out_shape=grads + [bf_full, small],
        in_specs=[smem()] + [hbm] * 16,
        out_specs=[hbm] * 6,
        input_output_aliases={11 + k: k for k in range(6)},
        scratch_shapes=[
            pltpu.VMEM(mask_flags.shape, jnp.int32), pltpu.VMEM((tokens, D), BF16),
            pltpu.VMEM((tokens, D), BF16), pltpu.VMEM((D, D), BF16), pltpu.VMEM((16, D), F32),
        ]
        + [pltpu.VMEM(h.shape, jnp.int32) for h in held]
        + weights_s
        + [square_s, square_s, pltpu.VMEM((tokens, D), BF16), pltpu.VMEM((8, D), F32)]
        + tile_s
        + [pltpu.SemaphoreType.DMA],
        compiler_params=params(62),
        cost_estimate=cost(1),
    )(
        scalars, mask_flags, att, grad, out_weight, vecs, *held, gate_up_weight, down_weight, *sums,
        dheads, small_sums,
    )
    return (*sums, att, invden, dheads, small_sums)


def on_device(
    hidden_states, mask_flags, block_offsets, alibi_slopes, mask_embedding, qkv_weight, query_bias,
    value_bias, out_weight, out_bias, first_gain, first_shift, gate_up_weight, down_weight,
    down_bias, second_gain, second_shift, output_grad,
):
    seqs, block_len = mask_flags.shape
    tokens = seqs * block_len
    batch, blocks = lax.axis_size("batch"), lax.axis_size("seq")
    shards = batch * blocks
    z = lax.axis_index("seq")
    me = lax.axis_index("batch") * blocks + z
    order_x, order_y, order_rest = bit_orders(batch, blocks)
    seq_bits = int(math.log2(blocks))
    place_y = places(order_y, D // shards)
    top_bit = len(order_x) - 3
    n = FF // CHUNK
    half = D // 2
    square = jax.ShapeDtypeStruct((half, D), BF16)
    others = blocks - 1
    vmem = pl.BlockSpec(memory_space=pltpu.VMEM)
    packed = jax.ShapeDtypeStruct((block_len, LANES), F32)
    bf_full = jax.ShapeDtypeStruct((tokens, D), BF16)
    last = [()]

    def after(*values):
        tied = lax.optimization_barrier((values, last[0]))[0]
        return tied if len(values) > 1 else tied[0]

    def done(value):
        last[0] = value

    def along(value, axis, pairs):
        return lax.ppermute(value, axis, pairs)

    def flip(value, bit):
        if bit >= seq_bits:
            axis, size, mask = "batch", batch, 1 << (bit - seq_bits)
        else:
            axis, size, mask = "seq", blocks, 1 << bit
        return along(value, axis, [(i, i ^ mask) for i in range(size)])

    fixed = lambda shape: pl.BlockSpec(shape, lambda i: (0,) * len(shape))
    x, vecs, flagx, scalars = pl.pallas_call(
        functools.partial(inputs_kernel, seqs, block_len, blocks),
        name="inputs",
        grid=(1,),
        out_shape=(
            bf_full, jax.ShapeDtypeStruct((16, D), F32), jax.ShapeDtypeStruct((tokens, LANES), F32),
            jax.ShapeDtypeStruct((8,), jnp.int32),
        ),
        in_specs=[smem(), smem(), fixed((tokens, D)), fixed((seqs, block_len))] + [fixed((D,))] * 9,
        out_specs=[
            fixed((tokens, D)), fixed((16, D)), fixed((tokens, LANES)), smem(),
        ],
        compiler_params=params(),
        cost_estimate=cost(1),
    )(
        alibi_slopes, block_offsets.reshape(1, seqs), hidden_states.reshape(tokens, D), mask_flags,
        mask_embedding, value_bias, out_bias, first_gain, first_shift, down_bias, second_gain,
        second_shift, query_bias,
    )

    near = [(i, i ^ 1) for i in range(blocks)]
    hops = blocks == 4

    def centre(value):
        pairs = []
        for b in range(batch):
            for at in range(blocks):
                to = b * blocks + 3 - at if at in (1, 2) else (b ^ 1) * blocks + at
                pairs.append((b * blocks + at, to))
        return along(value, ("batch", "seq"), pairs)

    def held(*values):
        values = after(*values)
        done(values)
        return values

    v, vw, wx, msg1, g, qm = pl.pallas_call(
        functools.partial(prep_kernel, seqs, block_len),
        name="masked_prep",
        out_shape=(
            bf_full, bf_full, packed, jax.ShapeDtypeStruct((MSG, D), F32),
            jax.ShapeDtypeStruct((D, LANES), BF16), jax.ShapeDtypeStruct((8, D), F32),
        ),
        in_specs=[smem(), smem()] + [vmem] * 3,
        out_specs=[vmem] * 6,
        compiler_params=params(),
        cost_estimate=cost(10),
    )(alibi_slopes, scalars, x, qkv_weight, vecs)
    done(msg1)
    recv1 = [along(msg1, "seq", [(i, i ^ k) for i in range(blocks)]) for k in range(1, blocks)]

    num, den = pl.pallas_call(
        functools.partial(local_kernel, seqs, block_len),
        name="masked_local",
        out_shape=(bf_full, packed),
        in_specs=[smem(), vmem, vmem],
        out_specs=[vmem] * 2,
        compiler_params=params(),
        cost_estimate=cost(0.1),
    )(alibi_slopes, after(vw), wx)
    done(num)
    recv1 = list(held(*recv1, msg1))[:-1]
    x_late = after(x)
    if hops:
        round1 = along(x_late, "seq", near), centre(x_late)
    else:
        round1 = tuple(
            along(x_late, "seq", [(i, i ^ k) for i in range(blocks)]) for k in range(1, blocks)
        )

    a_s, a_k, b_s, b_k, att_m, invden, dheads, small_a = masked_rows(
        batch, blocks, scalars, mask_flags, msg1, recv1, num, den,
        after(output_grad.reshape(tokens, D)), out_weight, vecs, gate_up_weight, down_weight,
    )
    done(small_a)
    round1 = held(*round1)
    if hops:
        round2 = along(round1[1], "seq", near), centre(round1[0])
    b_r, a_r = flip(b_s, order_x[0]), flip(a_s, order_x[0])

    uv, ud, msg2 = pl.pallas_call(
        functools.partial(inner_kernel, seqs, block_len),
        name="masked_inner",
        out_shape=(bf_full, packed, jax.ShapeDtypeStruct((MSG, D), F32)),
        in_specs=[smem()] + [vmem] * 4,
        out_specs=[vmem] * 3,
        compiler_params=params(),
        cost_estimate=cost(60),
    )(alibi_slopes, after(dheads), att_m, invden, vecs)
    done(msg2)

    q_own = project(after(x), qkv_weight, vecs, 0, 1, LOG2E * HD**-0.5)
    done(q_own)
    rows_a = SET_A * half
    seg_a = [[half] * SET_A] * 2
    more = n - SET_A
    seg_b = [[half] * more + [FF // 4, half], [half] * more + [FF // 4]]
    cut_in_half = lambda groups: [[rows // 2 for rows in group] for group in groups]
    b_k, b_r = after(b_k, b_r)
    bx_k, bx_s, by_k, by_s = add_rows(
        [(b_k, b_r, (0, 0), seg_b[0]), (b_k, b_r, (B_ROWS_X, B_ROWS_X), seg_b[1])], [[0], [1]], "add_core_b"
    )
    done(bx_k)
    bx_r, by_r = flip(bx_s, order_x[1]), flip(by_s, order_y[1])
    a_k, a_r = after(a_k, a_r)
    ax_k, ax_s, ay_k, ay_s = add_rows(
        [(a_k, a_r, (0, 0), seg_a[0]), (a_k, a_r, (rows_a, rows_a), seg_a[1])], [[0], [1]], "add_core_a"
    )
    done(ax_k)
    seg_a, seg_b = cut_in_half(seg_a), cut_in_half(seg_b)
    if hops:
        round2 = held(*round2)
    msg2_now = after(msg2)
    recv2 = [along(msg2_now, "seq", [(i, i ^ k) for i in range(blocks)]) for k in range(1, blocks)]
    kv_own = project(after(x), qkv_weight, vecs, 1, 2)
    done(kv_own)
    recv2 = list(held(*recv2, msg2))[:-1]
    ax_r, ay_r = flip(after(ax_s), order_x[1]), flip(after(ay_s), order_y[1])
    if hops:
        far = along(after(round2[1]), "seq", near)

    input_grad, value_s, value_k, small = pl.pallas_call(
        functools.partial(value_kernel, others, seqs, block_len, D // shards),
        name="value_grads",
        out_shape=(
            bf_full, jax.ShapeDtypeStruct((2 * SMALL + half, D), BF16),
            jax.ShapeDtypeStruct((half, D), BF16), jax.ShapeDtypeStruct((SMALL, D), F32),
        ),
        in_specs=[smem()] + [vmem] * (13 + len(recv1) + len(recv2)),
        out_specs=[vmem] * 4,
        scratch_shapes=[pltpu.VMEM((tokens, D), BF16), pltpu.VMEM((tokens, LANES), F32)],
        compiler_params=params(),
        cost_estimate=cost(60),
    )(
        scalars, flagx, msg1, msg2, *recv1, *recv2, uv, ud, wx, v, after(x), qkv_weight, g, vecs,
        place_y, small_a,
    )
    done(small)
    bx_r, by_r = held(bx_r, by_r)
    value_r = flip(after(value_s), order_y[0])
    bx_k, by_k = after(bx_k, by_k)
    bx_k, bx_s, by_k, by_s = add_rows(
        [(bx_k, bx_r, (0, 0), seg_b[0]), (by_k, by_r, (0, 0), seg_b[1])], [[0], [1]], "add_xy_b"
    )
    done(bx_k)
    value_k, value_s, small = add_small(*after(value_k, small, value_r), "add_core_value")
    done(small)
    bx_r, by_r = flip(after(bx_s), order_x[2]), flip(after(by_s), order_y[2])
    seg_b = cut_in_half(seg_b)
    if hops:
        far, _ = held(far, small)
    if hops:
        groups = [
            [round1[0]], [round2[1], round2[0]], [round1[1], far],
        ]
    else:
        groups = [[part] for part in round1]

    def attend(start, count, micros):
        block = lambda width=D: pl.BlockSpec((block_len, width), lambda i: (start + i, 0))
        spec, parts = [], []
        for group in groups:
            spec.append(list(range(len(parts), len(parts) + len(group))))
            parts += group
        out = pl.pallas_call(
            functools.partial(attention_kernel, start, spec),
            name="dense_attention",
            out_shape=jax.ShapeDtypeStruct((count * block_len, D), BF16),
            grid=(count,),
            in_specs=[smem(), smem(), block(), block(2 * D)]
            + [pl.BlockSpec((D, D), lambda i: (0, 1)), pl.BlockSpec((D, D), lambda i: (0, 2))]
            + [block()] * len(parts)
            + [pl.BlockSpec((MSG, D), lambda i: (0, 0))] * (others + 2),
            out_specs=pl.BlockSpec((block_len, D), lambda i: (i, 0)),
            scratch_shapes=[pltpu.VMEM((others * block_len, D), BF16)] * 2,
            compiler_params=params(),
            cost_estimate=cost(micros),
        )(
            alibi_slopes, scalars, after(q_own), kv_own, qkv_weight, qkv_weight, *parts, *recv1, msg1,
            vecs,
        )
        done(out)
        return out

    value_r = flip(after(value_s), order_y[1])
    attended = [attend(0, seqs - 1, 0.1)]
    bx_k, bx_r, by_k, by_r = after(bx_k, bx_r, by_k, by_r)
    b_k, b_s = add_rows(
        [(bx_k, bx_r, (0, 0), seg_b[0]), (by_k, by_r, (0, 0), seg_b[1])], [[0, 1]], "add_b"
    )
    done(b_k)
    b_r = flip(b_s, order_rest[0])
    seg_b = cut_in_half([seg_b[0] + seg_b[1]])
    ax_k, ax_r, ay_k, ay_r, value_k, value_r = after(ax_k, ax_r, ay_k, ay_r, value_k, value_r)
    ax_k, ax_s, ay_k, ay_s, small = add_rows(
        [
            (ax_k, ax_r, (0, 0), seg_a[0]), (ay_k, ay_r, (0, 0), seg_a[1]),
            (value_k, value_r, (0, 0), [value_k.shape[0]]),
        ],
        [[0], [1, 2]], "add_xy_a", small,
    )
    done(ax_k)
    ax_r, ay_r = flip(ax_s, order_x[2]), flip(ay_s, order_y[2])
    seg_a = cut_in_half([seg_a[0], seg_a[1] + [value_k.shape[0]]])
    attended.append(attend(seqs - 1, 1, 60))

    def step_a(bit):
        nonlocal a_k, a_r, seg_a, small
        a_k, a_r, small = after(a_k, a_r, small)
        a_k, a_s, small = add_rows([(a_k, a_r, (0, 0), seg_a[0])], [[0]], "add_a", small)
        done(a_k)
        seg_a = cut_in_half(seg_a)
        a_r = flip(a_s, bit)

    def step_b(bit):
        nonlocal b_k, b_r, seg_b
        b_k, b_r = after(b_k, b_r)
        b_k, b_s = add_rows([(b_k, b_r, (0, 0), seg_b[0])], [[0]], "add_b")
        done(b_k)
        seg_b = cut_in_half(seg_b)
        b_r = flip(b_s, bit)

    step_b(order_rest[1])
    ax_k, ax_r, ay_k, ay_r = after(ax_k, ax_r, ay_k, ay_r)
    a_k, a_s, small = add_rows(
        [(ax_k, ax_r, (0, 0), seg_a[0]), (ay_k, ay_r, (0, 0), seg_a[1])], [[0, 1]], "add_a", small
    )
    done(a_k)
    a_r = flip(a_s, order_rest[0])
    seg_a = cut_in_half([seg_a[0] + seg_a[1]])

    def ffn(part, first, size, whole):
        rows = pl.BlockSpec((size, D), lambda i: (first // size, 0))
        fixed = lambda shape: pl.BlockSpec(shape, lambda i: (0, 0))
        out = pl.pallas_call(
            functools.partial(dense_kernel, whole is not None),
            name="dense_ffn",
            out_shape=bf_full,
            grid=(n,),
            in_specs=[rows, fixed((size, D)), fixed((D, D)), fixed((16, D))]
            + [
                pl.BlockSpec((D, CHUNK), lambda i: (0, i)),
                pl.BlockSpec((D, CHUNK), lambda i: (0, n + i)),
                pl.BlockSpec((CHUNK, D), lambda i: (i, 0)),
            ]
            + ([] if whole is None else [pl.BlockSpec(memory_space=pl.ANY)]),
            out_specs=rows,
            input_output_aliases={} if whole is None else {7: 0},
            scratch_shapes=[
                pltpu.VMEM((size, D), F32), pltpu.VMEM((size, D), BF16), pltpu.VMEM((size, D), F32),
            ],
            compiler_params=params(),
            cost_estimate=cost(60),
        )(
            x, after(part), out_weight, vecs, gate_up_weight, gate_up_weight, down_weight,
            *([] if whole is None else [whole]),
        )
        done(out)
        return out

    last_rows = tokens - block_len
    output = ffn(attended[0], 0, last_rows, None)
    step_a(order_rest[1])
    b_r, _ = held(b_r, output)
    output = ffn(attended[1], last_rows, block_len, output)
    for bit in order_rest[2:]:
        step_b(bit)
        step_a(bit)
    (
        grad_gateup, grad_down, grad_outw, grad_qkv, grad_embed, grad_qbias, grad_vbias, grad_outb,
        grad_gain1, grad_shift1, grad_downb, grad_gain2, grad_shift2,
    ) = finish(
        scalars, *after(a_k, a_r, b_k, b_r, small), vecs, qm, FF // shards, D // shards,
    )

    shape = (seqs, block_len, D)
    return (
        output.reshape(shape), input_grad.reshape(shape), grad_embed, grad_qkv, grad_qbias,
        grad_vbias, grad_outw, grad_outb, grad_gain1, grad_shift1, grad_gateup, grad_down,
        grad_downb, grad_gain2, grad_shift2,
    )


def solution(mesh):
    data, pairs = P("batch", "seq", None), P("batch", "seq")
    in_specs = (data, pairs, pairs) + (P(),) * 14 + (data,)
    vector, matrix = P(("batch", "seq")), P(("batch", "seq"), None)
    out_specs = (
        data, data, vector, matrix, vector, vector, matrix, vector, vector, vector, matrix, matrix,
        vector, vector, vector,
    )
    return jax.shard_map(
        on_device, mesh=mesh, in_specs=in_specs, out_specs=out_specs, check_vma=False
    )
```

```python
import functools
import math

import jax
import jax.numpy as jnp
import numpy as np
from jax import lax
from jax.experimental import pallas as pl
from jax.experimental.pallas import tpu as pltpu
from jax.sharding import PartitionSpec as P

D = 768
FF = 3072
H = 12
HD = 64
CAP = 192
CHUNK = 768
LANES = 128
MSG = 16
SMALL = 24

F32 = jnp.float32
BF16 = jnp.bfloat16


def params(limit=62):
    return pltpu.CompilerParams(vmem_limit_bytes=limit * 1024 * 1024)


def cost(micros):
    return pl.CostEstimate(flops=int(micros * 1.15e9), bytes_accessed=1024, transcendentals=0)


def dot(a, b):
    return lax.dot_general(a, b, (((1,), (0,)), ((), ())), preferred_element_type=F32)


def dot_nt(a, b):
    return lax.dot_general(a, b, (((1,), (1,)), ((), ())), preferred_element_type=F32)


def dot_tn(a, b):
    return lax.dot_general(a, b, (((0,), (0,)), ((), ())), preferred_element_type=F32)


def split2(v):
    high = v.astype(BF16)
    return high, (v - high.astype(F32)).astype(BF16)


def dot_wide(v, b):
    high, rest = split2(v)
    return dot(high, b) + dot(rest, b)


def expand_one():
    row = lax.broadcasted_iota(jnp.int32, (LANES, D), 0)
    lane = lax.broadcasted_iota(jnp.int32, (LANES, D), 1)
    return jnp.where(lax.shift_right_logical(lane, 6) == row, 1.0, 0.0).astype(BF16)


def expand_seq(s):
    row = lax.broadcasted_iota(jnp.int32, (LANES, D), 0)
    lane = lax.broadcasted_iota(jnp.int32, (LANES, D), 1)
    return jnp.where(lax.shift_right_logical(lane, 6) + 16 * s == row, 1.0, 0.0).astype(BF16)


def reduce_seq(s):
    row = lax.broadcasted_iota(jnp.int32, (D, LANES), 0)
    lane = lax.broadcasted_iota(jnp.int32, (D, LANES), 1)
    return jnp.where(lax.shift_right_logical(row, 6) + 16 * s == lane, 1.0, 0.0).astype(BF16)


def reduce_one():
    row = lax.broadcasted_iota(jnp.int32, (D, LANES), 0)
    lane = lax.broadcasted_iota(jnp.int32, (D, LANES), 1)
    return jnp.where(lax.shift_right_logical(row, 6) == lane, 1.0, 0.0).astype(BF16)


def permuting(place_row, me, rows):
    n = place_row.shape[1]
    distance = place_row[0:1, :]
    source = (distance ^ me) * rows + place_row[1:2, :]
    row = lax.broadcasted_iota(jnp.int32, (n, n), 0)
    return jnp.where(row == source, 1.0, 0.0).astype(BF16)


def decay(slope_lane, block_len):
    t = lax.broadcasted_iota(jnp.int32, (block_len, D), 0).astype(F32)
    return jnp.exp(-slope_lane * t), jnp.exp(-slope_lane * (block_len - 1.0 - t))


def head_decay(slope, block_len):
    row = lax.broadcasted_iota(jnp.int32, (block_len, block_len), 0)
    lane = lax.broadcasted_iota(jnp.int32, (block_len, block_len), 1)
    return jnp.exp(-slope * jnp.abs(row - lane).astype(F32)).astype(BF16)


def local_decay_sums(slopes_ref, wide, packed, wide_out, packed_out, block_len, seqs):
    lane = lax.broadcasted_iota(jnp.int32, (block_len, LANES), 1)
    total = jnp.zeros((block_len, LANES), F32)
    for pair in range(H // 2):
        low, high = pair * LANES, (pair + 1) * LANES
        right = jnp.concatenate([wide[s][:, low:high] for s in range(seqs)] + [packed], axis=1)
        even = dot(head_decay(slopes_ref[2 * pair], block_len), right)
        odd = dot(head_decay(slopes_ref[2 * pair + 1], block_len), right)
        for s in range(seqs):
            rows = slice(s * block_len, (s + 1) * block_len)
            at = slice(s * LANES, (s + 1) * LANES)
            wide_out[rows, low:high] = jnp.where(lane < HD, even[:, at], odd[:, at]).astype(
                wide_out.dtype
            )
        at = slice(seqs * LANES, (seqs + 1) * LANES)
        total = jnp.where((lane & 15) == 2 * pair, even[:, at], total)
        total = jnp.where((lane & 15) == 2 * pair + 1, odd[:, at], total)
    packed_out[...] = total


def lane_value(row, index):
    lane = lax.broadcasted_iota(jnp.int32, row.shape, 1)
    return jnp.sum(jnp.where(lane == index, row, 0.0), axis=1, keepdims=True)


GELU = (
    0.7978849414614602, 0.03633308456815623, -3.259496805730905e-05, -5.530619733817487e-05,
    3.9647451634764645e-06, -1.322634044387524e-07, 1.756172658552303e-09,
)


def normal_cdf(v):
    square = v * v
    poly = GELU[6]
    for c in GELU[5::-1]:
        poly = poly * square + c
    return 0.5 + 0.5 * jnp.tanh(v * poly)


def norm_rows(v):
    centred = v - jnp.mean(v, axis=1, keepdims=True)
    scale = lax.rsqrt(jnp.mean(centred * centred, axis=1, keepdims=True) + 1e-05)
    return centred * scale, scale


def norm_back(upstream, normed, scale, gain):
    scaled = upstream * gain
    return scale * (
        scaled
        - jnp.mean(scaled, axis=1, keepdims=True)
        - normed * jnp.mean(scaled * normed, axis=1, keepdims=True)
    )


def colsum(v):
    return jnp.sum(v, axis=0, keepdims=True)


def inputs_kernel(seqs, block_len, blocks, slopes_ref, offs_ref, hidden_ref, flags_ref, *refs):
    vec_refs, (x_ref, vecs_ref, flagx_ref, sc_ref) = refs[:-4], refs[-4:]
    emb = vec_refs[0][...].astype(F32).reshape(1, D)
    lane = lax.broadcasted_iota(jnp.int32, (1, D), 1)
    slope = jnp.zeros((1, D), F32)
    for h in range(H):
        slope = jnp.where(lax.shift_right_logical(lane, 6) == h, slopes_ref[h], slope)
    vecs_ref[...] = jnp.zeros_like(vecs_ref)
    vecs_ref[0:1, :] = slope
    for k, r in enumerate(vec_refs):
        vecs_ref[k + 1 : k + 2, :] = r[...].astype(F32).reshape(1, D)
    sc_ref[0] = lax.axis_index("batch") * blocks + lax.axis_index("seq")
    sc_ref[1] = lax.axis_index("seq")
    sc_ref[2] = jnp.maximum(1, (jnp.sum(flags_ref[...]) + CAP - 1) // CAP)
    flags = flags_ref[...].astype(F32)
    for s in range(seqs):
        rows = slice(s * block_len, (s + 1) * block_len)
        column = jnp.broadcast_to(flags[s : s + 1, :], (LANES, block_len)).T
        flagx_ref[rows, :] = column
        mask = jnp.broadcast_to(column[:, 0:1], (block_len, D)) > 0.5
        x_ref[rows, :] = jnp.where(mask, emb, hidden_ref[rows, :].astype(F32)).astype(BF16)
        sc_ref[4 + s] = offs_ref[0, s]


def project_kernel(scale, x_ref, w_ref, bias_ref, out_ref):
    out = dot(x_ref[...], w_ref[...])
    if scale is not None:
        out = (out + bias_ref[9:10, :]) * scale
    out_ref[...] = out.astype(BF16)


def project(x, weight, vecs, first, count, scale=None):
    return pl.pallas_call(
        functools.partial(project_kernel, scale),
        name="project",
        out_shape=jax.ShapeDtypeStruct((x.shape[0], count * D), BF16),
        grid=(count,),
        in_specs=[
            pl.BlockSpec(x.shape, lambda i: (0, 0)),
            pl.BlockSpec((D, D), lambda i: (0, first + i)), pl.BlockSpec((16, D), lambda i: (0, 0)),
        ],
        out_specs=pl.BlockSpec((x.shape[0], D), lambda i: (0, i)),
        compiler_params=params(),
        cost_estimate=cost(0.1),
    )(x, weight, vecs)


def prep_kernel(
    seqs, block_len, slopes_ref, sc_ref, x_ref, wqkv_ref, vecs_ref,
    v_ref, vw_ref, wx_ref, msg_ref, g_ref, qm_ref,
):
    slope_lane = vecs_ref[0:1, :]
    emb8 = jnp.broadcast_to(vecs_ref[1:2, :], (8, D)).astype(BF16)
    qm = (dot(emb8, wqkv_ref[:, 0:D]) + vecs_ref[9:10, :]).astype(BF16).astype(F32)
    qm_ref[...] = qm
    scaled = wqkv_ref[:, D : 2 * D].astype(F32) * (qm[0:1, :] * (HD**-0.5))
    g = dot_wide(scaled, reduce_one())
    g_high, g_rest = split2(g)
    g_ref[...] = g_high
    expand = expand_one()
    dec_f, dec_r = decay(slope_lane, block_len)
    packed = jnp.zeros((block_len, LANES), F32)
    lane = lax.broadcasted_iota(jnp.int32, (block_len, LANES), 1)
    msg_ref[...] = jnp.zeros_like(msg_ref)
    lane8 = lax.broadcasted_iota(jnp.int32, (1, D), 1)
    offs_row = jnp.zeros((1, D), F32)
    x = x_ref[...]
    both = dot(x, jnp.concatenate([g_high, g_rest], axis=1))
    v_ref[...] = dot(x, wqkv_ref[:, 2 * D :]).astype(BF16)
    for s in range(seqs):
        rows = slice(s * block_len, (s + 1) * block_len)
        a = both[rows, :LANES] + both[rows, LANES:]
        v = v_ref[rows, :]
        top = jnp.max(a, axis=0, keepdims=True)
        w = jnp.exp(a - top)
        wx = dot_wide(w, expand)
        w = jnp.where(lane < 16, w, 0.0)
        packed += pltpu.roll(w, 16 * s, 1) if s else w
        vw = v.astype(F32) * wx
        vw_ref[rows, :] = vw.astype(BF16)
        t1, t2 = split2(top)
        t3 = (top - t1.astype(F32) - t2.astype(F32)).astype(BF16)
        tops = sum(dot(jnp.broadcast_to(t, (8, LANES)), expand) for t in (t1, t2, t3))
        msg_ref[s : s + 1, :] = tops[0:1, :]
        msg_ref[seqs + s : seqs + s + 1, :] = colsum(dec_r * vw)
        msg_ref[2 * seqs + s : 2 * seqs + s + 1, :] = colsum(dec_r * wx)
        msg_ref[3 * seqs + s : 3 * seqs + s + 1, :] = colsum(dec_f * vw)
        msg_ref[4 * seqs + s : 4 * seqs + s + 1, :] = colsum(dec_f * wx)
        offs_row = jnp.where(lane8 == s, sc_ref[4 + s].astype(F32), offs_row)
    msg_ref[MSG - 1 : MSG, :] = offs_row
    wx_ref[...] = packed


def local_kernel(seqs, block_len, slopes_ref, vw_ref, wx_ref, flags_ref, num_ref, den_ref, rank_ref):
    rank_ref[...] = jnp.broadcast_to(
        masked_ranks(flags_ref, seqs, seqs * block_len), rank_ref.shape
    )
    weighted = [vw_ref[s * block_len : (s + 1) * block_len, :] for s in range(seqs)]
    local_decay_sums(
        slopes_ref, weighted, wx_ref[...].astype(BF16), num_ref, den_ref, block_len, seqs
    )


def masked_kernel(others, seqs, block_len, rows_d, rows_f, low_count, top_bit, sc_ref, *refs):
    (rank_ref, msg_ref, *refs) = refs
    recv_refs, refs = refs[:others], refs[others:]
    (
        num_ref, den_ref, og_ref, wo_ref, vecs_ref, placex_ref, placey_ref, placed_ref,
        wgu_ref, wd_ref,
        as_ref, ak_ref, bs_ref, bk_ref,
        att_ref, invden_ref, dheads_ref, small_ref,
        wg_s, wu_s, wd_s, g_s, u_s, dk_s, ds_s, os_s, ok_s, lowx_s, lowy_s, mixed_s, d1_s, d2_s,
        acc_s, fn_s, in_sems, out_sems,
    ) = refs
    n = FF // CHUNK
    half = D // 2
    wide = CHUNK // 2
    me, z = sc_ref[0], sc_ref[1]
    tokens = seqs * block_len
    core = lax.shift_right_logical(me, top_bit) & 1
    plane = lax.shift_right_logical(me, top_bit + 1)

    def at(i):
        return pl.ds(pl.multiple_of(i * CHUNK, CHUNK), CHUNK)

    def loads(i):
        up_at = pl.ds(pl.multiple_of(FF + i * CHUNK, CHUNK), CHUNK)
        return [
            pltpu.make_async_copy(wgu_ref.at[:, at(i)], wg_s.at[i], in_sems.at[0, i]),
            pltpu.make_async_copy(wgu_ref.at[:, up_at], wu_s.at[i], in_sems.at[1, i]),
            pltpu.make_async_copy(wd_ref.at[at(i), :], wd_s.at[i], in_sems.at[2, i]),
        ]

    moves = gradient_moves(
        n, plane, (g_s, u_s, dk_s, ds_s, ok_s, os_s), (ak_ref, as_ref, bk_ref, bs_ref)
    )

    def stores(i, when):
        for k, (test, inside, outside) in enumerate(moves(i)):
            if test is not False:
                copy = pltpu.make_async_copy(inside, outside, out_sems.at[k, i])
                chosen(test, functools.partial(when, copy))

    out_copies = [
        pltpu.make_async_copy(inside, outside, out_sems.at[12, k])
        for k, (inside, outside) in enumerate(out_moves((ok_s, os_s), (bk_ref, bs_ref)))
    ]

    for i in range(n):
        for copy in loads(i):
            copy.start()

    slope_lane = vecs_ref[0:1, :]
    dec_f, dec_r = decay(slope_lane, block_len)
    invden = jnp.zeros((block_len, LANES), F32)
    for s in range(seqs):
        rows = slice(s * block_len, (s + 1) * block_len)

        def row(ref, kind):
            return ref[kind * seqs + s : kind * seqs + s + 1, :]

        own_off = lane_value(msg_ref[MSG - 1 : MSG, :], s)
        top = row(msg_ref, 0)
        for r in recv_refs:
            top = jnp.maximum(top, row(r, 0))
        own = jnp.exp(row(msg_ref, 0) - top)
        zero = jnp.zeros((1, D), F32)
        left_v, left_z, right_v, right_z = zero, zero, zero, zero
        for k, r in enumerate(recv_refs):
            gap = jnp.abs(lane_value(r[MSG - 1 : MSG, :], s) - own_off) - (block_len - 1.0)
            factor = jnp.exp(row(r, 0) - top - slope_lane * gap)
            is_left = (z ^ (k + 1)) < z
            f_left = jnp.where(is_left, factor, 0.0)
            f_right = jnp.where(is_left, 0.0, factor)
            left_v += f_left * row(r, 1)
            left_z += f_left * row(r, 2)
            right_v += f_right * row(r, 3)
            right_z += f_right * row(r, 4)
        den = own * dot_wide(den_ref[...], expand_seq(s)) + dec_f * left_z + dec_r * right_z
        num = own * num_ref[rows, :].astype(F32) + dec_f * left_v + dec_r * right_v
        inv = 1.0 / den
        invden = invden + dot_wide(inv * (1.0 / HD), reduce_seq(s))
        att_ref[rows, :] = (num * inv).astype(BF16)
    invden_ref[...] = invden
    rank = rank_ref[0:1, :]
    small_ref[...] = jnp.zeros_like(small_ref)

    masked_tile(
        0, True, me, rows_d, rows_f, low_count, core, rank, att_ref, og_ref, wo_ref, vecs_ref,
        placex_ref, placey_ref, placed_ref, wg_s, wu_s, wd_s, g_s, u_s, dk_s, ds_s, os_s, ok_s,
        dheads_ref, small_ref, lowx_s, lowy_s, mixed_s, d1_s, d2_s, acc_s, fn_s, loads, stores,
    )
    for copy in out_copies:
        copy.start()
    for i in range(n):
        stores(i, lambda copy: copy.wait())
    for copy in out_copies:
        copy.wait()


SET_A = 4
B_ROWS_X = (FF // CHUNK - SET_A) * (D // 2) + FF // 4 + D // 2
B_ROWS_Y = (FF // CHUNK - SET_A) * (D // 2) + FF // 4


def chosen(test, work):
    if test is True:
        work()
    else:
        pl.when(test)(work)


def gradient_moves(n, plane, inside, outside):
    g_s, u_s, dk_s, ds_s, _ok, _os = inside
    ak_ref, as_ref, bk_ref, bs_ref = outside
    half, part = D // 2, CHUNK // 4
    b_x = (n - SET_A) * half

    def rows_at(first, size):
        return pl.ds(first if isinstance(first, int) else pl.multiple_of(first, 32), size)

    def moves(i):
        rel = i ^ plane
        x_rows = rows_at(b_x + swap_pair(rel) * part, part)
        y_rows = rows_at(B_ROWS_X + (n - SET_A) * half + rel * part, part)
        out = []
        for side, a_ref, b_ref, d in ((0, ak_ref, bk_ref, dk_s), (half, as_ref, bs_ref, ds_s)):
            rows = pl.ds(side, half)
            for value, a_first, b_first in (
                (g_s, 0, 0), (u_s, SET_A * half, B_ROWS_X)
            ):
                if isinstance(i, int):
                    at_a, at_b = min(i, SET_A - 1), max(i - SET_A, 0)
                else:
                    at_a, at_b = jnp.minimum(i, SET_A - 1), jnp.maximum(i - SET_A, 0)
                to_a = a_ref.at[rows_at(a_first + at_a * half, half)]
                to_b = b_ref.at[rows_at(b_first + at_b * half, half)]
                out.append((i < SET_A, value.at[i, rows], to_a))
                out.append((i >= SET_A, value.at[i, rows], to_b))
            out.append((True, d.at[i, pl.ds(0, part)], b_ref.at[x_rows]))
            out.append((True, d.at[i, pl.ds(part, part)], b_ref.at[y_rows]))
        return out

    return moves


def out_moves(inside, outside):
    rows = pl.ds(B_ROWS_X - D // 2, D // 2)
    return [(value, ref.at[rows]) for value, ref in zip(inside, outside)]


def masked_tile(
    t, first, me, rows_d, rows_f, low_count, core, rank, att_ref, og_ref, wo_ref, vecs_ref,
    placex_ref, placey_ref, placed_ref, wg_s, wu_s, wd_s, g_s, u_s, dk_s, ds_s, os_ref, ok_ref,
    dheads_ref, small_ref, lowx_s, lowy_s, mixed_s, d1_s, d2_s, acc_s, fn_s, loads, stores,
):
    n = FF // CHUNK
    half = D // 2
    wide = CHUNK // 2
    tokens = att_ref.shape[0]

    def put(ref, value):
        ref[...] = (value if first else ref[...].astype(F32) + value).astype(BF16)

    place = lax.broadcasted_iota(jnp.int32, (CAP, tokens), 0) + t * CAP
    comp = jnp.where(place.astype(F32) == rank, 1.0, 0.0).astype(BF16)
    att_low = (dot(comp, att_ref[...]) + vecs_ref[2:3, :]).astype(BF16)
    first_sum = vecs_ref[1:2, :] + (dot(att_low, wo_ref[...]) + vecs_ref[3:4, :])
    first_normed, first_scale = norm_rows(first_sum)
    fn_s[...] = first_normed
    low = (first_normed * vecs_ref[4:5, :] + vecs_ref[5:6, :]).astype(BF16)
    change_x = permuting(placex_ref[...], me, rows_d)
    lowx_s[...] = dot(low, change_x).astype(BF16).T
    lowy_s[...] = dot(low, permuting(placey_ref[...], me, rows_d)).astype(BF16).T
    acc_s[...] = jnp.zeros((CAP, D), F32)

    def forward(i, c):
        for copy in loads(i):
            copy.wait()
        gate = dot(low, wg_s[i])
        up = dot(low, wu_s[i])
        phi = normal_cdf(gate)
        act = gate * phi
        mixed = (act * up).astype(BF16)
        mixed_s[i] = mixed
        d2_s[i] = act.astype(BF16)
        slope = phi + gate * (jnp.exp(-0.5 * gate * gate) * ((2.0 * math.pi) ** -0.5))
        d1_s[i] = (up * slope).astype(BF16)
        acc_s[...] += dot(mixed, wd_s[i])
        return c

    lax.fori_loop(0, n, forward, 0)
    first_out = fn_s[...] * vecs_ref[4:5, :] + vecs_ref[5:6, :]
    normed, scale = norm_rows(first_out + (acc_s[...] + vecs_ref[6:7, :]))
    up = dot(comp, og_ref[...])
    grad_second = norm_back(up, normed, scale, vecs_ref[7:8, :])
    acc_s[...] = grad_second
    bg = grad_second.astype(BF16)
    small_ref[0:1, :] += colsum(up * normed)
    small_ref[1:2, :] += colsum(up)
    small_ref[2:3, :] += colsum(bg.astype(F32))
    change_d = permuting(placed_ref[...], me & (low_count - 1), rows_f)

    def backward(i, c):
        mixed_grad = dot_nt(bg, wd_s[i]).astype(BF16).astype(F32)
        gate_grad = (mixed_grad * d1_s[i].astype(F32)).astype(BF16)
        up_grad = (mixed_grad * d2_s[i].astype(F32)).astype(BF16)
        put(g_s.at[i], dot(lowx_s[...], gate_grad))
        put(u_s.at[i], dot(lowy_s[...], up_grad))
        mixed = mixed_s[i]
        low_half, high_half = mixed[:, :wide], mixed[:, wide:]
        keep = jnp.where(core == 0, low_half, high_half)
        send = jnp.where(core == 0, high_half, low_half)
        put(dk_s.at[i], dot_tn(dot(keep, change_d).astype(BF16), bg))
        put(ds_s.at[i], dot_tn(dot(send, change_d).astype(BF16), bg))
        stores(i, lambda copy: copy.start())
        acc_s[...] += dot_nt(gate_grad, wg_s[i]) + dot_nt(up_grad, wu_s[i])
        return c

    lax.fori_loop(0, n, backward, 0)
    grad_first = acc_s[...]
    first_normed = fn_s[...]
    grad = norm_back(grad_first, first_normed, first_scale, vecs_ref[4:5, :])
    small_ref[3:4, :] += colsum(grad_first * first_normed)
    small_ref[4:5, :] += colsum(grad_first)
    attn_grad = grad.astype(BF16)
    small_ref[5:6, :] += colsum(attn_grad.astype(F32))
    small_ref[6:7, :] += colsum(grad)
    moved = dot(att_low, change_x).astype(BF16)
    grad_out = dot_tn(moved, attn_grad)
    put(ok_ref, grad_out[:half])
    put(os_ref, grad_out[half:])
    heads = dot_nt(attn_grad, wo_ref[...]).astype(BF16)
    small_ref[7:8, :] += colsum(heads.astype(F32))
    put(dheads_ref, dot_tn(comp, heads))


def masked_ranks(flags_ref, seqs, tokens):
    flags = jnp.concatenate([flags_ref[s : s + 1, :] for s in range(seqs)], axis=1).astype(F32)
    before = lax.broadcasted_iota(jnp.int32, (tokens, tokens), 0)
    after = lax.broadcasted_iota(jnp.int32, (tokens, tokens), 1)
    upper = jnp.where(before < after, 1.0, 0.0).astype(BF16)
    rank = dot(jnp.broadcast_to(flags, (8, tokens)).astype(BF16), upper)[0:1, :]
    return jnp.where(flags > 0.5, rank, -1.0)


def more_tiles_kernel(seqs, block_len, rows_d, rows_f, low_count, top_bit, sc_ref, *refs):
    held, (wgu_ref, wd_ref), grads, scratch = refs[:8], refs[8:10], refs[16:22], refs[22:]
    (
        flags_s, att_s, og_s, wo_s, vecs_s, placex_s, placey_s, placed_s, wg_s, wu_s, wd_s, g_s, u_s,
        dk_s, ds_s, os_s, ok_s, dheads_s, small_s, lowx_s, lowy_s, mixed_s, d1_s, d2_s, acc_s, fn_s,
        sem,
    ) = scratch
    as_ref, ak_ref, bs_ref, bk_ref, dheads_ref, small_ref = grads
    n = FF // CHUNK
    half = D // 2
    wide = CHUNK // 2
    me = sc_ref[0]
    core = lax.shift_right_logical(me, top_bit) & 1
    plane = lax.shift_right_logical(me, top_bit + 1)

    def move(source, target):
        copy = pltpu.make_async_copy(source, target, sem)
        copy.start()
        copy.wait()

    pairs = [(dheads_ref, dheads_s), (small_ref, small_s)]
    moves = gradient_moves(
        n, plane, (g_s, u_s, dk_s, ds_s, ok_s, os_s), (ak_ref, as_ref, bk_ref, bs_ref)
    )
    for i in range(n):
        pairs += [(outside, inside) for test, inside, outside in moves(i) if test is not False]
    pairs += [(o, i) for i, o in out_moves((ok_s, os_s), (bk_ref, bs_ref))]

    @pl.when(sc_ref[2] > 1)
    def _():
        for i in range(n):
            at = pl.ds(i * CHUNK, CHUNK)
            move(wgu_ref.at[:, at], wg_s.at[i])
            move(wgu_ref.at[:, pl.ds(FF + i * CHUNK, CHUNK)], wu_s.at[i])
            move(wd_ref.at[at, :], wd_s.at[i])
        for source, target in zip(held, scratch[:8]):
            move(source, target)
        for outside, inside in pairs:
            move(outside, inside)
        rank = masked_ranks(flags_s, seqs, seqs * block_len)

        def tile(t, carry):
            masked_tile(
                t, False, me, rows_d, rows_f, low_count, core, rank, att_s, og_s, wo_s, vecs_s,
                placex_s, placey_s, placed_s, wg_s, wu_s, wd_s, g_s, u_s, dk_s, ds_s, os_s, ok_s,
                dheads_s, small_s, lowx_s, lowy_s, mixed_s, d1_s, d2_s, acc_s, fn_s,
                lambda i: [], lambda i, when: None,
            )
            return carry

        lax.fori_loop(1, sc_ref[2], tile, 0)
        for outside, inside in pairs:
            move(inside, outside)


def inner_kernel(
    seqs, block_len, slopes_ref, dheads_ref, att_ref, invden_ref, vecs_ref, uv_ref, ud_ref, msg_ref
):
    slope_lane = vecs_ref[0:1, :]
    dec_f, dec_r = decay(slope_lane, block_len)
    wide = []
    packed = jnp.zeros((block_len, LANES), F32)
    msg_ref[...] = jnp.zeros_like(msg_ref)
    for s in range(seqs):
        rows = slice(s * block_len, (s + 1) * block_len)
        dheads = dheads_ref[rows, :].astype(F32)
        expand = expand_seq(s)
        inner = dot_wide(dheads * att_ref[rows, :].astype(F32), reduce_seq(s)) * invden_ref[...]
        packed += inner
        yv = dheads * dot_wide(invden_ref[...], expand)
        yd = dot_wide(inner, expand)
        wide.append(yv.astype(BF16))
        msg_ref[s : s + 1, :] = colsum(dec_r * yv)
        msg_ref[seqs + s : seqs + s + 1, :] = colsum(dec_r * yd)
        msg_ref[2 * seqs + s : 2 * seqs + s + 1, :] = colsum(dec_f * yv)
        msg_ref[3 * seqs + s : 3 * seqs + s + 1, :] = colsum(dec_f * yd)
    local_decay_sums(slopes_ref, wide, packed.astype(BF16), uv_ref, ud_ref, block_len, seqs)


def value_kernel(others, seqs, block_len, rows_d, sc_ref, *refs):
    (flags_ref, msg1_ref, msg2_ref, *refs) = refs
    recv1, recv2, refs = refs[:others], refs[others : 2 * others], refs[2 * others :]
    (
        uv_ref, ud_ref, wx_ref, v_ref, x_ref, wqkv_ref, g_ref, vecs_ref, placey_ref, smalla_ref,
        ig_ref, vs_ref, vk_ref, small_ref, dv_s, t_s,
    ) = refs
    me, z = sc_ref[0], sc_ref[1]
    slope_lane = vecs_ref[0:1, :]
    dec_f, dec_r = decay(slope_lane, block_len)
    reduce = reduce_one()
    embed = smalla_ref[6:7, :]
    half = D // 2
    for s in range(seqs):
        rows = slice(s * block_len, (s + 1) * block_len)

        def row(ref, kind):
            return ref[kind * seqs + s : kind * seqs + s + 1, :]

        own_off = lane_value(msg1_ref[MSG - 1 : MSG, :], s)
        top = row(msg1_ref, 0)
        for r in recv1:
            top = jnp.maximum(top, row(r, 0))
        own = jnp.exp(row(msg1_ref, 0) - top)
        zero = jnp.zeros((1, D), F32)
        left_v, left_d, right_v, right_d = zero, zero, zero, zero
        for k, (r1, r2) in enumerate(zip(recv1, recv2)):
            gap = jnp.abs(lane_value(r1[MSG - 1 : MSG, :], s) - own_off) - (block_len - 1.0)
            factor = jnp.exp(-slope_lane * gap)
            is_left = (z ^ (k + 1)) < z
            f_left = jnp.where(is_left, factor, 0.0)
            f_right = jnp.where(is_left, 0.0, factor)
            left_v += f_left * row(r2, 0)
            left_d += f_left * row(r2, 1)
            right_v += f_right * row(r2, 2)
            right_d += f_right * row(r2, 3)
        expand = expand_seq(s)
        weight = dot_wide(wx_ref[...], expand) * own
        uv = weight * (uv_ref[rows, :].astype(F32) + dec_f * left_v + dec_r * right_v)
        ud = weight * (dot_wide(ud_ref[...], expand) + dec_f * left_d + dec_r * right_d)
        dv = uv.astype(BF16)
        dv_s[rows, :] = dv
        t = dot_wide(uv * v_ref[rows, :].astype(F32) - ud * (1.0 / HD), reduce)
        t_s[rows, :] = t
    dx = dot_nt(dv_s[...], wqkv_ref[:, 2 * D :]) + dot_nt(t_s[...].astype(BF16), g_ref[...])
    masked = jnp.broadcast_to(flags_ref[:, 0:1], dx.shape) > 0.5
    ig_ref[...] = jnp.where(masked, 0.0, dx).astype(BF16)
    embed += colsum(jnp.where(masked, dx, 0.0))
    x = x_ref[...]
    xp = dot(x, permuting(placey_ref[...], me, rows_d)).astype(BF16)
    gv = dot_tn(xp, dv_s[...]).astype(BF16)
    vk_ref[...] = gv[:half]
    vs_ref[0:half, :] = gv[half:]
    t_high, t_rest = split2(t_s[...])
    a_t = (dot_tn(t_high, x) + dot_tn(t_rest, x))[0:16, :]
    both = dot_wide(a_t, wqkv_ref[:, D : 2 * D]) * (HD**-0.5)
    head = lax.broadcasted_iota(jnp.int32, (16, D), 0)
    lane = lax.broadcasted_iota(jnp.int32, (16, D), 1)
    query = colsum(jnp.where(lax.shift_right_logical(lane, 6) == head, both, 0.0))
    q_high, q_rest = split2(jnp.broadcast_to(query, (8, D)))
    wq = wqkv_ref[:, 0:D]
    embed += (dot_nt(q_high, wq) + dot_nt(q_rest, wq))[0:1, :]
    small_ref[0:8, :] = smalla_ref[...]
    small_ref[6:7, :] = embed
    small_ref[8:24, :] = a_t
    small_ref[20:21, :] = query
    put_small(vs_ref, half, small_ref[...])


FEATS = 6
LOG2E = math.log2(math.e)


def attention_kernel(start, spec, slopes_ref, sc_ref, q_ref, own_ref, wk_ref, wv_ref, *refs):
    others = len(spec)
    count = sum(len(group) for group in spec)
    part_refs, msg_refs, (msg_ref, vecs_ref, out_ref, k_s, v_s) = (
        refs[:count], refs[count : count + others], refs[count + others :],
    )
    s = start + pl.program_id(0)
    block_len = q_ref.shape[0]
    z = sc_ref[1]
    lane = lax.broadcasted_iota(jnp.int32, (block_len, LANES), 1)
    token = lax.broadcasted_iota(jnp.int32, (block_len, LANES), 0).astype(F32)
    head_of = lane // FEATS
    kind = lane - head_of * FEATS
    row = lax.broadcasted_iota(jnp.int32, (block_len, block_len), 0)
    col = lax.broadcasted_iota(jnp.int32, (block_len, block_len), 1)
    apart = jnp.abs(row - col).astype(F32) * LOG2E
    qvalue = jnp.where(kind < 3, token, 1.0)

    rows = []
    for k in range(others):
        parts = [part_refs[at][...] for at in spec[k]]
        x = parts[0]
        if len(parts) == 2:
            x = jnp.where((z == 1) | (z == 2), parts[0], parts[1])
        rows.append(x)
    x = jnp.concatenate(rows, axis=0)
    k_s[...] = dot(x, wk_ref[...]).astype(BF16)
    v_s[...] = dot(x, wv_ref[...]).astype(BF16)

    slope = jnp.zeros((1, LANES), F32)
    lane1 = lax.broadcasted_iota(jnp.int32, (1, LANES), 1)
    for h in range(H):
        slope = jnp.where(lane1 // FEATS == h, slopes_ref[h] * LOG2E, slope)
    kind1 = lane1 - (lane1 // FEATS) * FEATS
    own_off = lane_value(msg_ref[MSG - 1 : MSG, :], s)
    feats = []
    for k in range(others):
        gap = jnp.abs(lane_value(msg_refs[k][MSG - 1 : MSG, :], s) - own_off)
        sign = jnp.where((z ^ (k + 1)) < z, 1.0, -1.0)
        value = jnp.where(kind1 < 3, -sign * slope, slope * (sign * token - gap))
        p1 = value.astype(BF16).astype(F32)
        p2 = (value - p1).astype(BF16).astype(F32)
        p3 = value - p1 - p2
        part = jnp.where(kind1 % 3 == 0, p1, jnp.where(kind1 % 3 == 1, p2, p3))
        feats.append(part.astype(BF16))
    ones = jnp.ones((block_len, LANES), BF16)
    zero = jnp.zeros((), BF16)
    for pair in range(H // 2):
        low, high = pair * LANES, (pair + 1) * LANES
        q = q_ref[:, low:high]
        block = lambda ref, k: ref[k * block_len : (k + 1) * block_len, low:high]
        qh = jnp.concatenate([jnp.where(lane < HD, q, zero), jnp.where(lane < HD, zero, q)], axis=0)
        qfeat = jnp.concatenate(
            [jnp.where(head_of == 2 * pair + e, qvalue, 0.0).astype(BF16) for e in range(2)], axis=0
        )
        qf = jnp.concatenate([qh, qfeat], axis=1)
        bias = jnp.concatenate([apart * slopes_ref[2 * pair + e] for e in range(2)], axis=0)
        scores = [dot_nt(qh, own_ref[:, low:high]) - bias]
        for k in range(others):
            scores.append(dot_nt(qf, jnp.concatenate([block(k_s, k), feats[k]], axis=1)))
        top = scores[0]
        for sc in scores[1:]:
            top = jnp.maximum(top, sc)
        top = jnp.max(top, axis=1, keepdims=True)
        values = [own_ref[:, D + low : D + high]] + [block(v_s, k) for k in range(others)]
        total = None
        for sc, value in zip(scores, values):
            part = dot(jnp.exp2(sc - top).astype(BF16), jnp.concatenate([value, ones], axis=1))
            total = part if total is None else total + part
        out = total[:, :LANES] / total[:, LANES:]
        out_ref[:, low:high] = (
            jnp.where(lane < HD, out[:block_len], out[block_len:]) + vecs_ref[2:3, low:high]
        ).astype(BF16)


def dense_kernel(into, x_ref, att_ref, wo_ref, vecs_ref, wg_ref, wu_ref, wd_ref, *refs):
    out_ref, fo_s, low_s, acc_s = refs[1:] if into else refs
    step = pl.program_id(0)

    @pl.when(step == 0)
    def _():
        first_sum = x_ref[...].astype(F32) + (dot(att_ref[...], wo_ref[...]) + vecs_ref[3:4, :])
        normed, _scale = norm_rows(first_sum)
        first_out = normed * vecs_ref[4:5, :] + vecs_ref[5:6, :]
        fo_s[...] = first_out
        low_s[...] = first_out.astype(BF16)
        acc_s[...] = jnp.zeros_like(acc_s)

    low = low_s[...]
    gate = dot(low, wg_ref[...])
    up = dot(low, wu_ref[...])
    mixed = (gate * normal_cdf(gate) * up).astype(BF16)
    acc_s[...] += dot(mixed, wd_ref[...])

    @pl.when(step == pl.num_programs(0) - 1)
    def _():
        normed, _scale = norm_rows(fo_s[...] + (acc_s[...] + vecs_ref[6:7, :]))
        out_ref[...] = (normed * vecs_ref[7:8, :] + vecs_ref[8:9, :]).astype(BF16)


def put_small(ref, at, small):
    high, rest = split2(small)
    ref[at : at + SMALL, :] = high
    ref[at + SMALL : at + 2 * SMALL, :] = rest


def get_small(ref, at):
    return ref[at : at + SMALL, :].astype(F32) + ref[at + SMALL : at + 2 * SMALL, :].astype(F32)


def add_rows_kernel(spec, join, *refs):
    count = len(spec)
    arrays, refs = refs[: 2 * count], refs[2 * count :]
    kept, sent = [], []
    for at, ((first, got_first), segments) in enumerate(spec):
        keep, got = arrays[2 * at : 2 * at + 2]
        rows = sum(segments)
        total = keep[first : first + rows, :].astype(F32)
        total += got[got_first : got_first + rows, :].astype(F32)
        one, two = halves(total, segments)
        kept.append(one)
        sent.append(two)
    small = None
    if len(refs) == 2 * len(join) + 2:
        small_ref, refs = refs[0], refs[1:]
        got = arrays[-1]
        top = got.shape[0] - 2 * SMALL
        small = (
            small_ref[...] + got[top : top + SMALL, :].astype(F32)
            + got[top + SMALL : top + 2 * SMALL, :].astype(F32)
        )
        refs[-1][...] = small
    for at, group in enumerate(join):
        keep_out, send_out = refs[2 * at : 2 * at + 2]
        keep_out[...] = jnp.concatenate([kept[k] for k in group], axis=0).astype(BF16)
        sending = jnp.concatenate([sent[k] for k in group], axis=0).astype(BF16)
        rows = sending.shape[0]
        send_out[0:rows, :] = sending
        if small is not None and at == len(join) - 1:
            high, rest = split2(small)
            send_out[rows : rows + SMALL, :] = high
            send_out[rows + SMALL : rows + 2 * SMALL, :] = rest


def add_rows(pieces, join, name, small=None):
    spec = [(first, tuple(segments)) for _k, _r, first, segments in pieces]
    arrays = [v for keep, got, _f, _s in pieces for v in (keep, got)]
    halved = [sum(segments) // 2 for _f, segments in spec]
    sizes = [sum(halved[k] for k in group) for group in join]
    if any(rows % 16 for _f, segments in spec for rows in segments):
        return add_rows_plain(pieces, join, small)
    cut = 2 if sum(sizes) > 1024 else 1
    col = lambda rows: pl.BlockSpec((rows, D // cut), lambda i: (0, i))
    outs = []
    for at, size in enumerate(sizes):
        more = 2 * SMALL if small is not None and at == len(sizes) - 1 else 0
        outs += [size, size + more]
    shapes = [jax.ShapeDtypeStruct((rows, D), BF16) for rows in outs]
    specs = [col(rows) for rows in outs]
    if small is not None:
        arrays.append(small)
        shapes.append(jax.ShapeDtypeStruct((SMALL, D), F32))
        specs.append(col(SMALL))
    return pl.pallas_call(
        functools.partial(add_rows_kernel, spec, join),
        name=name,
        grid=(cut,),
        out_shape=shapes,
        in_specs=[col(v.shape[0]) for v in arrays],
        out_specs=specs,
        compiler_params=params(),
        cost_estimate=cost(0.1),
    )(*arrays)


def add_rows_plain(pieces, join, small):
    kept, sent = [], []
    for keep, got, (first, got_first), segments in pieces:
        rows = sum(segments)
        total = keep[first : first + rows].astype(F32) + got[got_first : got_first + rows].astype(F32)
        one, two = halves(total.astype(BF16), segments)
        kept.append(one)
        sent.append(two)
    outs = []
    for at, group in enumerate(join):
        outs.append(jnp.concatenate([kept[k] for k in group], axis=0))
        send = [sent[k] for k in group]
        if small is not None and at == len(join) - 1:
            tail = pieces[-1][1][-2 * SMALL :].astype(F32)
            small = small + tail[:SMALL] + tail[SMALL:]
            send += list(split2(small))
        outs.append(jnp.concatenate(send, axis=0))
    return outs + ([small] if small is not None else [])


def add_small_kernel(keep, small, got, keep_out, send_out, small_out):
    half = keep.shape[0] // 2
    total = keep[...].astype(F32) + got[0 : 2 * half, :].astype(F32)
    keep_out[...] = total[:half].astype(BF16)
    send_out[0:half, :] = total[half:].astype(BF16)
    both = small[...] + get_small(got, 2 * half)
    small_out[...] = both
    put_small(send_out, half, both)


def add_small(keep, small, got, name):
    rows = keep.shape[0] // 2
    full = lambda shape: pl.BlockSpec(shape, lambda i: (0, 0))
    outs = [(rows, D), (rows + 2 * SMALL, D), (SMALL, D)]
    return pl.pallas_call(
        add_small_kernel,
        name=name,
        grid=(1,),
        out_shape=[
            jax.ShapeDtypeStruct(o, t) for o, t in zip(outs, (BF16, BF16, F32))
        ],
        in_specs=[full(v.shape) for v in (keep, small, got)],
        out_specs=[full(o) for o in outs],
        compiler_params=params(),
        cost_estimate=cost(0.1),
    )(keep, small, got)


def finish_kernel(
    rows_f, rows_d, sc_ref, a_k, a_r, b_k, b_r, small_ref, vecs_ref, qm_ref,
    gateup_ref, down_ref, out_ref, qkv_ref, *vector_refs,
):
    rows_a = a_k.shape[0]
    a_total = a_k[...].astype(F32) + a_r[0:rows_a, :].astype(F32)
    b_total = b_k[...].astype(F32) + b_r[...].astype(F32)
    gateup, down, out, value = unpack(a_total, b_total, rows_f, rows_d)
    for at, part in enumerate(gateup):
        gateup_ref[:, at * CHUNK : (at + 1) * CHUNK] = part
    down_ref[...] = down
    out_ref[...] = out
    small = (
        small_ref[...] + a_r[rows_a : rows_a + SMALL, :].astype(F32)
        + a_r[rows_a + SMALL : rows_a + 2 * SMALL, :].astype(F32)
    )
    row = lax.broadcasted_iota(jnp.int32, (D, LANES), 0)
    lane = lax.broadcasted_iota(jnp.int32, (D, LANES), 1)
    pick = jnp.where((row == lane + sc_ref[0] * rows_d) & (lane < rows_d), 1.0, 0.0).astype(BF16)
    both = jnp.concatenate([small, jnp.broadcast_to(vecs_ref[1:2, :], (8, D))], axis=0)
    p1 = both.astype(BF16)
    p2 = (both - p1.astype(F32)).astype(BF16)
    p3 = (both - p1.astype(F32) - p2.astype(F32)).astype(BF16)
    mine = dot(p1, pick) + dot(p2, pick) + dot(p3, pick)
    for ref, at in zip(vector_refs, SMALL_ROWS):
        ref[...] = mine[at : at + 1, 0:rows_d].reshape(rows_d)
    columns = mine.T
    emb = jnp.broadcast_to(columns[0:rows_d, SMALL : SMALL + 1], (rows_d, D))
    qkv_ref[:, 0:D] = emb * small[20:21, :]
    heads = columns[:, 8 : 8 + 16]
    key = jnp.concatenate(
        [jnp.broadcast_to(heads[0:rows_d, h : h + 1], (rows_d, HD)) for h in range(H)], axis=1
    )
    qkv_ref[:, D : 2 * D] = key * (qm_ref[0:1, :] * (HD**-0.5))
    qkv_ref[:, 2 * D :] = value


SMALL_ROWS = (6, 20, 7, 5, 3, 4, 2, 0, 1)


def unpack(a_total, b_total, rows_f, rows_d):
    n, part = FF // CHUNK, rows_f // 2
    a = [a_total[k * rows_d : (k + 1) * rows_d] for k in range(2 * n + 1)]
    down = jnp.concatenate([b_total[:part], b_total[part + rows_d :]], axis=0)
    return a[: 2 * n], down, b_total[part : part + rows_d], a[2 * n]


def finish(scalars, a_k, a_r, b_k, b_r, small, vecs, qm, rows_f, rows_d):
    outs = [(rows_d, 2 * FF), (rows_f, D), (rows_d, D), (rows_d, 3 * D)] + [(rows_d,)] * 9
    if rows_d % 8:
        rows_a = a_k.shape[0]
        gateup, down, out, value = unpack(
            a_k.astype(F32) + a_r[:rows_a].astype(F32), b_k.astype(F32) + b_r.astype(F32), rows_f,
            rows_d,
        )
        small = small + a_r[rows_a : rows_a + SMALL].astype(F32) + a_r[rows_a + SMALL :].astype(F32)
        mine = lax.dynamic_slice_in_dim(small, scalars[0] * rows_d, rows_d, 1)
        emb = lax.dynamic_slice_in_dim(vecs[1], scalars[0] * rows_d, rows_d, 0)
        key = jnp.repeat(mine[8 : 8 + H].T, HD, axis=1) * (qm[0:1, :] * (HD**-0.5))
        qkv = jnp.concatenate([emb[:, None] * small[20][None, :], key, value], axis=1)
        return [jnp.concatenate(gateup, axis=1), down, out, qkv] + [mine[k] for k in SMALL_ROWS]
    full = lambda shape: pl.BlockSpec(shape, lambda i: (0,) * len(shape))
    arrays = (a_k, a_r, b_k, b_r, small, vecs, qm)
    return pl.pallas_call(
        functools.partial(finish_kernel, rows_f, rows_d),
        name="finish",
        grid=(1,),
        out_shape=[jax.ShapeDtypeStruct(o, F32) for o in outs],
        in_specs=[smem()] + [full(v.shape) for v in arrays],
        out_specs=[full(o) for o in outs],
        compiler_params=params(),
        cost_estimate=cost(1),
    )(scalars, *arrays)


def halves(total, segments):
    first, second, at = [], [], 0
    for rows in segments:
        first.append(total[at : at + rows // 2])
        second.append(total[at + rows // 2 : at + rows])
        at += rows
    return jnp.concatenate(first, axis=0), jnp.concatenate(second, axis=0)


def bit_orders(batch, blocks):
    n = int(math.log2(batch * blocks))
    seq_bits = int(math.log2(blocks))
    rest = list(range(seq_bits, n - 3)) + list(range(seq_bits))
    top = [n - 3, n - 2, n - 1]
    return [*top, *rest], [top[0], top[2], top[1], *rest], rest


def places(order, rows, parts=1):
    n = len(order)
    place = np.arange(2**n)
    rel = np.zeros(2**n, np.int32)
    for k, bit in enumerate(order):
        rel |= ((place >> (n - 1 - k)) & 1).astype(np.int32) << bit
    out = np.zeros((8, 2**n * rows), np.int32)
    size = rows // parts
    out[0] = np.tile(np.repeat(rel, size), parts)
    out[1] = np.concatenate([np.tile(np.arange(size) + p * size, 2**n) for p in range(parts)])
    return out


def swap_pair(i):
    return (i & 1) * 2 + lax.shift_right_logical(i, 1)


def smem():
    return pl.BlockSpec(memory_space=pltpu.SMEM)


def masked_rows(
    batch, blocks, scalars, mask_flags, rank, msg1, recv1, num, den, grad, out_weight, vecs,
    gate_up_weight, down_weight,
):
    seqs, block_len = mask_flags.shape
    tokens = seqs * block_len
    shards = batch * blocks
    others = blocks - 1
    n = FF // CHUNK
    half = D // 2
    order_x, order_y, order_rest = bit_orders(batch, blocks)
    top_bit = len(order_x) - 3
    vmem, hbm = pl.BlockSpec(memory_space=pltpu.VMEM), pl.BlockSpec(memory_space=pl.ANY)
    bf_full = jax.ShapeDtypeStruct((tokens, D), BF16)
    set_a = jax.ShapeDtypeStruct((2 * SET_A * half, D), BF16)
    set_b = jax.ShapeDtypeStruct((B_ROWS_X + B_ROWS_Y, D), BF16)
    chunks = lambda rows, width: pltpu.VMEM((n, rows, width), BF16)
    grads = [set_a] * 2 + [set_b] * 2
    square_s = pltpu.VMEM((half, D), BF16)
    weights_s = [
        chunks(D, CHUNK), chunks(D, CHUNK), chunks(CHUNK, D), chunks(D, CHUNK), chunks(D, CHUNK),
        chunks(CHUNK // 2, D), chunks(CHUNK // 2, D),
    ]
    tile_s = [
        pltpu.VMEM((D, CAP), BF16), pltpu.VMEM((D, CAP), BF16), chunks(CAP, CHUNK),
        chunks(CAP, CHUNK), chunks(CAP, CHUNK), pltpu.VMEM((CAP, D), F32), pltpu.VMEM((CAP, D), F32),
    ]
    held = [
        places(order_x, D // shards), places(order_y, D // shards),
        places(order_rest, FF // shards, 2),
    ]
    small = jax.ShapeDtypeStruct((8, D), F32)
    packed = jax.ShapeDtypeStruct((block_len, LANES), F32)
    *sums, att, invden, dheads, small_sums = pl.pallas_call(
        functools.partial(
            masked_kernel, others, seqs, block_len, D // shards, FF // shards, shards // 8, top_bit
        ),
        name="masked_rows",
        out_shape=grads + [bf_full, packed, bf_full, small],
        in_specs=[smem()] + [vmem] * (10 + len(recv1)) + [hbm] * 2,
        out_specs=[hbm] * 4 + [vmem] * 4,
        scratch_shapes=weights_s + [square_s, square_s] + tile_s
        + [pltpu.SemaphoreType.DMA((3, n)), pltpu.SemaphoreType.DMA((13, n))],
        compiler_params=params(62),
        cost_estimate=cost(60),
    )(
        scalars, rank, msg1, *recv1, num, den, grad, out_weight, vecs, *held, gate_up_weight,
        down_weight,
    )
    *sums, dheads, small_sums = pl.pallas_call(
        functools.partial(
            more_tiles_kernel, seqs, block_len, D // shards, FF // shards, shards // 8, top_bit
        ),
        name="more_masked_rows",
        out_shape=grads + [bf_full, small],
        in_specs=[smem()] + [hbm] * 16,
        out_specs=[hbm] * 6,
        input_output_aliases={11 + k: k for k in range(6)},
        scratch_shapes=[
            pltpu.VMEM(mask_flags.shape, jnp.int32), pltpu.VMEM((tokens, D), BF16),
            pltpu.VMEM((tokens, D), BF16), pltpu.VMEM((D, D), BF16), pltpu.VMEM((16, D), F32),
        ]
        + [pltpu.VMEM(h.shape, jnp.int32) for h in held]
        + weights_s
        + [square_s, square_s, pltpu.VMEM((tokens, D), BF16), pltpu.VMEM((8, D), F32)]
        + tile_s
        + [pltpu.SemaphoreType.DMA],
        compiler_params=params(62),
        cost_estimate=cost(1),
    )(
        scalars, mask_flags, att, grad, out_weight, vecs, *held, gate_up_weight, down_weight, *sums,
        dheads, small_sums,
    )
    return (*sums, att, invden, dheads, small_sums)


def on_device(
    hidden_states, mask_flags, block_offsets, alibi_slopes, mask_embedding, qkv_weight, query_bias,
    value_bias, out_weight, out_bias, first_gain, first_shift, gate_up_weight, down_weight,
    down_bias, second_gain, second_shift, output_grad,
):
    seqs, block_len = mask_flags.shape
    tokens = seqs * block_len
    batch, blocks = lax.axis_size("batch"), lax.axis_size("seq")
    shards = batch * blocks
    z = lax.axis_index("seq")
    me = lax.axis_index("batch") * blocks + z
    order_x, order_y, order_rest = bit_orders(batch, blocks)
    seq_bits = int(math.log2(blocks))
    place_y = places(order_y, D // shards)
    top_bit = len(order_x) - 3
    n = FF // CHUNK
    half = D // 2
    square = jax.ShapeDtypeStruct((half, D), BF16)
    others = blocks - 1
    vmem = pl.BlockSpec(memory_space=pltpu.VMEM)
    packed = jax.ShapeDtypeStruct((block_len, LANES), F32)
    bf_full = jax.ShapeDtypeStruct((tokens, D), BF16)
    last = [()]

    def after(*values):
        tied = lax.optimization_barrier((values, last[0]))[0]
        return tied if len(values) > 1 else tied[0]

    def done(value):
        last[0] = value

    def along(value, axis, pairs):
        return lax.ppermute(value, axis, pairs)

    def flip(value, bit):
        if bit >= seq_bits:
            axis, size, mask = "batch", batch, 1 << (bit - seq_bits)
        else:
            axis, size, mask = "seq", blocks, 1 << bit
        return along(value, axis, [(i, i ^ mask) for i in range(size)])

    fixed = lambda shape: pl.BlockSpec(shape, lambda i: (0,) * len(shape))
    x, vecs, flagx, scalars = pl.pallas_call(
        functools.partial(inputs_kernel, seqs, block_len, blocks),
        name="inputs",
        grid=(1,),
        out_shape=(
            bf_full, jax.ShapeDtypeStruct((16, D), F32), jax.ShapeDtypeStruct((tokens, LANES), F32),
            jax.ShapeDtypeStruct((8,), jnp.int32),
        ),
        in_specs=[smem(), smem(), fixed((tokens, D)), fixed((seqs, block_len))] + [fixed((D,))] * 9,
        out_specs=[
            fixed((tokens, D)), fixed((16, D)), fixed((tokens, LANES)), smem(),
        ],
        compiler_params=params(),
        cost_estimate=cost(1),
    )(
        alibi_slopes, block_offsets.reshape(1, seqs), hidden_states.reshape(tokens, D), mask_flags,
        mask_embedding, value_bias, out_bias, first_gain, first_shift, down_bias, second_gain,
        second_shift, query_bias,
    )

    near = [(i, i ^ 1) for i in range(blocks)]
    hops = blocks == 4

    def centre(value):
        pairs = []
        for b in range(batch):
            for at in range(blocks):
                to = b * blocks + 3 - at if at in (1, 2) else (b ^ 1) * blocks + at
                pairs.append((b * blocks + at, to))
        return along(value, ("batch", "seq"), pairs)

    def held(*values):
        values = after(*values)
        done(values)
        return values

    v, vw, wx, msg1, g, qm = pl.pallas_call(
        functools.partial(prep_kernel, seqs, block_len),
        name="masked_prep",
        out_shape=(
            bf_full, bf_full, packed, jax.ShapeDtypeStruct((MSG, D), F32),
            jax.ShapeDtypeStruct((D, LANES), BF16), jax.ShapeDtypeStruct((8, D), F32),
        ),
        in_specs=[smem(), smem()] + [vmem] * 3,
        out_specs=[vmem] * 6,
        compiler_params=params(),
        cost_estimate=cost(10),
    )(alibi_slopes, scalars, x, qkv_weight, vecs)
    done(msg1)
    recv1 = [along(msg1, "seq", [(i, i ^ k) for i in range(blocks)]) for k in range(1, blocks)]

    num, den, rank = pl.pallas_call(
        functools.partial(local_kernel, seqs, block_len),
        name="masked_local",
        out_shape=(bf_full, packed, jax.ShapeDtypeStruct((8, tokens), F32)),
        in_specs=[smem(), vmem, vmem, vmem],
        out_specs=[vmem] * 3,
        compiler_params=params(),
        cost_estimate=cost(0.1),
    )(alibi_slopes, after(vw), wx, mask_flags)
    done(num)
    recv1 = list(held(*recv1, msg1))[:-1]
    x_late = after(x)
    if hops:
        round1 = along(x_late, "seq", near), centre(x_late)
    else:
        round1 = tuple(
            along(x_late, "seq", [(i, i ^ k) for i in range(blocks)]) for k in range(1, blocks)
        )

    a_s, a_k, b_s, b_k, att_m, invden, dheads, small_a = masked_rows(
        batch, blocks, scalars, mask_flags, rank, msg1, recv1, num, den,
        after(output_grad.reshape(tokens, D)), out_weight, vecs, gate_up_weight, down_weight,
    )
    done(small_a)
    round1 = held(*round1)
    if hops:
        round2 = along(round1[1], "seq", near), centre(round1[0])
    b_r, a_r = flip(b_s, order_x[0]), flip(a_s, order_x[0])

    uv, ud, msg2 = pl.pallas_call(
        functools.partial(inner_kernel, seqs, block_len),
        name="masked_inner",
        out_shape=(bf_full, packed, jax.ShapeDtypeStruct((MSG, D), F32)),
        in_specs=[smem()] + [vmem] * 4,
        out_specs=[vmem] * 3,
        compiler_params=params(),
        cost_estimate=cost(60),
    )(alibi_slopes, after(dheads), att_m, invden, vecs)
    done(msg2)

    q_own = project(after(x), qkv_weight, vecs, 0, 1, LOG2E * HD**-0.5)
    done(q_own)
    rows_a = SET_A * half
    seg_a = [[half] * SET_A] * 2
    more = n - SET_A
    seg_b = [[half] * more + [FF // 4, half], [half] * more + [FF // 4]]
    cut_in_half = lambda groups: [[rows // 2 for rows in group] for group in groups]
    b_k, b_r = after(b_k, b_r)
    bx_k, bx_s, by_k, by_s = add_rows(
        [(b_k, b_r, (0, 0), seg_b[0]), (b_k, b_r, (B_ROWS_X, B_ROWS_X), seg_b[1])], [[0], [1]], "add_core_b"
    )
    done(bx_k)
    bx_r, by_r = flip(bx_s, order_x[1]), flip(by_s, order_y[1])
    a_k, a_r = after(a_k, a_r)
    ax_k, ax_s, ay_k, ay_s = add_rows(
        [(a_k, a_r, (0, 0), seg_a[0]), (a_k, a_r, (rows_a, rows_a), seg_a[1])], [[0], [1]], "add_core_a"
    )
    done(ax_k)
    seg_a, seg_b = cut_in_half(seg_a), cut_in_half(seg_b)
    if hops:
        round2 = held(*round2)
    msg2_now = after(msg2)
    recv2 = [along(msg2_now, "seq", [(i, i ^ k) for i in range(blocks)]) for k in range(1, blocks)]
    kv_own = project(after(x), qkv_weight, vecs, 1, 2)
    done(kv_own)
    recv2 = list(held(*recv2, msg2))[:-1]
    ax_r, ay_r = flip(after(ax_s), order_x[1]), flip(after(ay_s), order_y[1])
    if hops:
        far = along(after(round2[1]), "seq", near)

    input_grad, value_s, value_k, small = pl.pallas_call(
        functools.partial(value_kernel, others, seqs, block_len, D // shards),
        name="value_grads",
        out_shape=(
            bf_full, jax.ShapeDtypeStruct((2 * SMALL + half, D), BF16),
            jax.ShapeDtypeStruct((half, D), BF16), jax.ShapeDtypeStruct((SMALL, D), F32),
        ),
        in_specs=[smem()] + [vmem] * (13 + len(recv1) + len(recv2)),
        out_specs=[vmem] * 4,
        scratch_shapes=[pltpu.VMEM((tokens, D), BF16), pltpu.VMEM((tokens, LANES), F32)],
        compiler_params=params(),
        cost_estimate=cost(60),
    )(
        scalars, flagx, msg1, msg2, *recv1, *recv2, uv, ud, wx, v, after(x), qkv_weight, g, vecs,
        place_y, small_a,
    )
    done(small)
    bx_r, by_r = held(bx_r, by_r)
    value_r = flip(after(value_s), order_y[0])
    bx_k, by_k = after(bx_k, by_k)
    bx_k, bx_s, by_k, by_s = add_rows(
        [(bx_k, bx_r, (0, 0), seg_b[0]), (by_k, by_r, (0, 0), seg_b[1])], [[0], [1]], "add_xy_b"
    )
    done(bx_k)
    value_k, value_s, small = add_small(*after(value_k, small, value_r), "add_core_value")
    done(small)
    bx_r, by_r = flip(after(bx_s), order_x[2]), flip(after(by_s), order_y[2])
    seg_b = cut_in_half(seg_b)
    if hops:
        far, _ = held(far, small)
    if hops:
        groups = [
            [round1[0]], [round2[1], round2[0]], [round1[1], far],
        ]
    else:
        groups = [[part] for part in round1]

    def attend(start, count, micros):
        block = lambda width=D: pl.BlockSpec((block_len, width), lambda i: (start + i, 0))
        spec, parts = [], []
        for group in groups:
            spec.append(list(range(len(parts), len(parts) + len(group))))
            parts += group
        out = pl.pallas_call(
            functools.partial(attention_kernel, start, spec),
            name="dense_attention",
            out_shape=jax.ShapeDtypeStruct((count * block_len, D), BF16),
            grid=(count,),
            in_specs=[smem(), smem(), block(), block(2 * D)]
            + [pl.BlockSpec((D, D), lambda i: (0, 1)), pl.BlockSpec((D, D), lambda i: (0, 2))]
            + [block()] * len(parts)
            + [pl.BlockSpec((MSG, D), lambda i: (0, 0))] * (others + 2),
            out_specs=pl.BlockSpec((block_len, D), lambda i: (i, 0)),
            scratch_shapes=[pltpu.VMEM((others * block_len, D), BF16)] * 2,
            compiler_params=params(),
            cost_estimate=cost(micros),
        )(
            alibi_slopes, scalars, after(q_own), kv_own, qkv_weight, qkv_weight, *parts, *recv1, msg1,
            vecs,
        )
        done(out)
        return out

    value_r = flip(after(value_s), order_y[1])
    attended = [attend(0, seqs - 1, 0.1)]
    bx_k, bx_r, by_k, by_r = after(bx_k, bx_r, by_k, by_r)
    b_k, b_s = add_rows(
        [(bx_k, bx_r, (0, 0), seg_b[0]), (by_k, by_r, (0, 0), seg_b[1])], [[0, 1]], "add_b"
    )
    done(b_k)
    b_r = flip(b_s, order_rest[0])
    seg_b = cut_in_half([seg_b[0] + seg_b[1]])
    ax_k, ax_r, ay_k, ay_r, value_k, value_r = after(ax_k, ax_r, ay_k, ay_r, value_k, value_r)
    ax_k, ax_s, ay_k, ay_s, small = add_rows(
        [
            (ax_k, ax_r, (0, 0), seg_a[0]), (ay_k, ay_r, (0, 0), seg_a[1]),
            (value_k, value_r, (0, 0), [value_k.shape[0]]),
        ],
        [[0], [1, 2]], "add_xy_a", small,
    )
    done(ax_k)
    ax_r, ay_r = flip(ax_s, order_x[2]), flip(ay_s, order_y[2])
    seg_a = cut_in_half([seg_a[0], seg_a[1] + [value_k.shape[0]]])
    attended.append(attend(seqs - 1, 1, 60))

    def step_a(bit):
        nonlocal a_k, a_r, seg_a, small
        a_k, a_r, small = after(a_k, a_r, small)
        a_k, a_s, small = add_rows([(a_k, a_r, (0, 0), seg_a[0])], [[0]], "add_a", small)
        done(a_k)
        seg_a = cut_in_half(seg_a)
        a_r = flip(a_s, bit)

    def step_b(bit):
        nonlocal b_k, b_r, seg_b
        b_k, b_r = after(b_k, b_r)
        b_k, b_s = add_rows([(b_k, b_r, (0, 0), seg_b[0])], [[0]], "add_b")
        done(b_k)
        seg_b = cut_in_half(seg_b)
        b_r = flip(b_s, bit)

    step_b(order_rest[1])
    ax_k, ax_r, ay_k, ay_r = after(ax_k, ax_r, ay_k, ay_r)
    a_k, a_s, small = add_rows(
        [(ax_k, ax_r, (0, 0), seg_a[0]), (ay_k, ay_r, (0, 0), seg_a[1])], [[0, 1]], "add_a", small
    )
    done(a_k)
    a_r = flip(a_s, order_rest[0])
    seg_a = cut_in_half([seg_a[0] + seg_a[1]])

    def ffn(part, first, size, whole):
        rows = pl.BlockSpec((size, D), lambda i: (first // size, 0))
        fixed = lambda shape: pl.BlockSpec(shape, lambda i: (0, 0))
        out = pl.pallas_call(
            functools.partial(dense_kernel, whole is not None),
            name="dense_ffn",
            out_shape=bf_full,
            grid=(n,),
            in_specs=[rows, fixed((size, D)), fixed((D, D)), fixed((16, D))]
            + [
                pl.BlockSpec((D, CHUNK), lambda i: (0, i)),
                pl.BlockSpec((D, CHUNK), lambda i: (0, n + i)),
                pl.BlockSpec((CHUNK, D), lambda i: (i, 0)),
            ]
            + ([] if whole is None else [pl.BlockSpec(memory_space=pl.ANY)]),
            out_specs=rows,
            input_output_aliases={} if whole is None else {7: 0},
            scratch_shapes=[
                pltpu.VMEM((size, D), F32), pltpu.VMEM((size, D), BF16), pltpu.VMEM((size, D), F32),
            ],
            compiler_params=params(),
            cost_estimate=cost(60),
        )(
            x, after(part), out_weight, vecs, gate_up_weight, gate_up_weight, down_weight,
            *([] if whole is None else [whole]),
        )
        done(out)
        return out

    last_rows = tokens - block_len
    output = ffn(attended[0], 0, last_rows, None)
    step_a(order_rest[1])
    b_r, _ = held(b_r, output)
    output = ffn(attended[1], last_rows, block_len, output)
    for bit in order_rest[2:]:
        step_b(bit)
        step_a(bit)
    (
        grad_gateup, grad_down, grad_outw, grad_qkv, grad_embed, grad_qbias, grad_vbias, grad_outb,
        grad_gain1, grad_shift1, grad_downb, grad_gain2, grad_shift2,
    ) = finish(
        scalars, *after(a_k, a_r, b_k, b_r, small), vecs, qm, FF // shards, D // shards,
    )

    shape = (seqs, block_len, D)
    return (
        output.reshape(shape), input_grad.reshape(shape), grad_embed, grad_qkv, grad_qbias,
        grad_vbias, grad_outw, grad_outb, grad_gain1, grad_shift1, grad_gateup, grad_down,
        grad_downb, grad_gain2, grad_shift2,
    )


def solution(mesh):
    data, pairs = P("batch", "seq", None), P("batch", "seq")
    in_specs = (data, pairs, pairs) + (P(),) * 14 + (data,)
    vector, matrix = P(("batch", "seq")), P(("batch", "seq"), None)
    out_specs = (
        data, data, vector, matrix, vector, vector, matrix, vector, vector, vector, matrix, matrix,
        vector, vector, vector,
    )
    return jax.shard_map(
        on_device, mesh=mesh, in_specs=in_specs, out_specs=out_specs, check_vma=False
    )
```
